32 devices in a mesh: seq: 8 (over y, x, core), row: 4 (over z).
Axes of the slice: x: 2, y: 2, z: 4, core: 2. Of those that a mesh axis runs over, the one named last changes fastest.
Arguments:
- hidden_in: bfloat16 [4, 1024, 2304], P('row', 'seq'), may hold values from -6 to 6
- cotangent: bfloat16 [4, 1024, 2304], P('row', 'seq'), may hold values from -6 to 6
- doc_lengths: int32 [4, 8], P('row'), may hold values from 1 to 896, as said below
- gain_attn_in: float32 [2304], replicated, may hold values from 0.1 to 1.9
- gain_attn_out: float32 [2304], replicated, may hold values from 0.1 to 1.9
- gain_ffw_in: float32 [2304], replicated, may hold values from 0.1 to 1.9
- gain_ffw_out: float32 [2304], replicated, may hold values from 0.1 to 1.9
- query_codes: int32 [2304, 2048], P('seq'), may hold values from -128 to 127
- key_integer_codes: int32 [2304, 1024], P('seq'), may hold values from -128 to 127
- value_integer_codes: int32 [2304, 1024], P('seq'), may hold values from -128 to 127
- out_codes: int32 [2304, 2048], P('seq'), may hold values from -128 to 127
- gate_codes: int32 [2304, 9216], P('seq'), may hold values from -128 to 127
- up_codes: int32 [2304, 9216], P('seq'), may hold values from -128 to 127
- down_codes: int32 [2304, 9216], P('seq'), may hold values from -128 to 127
Outputs:
- block_out: bfloat16 [4, 1024, 2304], P('row', 'seq')
- grad_input: float32 [4, 1024, 2304], P('row', 'seq')
- grad_gain_attn_in: float32 [2304], P('seq')
- grad_gain_attn_out: float32 [2304], P('seq')
- grad_gain_ffw_in: float32 [2304], P('seq')
- grad_gain_ffw_out: float32 [2304], P('seq')
- grad_query: float32 [2304, 2048], P('seq')
- grad_key: float32 [2304, 1024], P('seq')
- grad_value: float32 [2304, 1024], P('seq')
- grad_out: float32 [2304, 2048], P('seq')
- grad_gate: float32 [2304, 9216], P('seq')
- grad_up: float32 [2304, 9216], P('seq')
- grad_down: float32 [2304, 9216], P('seq')
The draws below stay inside these ranges and needn't reach their ends.
Inputs may be any that keep to these rules, and one draw needn't show every extreme that they name: `doc_lengths`: in each row the lengths sum to 1024; one document, never the first or the last, holds 896 tokens, and the others hold 128 tokens together.
All inputs are finite; a program needn't handle non-finite values.
Results may differ from the reference program's by a relative error of at most 0.023.
Values may be sent and summed in bfloat16 or wider, within the bound.
No kernel may reach another device: no remote copies, remote signals or barrier semaphores. Data moves between devices by JAX's collectives and lax.ppermute only.
A program may use at most 640 MiB of HBM per device.

```python
import jax
import jax.numpy as jnp
from jax import lax

MODEL_WIDTH = 2304
QUERY_HEADS = 8
KEY_VALUE_HEADS = 4
HEAD_SIZE = 256
FF = 9216
DOCS = 8
SOFTCAP = 15
PACKED_LENGTH = 1024
TOK_SHARD = 128
ROWS = 4


def packed_lengths(row_key):
    place_key, cut_key = jax.random.split(row_key)
    long_slot = jax.random.randint(place_key, (), 1, DOCS - 1, dtype=jnp.int32)
    cut_points = jnp.sort(jax.random.permutation(cut_key, TOK_SHARD - 1)[:DOCS - 2] + 1).astype(jnp.int32)
    bounds = jnp.concatenate([jnp.zeros((1,), jnp.int32), cut_points, jnp.full((1,), TOK_SHARD, jnp.int32)])
    short_docs = bounds[1:] - bounds[:-1]
    slot_ids = jnp.arange(DOCS, dtype=jnp.int32)
    earlier = short_docs[jnp.clip(slot_ids, 0, DOCS - 2)]
    later_docs = short_docs[jnp.clip(slot_ids - 1, 0, DOCS - 2)]
    long_length = jnp.full((DOCS,), PACKED_LENGTH - TOK_SHARD, jnp.int32)
    return jnp.where(slot_ids < long_slot, earlier, jnp.where(slot_ids == long_slot, long_length, later_docs)).astype(jnp.int32)


def draw_doc_lengths(key, part):
    key = jax.random.fold_in(key, 11)
    row_keys = jax.random.split(key, ROWS)
    return jax.vmap(packed_lengths)(row_keys)


def with_ends(result, rng, low, largest):
    extent = result.shape
    place = [jax.random.randint(jax.random.fold_in(rng, axis), (), 0, extent[axis]) for axis in range(len(extent))]
    result = result.at[tuple(place)].set(low)
    longest = extent.index(max(extent))
    place[longest] = (place[longest] + 1) % extent[longest]
    return result.at[tuple(place)].set(largest)


def steps_of(own_key, dims, cuts, least, largest):
    def one(position, parts):
        steps = jax.random.uniform(jax.random.fold_in(jax.random.fold_in(own_key, 6), position), (parts,), jnp.float32, least / len(cuts), largest / len(cuts))
        return jnp.repeat(jnp.exp(steps), dims[position] // parts).reshape((-1,) + (1,) * (len(dims) - position - 1))

    gain = one(*cuts[0])
    for cut in cuts[1:]:
        gain = gain * one(*cut)
    return gain


def centred(stream_key, dims, deviation, reach, cuts=(), kind=jnp.bfloat16):
    entries = deviation * jax.random.normal(stream_key, dims, jnp.float32)
    if cuts:
        entries = entries * steps_of(stream_key, dims, cuts, -0.22, 0.18)
    return jnp.clip(entries, -reach, reach).astype(kind)


def setup_inputs(seed: int = 0) -> dict:
    keys = jax.random.split(jax.random.key(seed), 15)
    hidden_in = centred(keys[0], (ROWS, PACKED_LENGTH, MODEL_WIDTH), 1.0, 6.0, ((0, 4), (1, 8)))
    cotangent = centred(keys[1], (ROWS, PACKED_LENGTH, MODEL_WIDTH), 1.0, 6.0, ((0, 4), (1, 8)))
    doc_lengths = draw_doc_lengths(jax.random.fold_in(keys[14], 71), 0)
    gain_attn_in = jnp.clip(1.0 + 0.18 * jax.random.normal(keys[3], (MODEL_WIDTH,), jnp.float32), 0.1, 1.9)
    gain_attn_out = jnp.clip(1.0 + 0.18 * jax.random.normal(keys[4], (MODEL_WIDTH,), jnp.float32), 0.1, 1.9)
    gain_ffw_in = jnp.clip(1.0 + 0.18 * jax.random.normal(keys[5], (MODEL_WIDTH,), jnp.float32), 0.1, 1.9)
    gain_ffw_out = jnp.clip(1.0 + 0.18 * jax.random.normal(keys[6], (MODEL_WIDTH,), jnp.float32), 0.1, 1.9)
    query_codes = with_ends(jax.random.randint(keys[7], (MODEL_WIDTH, QUERY_HEADS * HEAD_SIZE), -128, 128), jax.random.fold_in(keys[7], 1), -128, 127).astype(jnp.int32)
    key_integer_codes = with_ends(jax.random.randint(keys[8], (MODEL_WIDTH, KEY_VALUE_HEADS * HEAD_SIZE), -128, 128), jax.random.fold_in(keys[8], 1), -128, 127).astype(jnp.int32)
    value_integer_codes = with_ends(jax.random.randint(keys[9], (MODEL_WIDTH, KEY_VALUE_HEADS * HEAD_SIZE), -128, 128), jax.random.fold_in(keys[9], 1), -128, 127).astype(jnp.int32)
    out_codes = with_ends(jax.random.randint(keys[10], (MODEL_WIDTH, QUERY_HEADS * HEAD_SIZE), -128, 128), jax.random.fold_in(keys[10], 1), -128, 127).astype(jnp.int32)
    gate_codes = with_ends(jax.random.randint(keys[11], (MODEL_WIDTH, FF), -128, 128), jax.random.fold_in(keys[11], 1), -128, 127).astype(jnp.int32)
    up_codes = with_ends(jax.random.randint(keys[12], (MODEL_WIDTH, FF), -128, 128), jax.random.fold_in(keys[12], 1), -128, 127).astype(jnp.int32)
    down_codes = with_ends(jax.random.randint(keys[13], (MODEL_WIDTH, FF), -128, 128), jax.random.fold_in(keys[13], 1), -128, 127).astype(jnp.int32)
    return dict(hidden_in=hidden_in, cotangent=cotangent, doc_lengths=doc_lengths, gain_attn_in=gain_attn_in, gain_attn_out=gain_attn_out, gain_ffw_in=gain_ffw_in, gain_ffw_out=gain_ffw_out, query_codes=query_codes, key_integer_codes=key_integer_codes, value_integer_codes=value_integer_codes, out_codes=out_codes, gate_codes=gate_codes, up_codes=up_codes, down_codes=down_codes)


epsilon = 1e-06
code_unit = 1.0 / 72.0
key_unit = 1.0 / 44.0
large_negative_fill = -1e+30

@jax.custom_vjp
def low(v):
    return lax.optimization_barrier(v.astype(jnp.bfloat16)).astype(jnp.float32)

@jax.custom_vjp
def low_back(v):
    return v

def low_keep(v):
    return (low(v), None)

def low_pass(kept, grad):
    return (grad,)

def back_keep(v):
    return (v, None)

def back_low(kept, grad):
    return (low(grad),)
low.defvjp(low_keep, low_pass)
low_back.defvjp(back_keep, back_low)

def rms_scale(values):
    return lax.rsqrt(lax.optimization_barrier(jnp.mean(values * values, axis=-1, keepdims=True)) + epsilon)

def norm_gain(values, gain_vector):
    return values * rms_scale(values) * gain_vector

def matmul_high(left_side, right_side):
    return jnp.dot(left_side, right_side, precision=lax.Precision.HIGHEST, preferred_element_type=jnp.float32)

def doc_layout(lengths, first_index, row_count):
    doc_ends = jnp.cumsum(lengths).astype(jnp.int32)
    starts = (doc_ends - lengths).astype(jnp.int32)
    token_index = (first_index + jnp.arange(row_count, dtype=jnp.int32)).astype(jnp.int32)
    doc_number = lax.optimization_barrier(jnp.sum((token_index[:, None] >= doc_ends[None, :]).astype(jnp.int32), axis=1)).astype(jnp.int32)
    picked = doc_number[:, None] == jnp.arange(lengths.shape[0], dtype=jnp.int32)[None, :]
    doc_start = lax.optimization_barrier(jnp.sum(jnp.where(picked, starts[None, :], 0), axis=1)).astype(jnp.int32)
    return (token_index, doc_start)

def rotary_tables(positions, head_size):
    half_size = head_size // 2
    frequencies = 10000.0 ** (-(2.0 * jnp.arange(half_size, dtype=jnp.float32)) / head_size)
    angles = positions.astype(jnp.float32)[:, None] * frequencies[None, :]
    return (jnp.cos(angles), jnp.sin(angles))

def apply_rotary(values, cosine_table, sine_table):
    half_size = values.shape[-1] // 2
    first_half = values[..., :half_size]
    second_half = values[..., half_size:]
    cos_wide = cosine_table[:, None, :]
    sin_wide = sine_table[:, None, :]
    return jnp.concatenate([first_half * cos_wide - second_half * sin_wide, second_half * cos_wide + first_half * sin_wide], axis=-1)

def attend(heads_of_queries, heads_of_keys, heads_of_values, token_index, doc_start):
    rows_per_block = min(512, PACKED_LENGTH)
    count_of_blocks = PACKED_LENGTH // rows_per_block
    heads_per_group = QUERY_HEADS // KEY_VALUE_HEADS
    head_scale = HEAD_SIZE ** (-0.5)
    blocks_of_queries = heads_of_queries.reshape(count_of_blocks, rows_per_block, KEY_VALUE_HEADS, heads_per_group, HEAD_SIZE)
    index_blocks = token_index.reshape(count_of_blocks, rows_per_block)
    start_blocks = doc_start.reshape(count_of_blocks, rows_per_block)
    key_index = jnp.arange(PACKED_LENGTH, dtype=jnp.int32)

    @jax.checkpoint
    def one_block(block_in):
        block_of_queries, index_block, start_block = block_in
        raw_scores = low_back(jnp.einsum('tkgd,rkd->kgtr', block_of_queries, heads_of_keys, precision=lax.Precision.HIGHEST) * head_scale)
        capped = SOFTCAP * jnp.tanh(raw_scores / SOFTCAP)
        visible = (key_index[None, :] <= index_block[:, None]) & (key_index[None, :] >= start_block[:, None])
        probs = jax.nn.softmax(jnp.where(visible, capped, large_negative_fill), axis=-1)
        mixed_rows = jnp.einsum('kgtr,rkd->tkgd', low(probs), heads_of_values, precision=lax.Precision.HIGHEST)
        return mixed_rows.reshape(rows_per_block, QUERY_HEADS * HEAD_SIZE)
    return lax.map(one_block, (blocks_of_queries, index_blocks, start_blocks)).reshape(PACKED_LENGTH, QUERY_HEADS * HEAD_SIZE)

def reference(hidden_in, cotangent, doc_lengths, gain_attn_in, gain_attn_out, gain_ffw_in, gain_ffw_out, query_codes, key_integer_codes, value_integer_codes, out_codes, gate_codes, up_codes, down_codes):
    scale_qk = key_unit * MODEL_WIDTH ** (-0.5)
    scale_in = code_unit * MODEL_WIDTH ** (-0.5)
    scale_out = code_unit * (QUERY_HEADS * HEAD_SIZE) ** (-0.5)
    scale_down = code_unit * FF ** (-0.5)
    w_query = query_codes.astype(jnp.float32) * scale_qk
    w_key = key_integer_codes.astype(jnp.float32) * scale_qk
    w_value = value_integer_codes.astype(jnp.float32) * scale_in
    w_out = out_codes.astype(jnp.float32) * scale_out
    w_gate = (gate_codes // 16 * 16 + 8).astype(jnp.float32) * scale_in
    w_up = (up_codes // 16 * 16 + 8).astype(jnp.float32) * scale_in
    w_down = (down_codes // 64 * 64 + 32).astype(jnp.float32) * scale_down
    params = (gain_attn_in, gain_attn_out, gain_ffw_in, gain_ffw_out, w_query, w_key, w_value, w_out, w_gate, w_up, w_down)

    def row_step(totals, row_in):
        row_tokens, row_upstream, row_lengths = row_in
        token_index, doc_start = doc_layout(row_lengths, jnp.int32(0), PACKED_LENGTH)
        cosine_table, sine_table = rotary_tables(token_index - doc_start, HEAD_SIZE)

        def layer_map(tokens, weights):
            gain_one, gain_two, gain_three, gain_four, wq_full, wk_full, wv_full, wo_full, wg_full, wu_full, wd_full = weights
            normed_in = low(norm_gain(tokens, gain_one))
            query_lin = low_back(matmul_high(normed_in, wq_full))
            key_linear = low_back(matmul_high(normed_in, wk_full))
            value_linear = low_back(matmul_high(normed_in, wv_full))
            heads_of_queries = low(apply_rotary(query_lin.reshape(PACKED_LENGTH, QUERY_HEADS, HEAD_SIZE), cosine_table, sine_table))
            heads_of_keys = low(apply_rotary(key_linear.reshape(PACKED_LENGTH, KEY_VALUE_HEADS, HEAD_SIZE), cosine_table, sine_table))
            heads_of_values = low(value_linear).reshape(PACKED_LENGTH, KEY_VALUE_HEADS, HEAD_SIZE)
            attended = low(low_back(attend(heads_of_queries, heads_of_keys, heads_of_values, token_index, doc_start)))
            attn_proj = low_back(matmul_high(attended, wo_full.T))
            middle = tokens + norm_gain(attn_proj, gain_two)
            normed_mid = low(norm_gain(middle, gain_three))
            gate_lin = low_back(matmul_high(normed_mid, wg_full))
            up_lin = low_back(matmul_high(normed_mid, wu_full))
            mixed_rows = low(jax.nn.gelu(gate_lin, approximate=True) * up_lin)
            ffn_proj = low_back(matmul_high(mixed_rows, wd_full.T))
            return middle + norm_gain(ffn_proj, gain_four)
        block_out, pullback = jax.vjp(layer_map, row_tokens.astype(jnp.float32), params)
        grad_parts = pullback(row_upstream.astype(jnp.float32))
        totals = jax.tree.map(lambda total_part, new_part: total_part + new_part, totals, grad_parts[1])
        return (totals, (block_out.astype(jnp.bfloat16), grad_parts[0]))
    zeros_tree = jax.tree.map(jnp.zeros_like, params)
    totals, (block_rows_out, grad_input) = lax.scan(row_step, zeros_tree, (hidden_in, cotangent, doc_lengths))
    return (block_rows_out, grad_input, totals[0], totals[1], totals[2], totals[3], totals[4], totals[5], totals[6], totals[7], totals[8], totals[9], totals[10])
```

```python
import jax
import jax.numpy as jnp
from jax import lax
from jax.sharding import PartitionSpec as P

MODEL_WIDTH = 2304
QUERY_HEADS = 8
KEY_VALUE_HEADS = 4
HEAD_SIZE = 256
FF = 9216
SOFTCAP = 15


epsilon = 1e-06
code_unit = 1.0 / 72.0
key_unit = 1.0 / 44.0
large_negative_fill = -1e30


def codes_eight(code_block):
    return code_block.astype(jnp.bfloat16)


def codes_four(code_block):
    return (code_block // 16 * 16 + 8).astype(jnp.bfloat16)


def codes_two(code_block):
    return (code_block // 64 * 64 + 32).astype(jnp.bfloat16)


def rms_scale(values):
    return lax.rsqrt(jnp.mean(values * values, axis=-1, keepdims=True) + epsilon)


def norm_gain(values, gain_vector):
    return values * rms_scale(values) * gain_vector


def geglu(gate_values, up_values):
    return jax.nn.gelu(gate_values, approximate=True) * up_values


def cross_rows(left_side, right_side):
    return lax.dot_general(
        left_side, right_side, (((0,), (0,)), ((), ())), preferred_element_type=jnp.float32
    )


def times_transposed(left_side, right_side):
    return lax.dot_general(
        left_side, right_side, (((1,), (1,)), ((), ())), preferred_element_type=jnp.float32
    )


def doc_layout(lengths, first_index, row_count):
    doc_ends = jnp.cumsum(lengths)
    starts = doc_ends - lengths
    token_index = first_index + jnp.arange(row_count, dtype=jnp.int32)
    doc_number = jnp.sum((token_index[:, None] >= doc_ends[None, :]).astype(jnp.int32), axis=1)
    picked = doc_number[:, None] == jnp.arange(lengths.shape[0], dtype=jnp.int32)[None, :]
    doc_start = jnp.sum(jnp.where(picked, starts[None, :], 0), axis=1)
    return (token_index, doc_start)


def rotary_tables(positions, head_size):
    half_size = head_size // 2
    frequencies = 10000.0 ** (-(2.0 * jnp.arange(half_size, dtype=jnp.float32)) / head_size)
    angles = positions.astype(jnp.float32)[:, None] * frequencies[None, :]
    return (jnp.cos(angles), jnp.sin(angles))


def apply_rotary(values, cosine_table, sine_table):
    half_size = values.shape[-1] // 2
    first_half = values[..., :half_size]
    second_half = values[..., half_size:]
    cos_wide = cosine_table[:, None, :]
    sin_wide = sine_table[:, None, :]
    return jnp.concatenate(
        [
            first_half * cos_wide - second_half * sin_wide,
            second_half * cos_wide + first_half * sin_wide,
        ],
        axis=-1,
    )


def inverse_rotary(value_gradients, cosine_table, sine_table):
    half_size = value_gradients.shape[-1] // 2
    first_half = value_gradients[..., :half_size]
    second_half = value_gradients[..., half_size:]
    cos_wide = cosine_table[:, None, :]
    sin_wide = sine_table[:, None, :]
    return jnp.concatenate(
        [
            first_half * cos_wide + second_half * sin_wide,
            second_half * cos_wide - first_half * sin_wide,
        ],
        axis=-1,
    )


def score_grads(
    heads_of_queries,
    head_gradients,
    log_totals,
    deltas,
    query_index,
    query_start,
    heads_of_keys,
    heads_of_values,
    key_index,
):
    head_scale = HEAD_SIZE ** (-0.5)
    raw_scores = (
        jnp.einsum(
            "tkgd,rkd->kgtr", heads_of_queries, heads_of_keys, preferred_element_type=jnp.float32
        )
        * head_scale
    )
    capped = SOFTCAP * jnp.tanh(raw_scores / SOFTCAP)
    visible = (key_index[None, :] <= query_index[:, None]) & (
        key_index[None, :] >= query_start[:, None]
    )
    probs = jnp.where(visible, jnp.exp(capped - log_totals[..., None]), 0.0)
    grad_probs = jnp.einsum(
        "tkgd,rkd->kgtr", head_gradients, heads_of_values, preferred_element_type=jnp.float32
    )
    grad_capped = probs * (grad_probs - deltas[..., None])
    grad_raw = (grad_capped * (1.0 - (capped / SOFTCAP) ** 2)).astype(jnp.bfloat16)
    return (grad_raw, probs.astype(jnp.bfloat16))


def reduce_terms(grad_terms):
    shares = lax.psum_scatter(grad_terms, "seq", scatter_dimension=0, tiled=True)
    return lax.psum(shares, "row")


def token_body(
    hidden_in,
    cotangent,
    doc_lengths,
    gain_attn_in,
    gain_attn_out,
    gain_ffw_in,
    gain_ffw_out,
    query_codes,
    key_integer_codes,
    value_integer_codes,
    out_codes,
    gate_codes,
    up_codes,
    down_codes,
):
    tokens = hidden_in[0].astype(jnp.float32)
    upstream = cotangent[0].astype(jnp.float32)
    lengths = doc_lengths[0]
    resident_rows = tokens.shape[0]
    heads_per_group = QUERY_HEADS // KEY_VALUE_HEADS
    head_scale = HEAD_SIZE ** (-0.5)
    scale_qk = key_unit * MODEL_WIDTH ** (-0.5)
    scale_in = code_unit * MODEL_WIDTH ** (-0.5)
    scale_out = code_unit * (QUERY_HEADS * HEAD_SIZE) ** (-0.5)
    scale_down = code_unit * FF ** (-0.5)
    part_count = 8
    part_width = gate_codes.shape[1] // part_count
    first_row = lax.axis_index("seq") * resident_rows
    local_index, local_start = doc_layout(lengths, first_row, resident_rows)
    cosine_table, sine_table = rotary_tables(local_index - local_start, HEAD_SIZE)

    def attention_weights():
        return (
            lax.all_gather(codes_eight(query_codes), "seq", axis=0, tiled=True),
            lax.all_gather(codes_eight(key_integer_codes), "seq", axis=0, tiled=True),
            lax.all_gather(codes_eight(value_integer_codes), "seq", axis=0, tiled=True),
            lax.all_gather(codes_eight(out_codes), "seq", axis=0, tiled=True),
        )

    def ffn_weights(part_number):
        column_start = part_number * part_width
        column_end = column_start + part_width
        return (
            lax.all_gather(
                codes_four(gate_codes[:, column_start:column_end]), "seq", axis=0, tiled=True
            ),
            lax.all_gather(
                codes_four(up_codes[:, column_start:column_end]), "seq", axis=0, tiled=True
            ),
            lax.all_gather(
                codes_two(down_codes[:, column_start:column_end]), "seq", axis=0, tiled=True
            ),
        )

    attn_set = attention_weights()
    w_query, w_key, w_value, w_out = attn_set
    normed_in = norm_gain(tokens, gain_attn_in).astype(jnp.bfloat16)
    query_lin = jnp.dot(normed_in, w_query, preferred_element_type=jnp.float32) * scale_qk
    key_linear = jnp.dot(normed_in, w_key, preferred_element_type=jnp.float32) * scale_qk
    value_linear = jnp.dot(normed_in, w_value, preferred_element_type=jnp.float32) * scale_in
    rows_of_queries = (
        apply_rotary(
            query_lin.reshape(resident_rows, QUERY_HEADS, HEAD_SIZE), cosine_table, sine_table
        )
        .astype(jnp.bfloat16)
        .reshape(resident_rows, QUERY_HEADS * HEAD_SIZE)
    )
    rows_of_keys = (
        apply_rotary(
            key_linear.reshape(resident_rows, KEY_VALUE_HEADS, HEAD_SIZE), cosine_table, sine_table
        )
        .astype(jnp.bfloat16)
        .reshape(resident_rows, KEY_VALUE_HEADS * HEAD_SIZE)
    )
    rows_of_values = value_linear.astype(jnp.bfloat16)
    heads_of_queries = rows_of_queries.reshape(
        resident_rows, KEY_VALUE_HEADS, heads_per_group, HEAD_SIZE
    )
    running_maximum = jnp.full(
        (KEY_VALUE_HEADS, heads_per_group, resident_rows), large_negative_fill, jnp.float32
    )
    block_of_keys = lax.all_gather(rows_of_keys, "seq", axis=0, tiled=True)
    block_of_values = lax.all_gather(rows_of_values, "seq", axis=0, tiled=True)
    rows_per_block = block_of_keys.shape[0]
    heads_of_keys = block_of_keys.reshape(rows_per_block, KEY_VALUE_HEADS, HEAD_SIZE)
    heads_of_values = block_of_values.reshape(rows_per_block, KEY_VALUE_HEADS, HEAD_SIZE)
    key_index = jnp.arange(rows_per_block, dtype=jnp.int32)
    raw_scores = (
        jnp.einsum(
            "tkgd,rkd->kgtr", heads_of_queries, heads_of_keys, preferred_element_type=jnp.float32
        )
        * head_scale
    )
    capped = SOFTCAP * jnp.tanh(raw_scores / SOFTCAP)
    visible = (key_index[None, :] <= local_index[:, None]) & (
        key_index[None, :] >= local_start[:, None]
    )
    masked = jnp.where(visible, capped, large_negative_fill)
    new_max = jnp.maximum(running_maximum, jnp.max(masked, axis=-1))
    weights = jnp.where(visible, jnp.exp(masked - new_max[..., None]), 0.0)
    run_total = jnp.sum(weights, axis=-1)
    weighted = jnp.einsum(
        "kgtr,rkd->kgtd",
        weights.astype(jnp.bfloat16),
        heads_of_values,
        preferred_element_type=jnp.float32,
    )
    weighted, running_maximum, run_total = (weighted, new_max, run_total)
    attn_heads = weighted / run_total[..., None]
    log_totals = running_maximum + jnp.log(run_total)
    attended = (
        attn_heads.transpose(2, 0, 1, 3)
        .reshape(resident_rows, QUERY_HEADS * HEAD_SIZE)
        .astype(jnp.bfloat16)
    )
    attn_proj = times_transposed(attended, w_out) * scale_out
    middle = tokens + norm_gain(attn_proj, gain_attn_out)
    normed_mid = norm_gain(middle, gain_ffw_in).astype(jnp.bfloat16)
    ffn_proj = jnp.zeros((resident_rows, tokens.shape[1]), jnp.float32)
    gate_store = []
    up_store = []
    mixed_store = []
    ffn_sets = []
    for part_number in range(part_count):
        ffn_set = ffn_weights(part_number)
        w_gate, w_up, w_down = ffn_set
        gate_lin = jnp.dot(normed_mid, w_gate, preferred_element_type=jnp.float32) * scale_in
        up_lin = jnp.dot(normed_mid, w_up, preferred_element_type=jnp.float32) * scale_in
        mixed_rows = geglu(gate_lin, up_lin).astype(jnp.bfloat16)
        ffn_proj = ffn_proj + times_transposed(mixed_rows, w_down) * scale_down
        gate_store.append(gate_lin)
        up_store.append(up_lin)
        mixed_store.append(mixed_rows)
        ffn_sets.append(ffn_set)
    block_out = (middle + norm_gain(ffn_proj, gain_ffw_out)).astype(jnp.bfloat16)
    _, post_pull = jax.vjp(norm_gain, ffn_proj, gain_ffw_out)
    grad_ffn_proj, grad_gain_four = post_pull(upstream)
    grad_ffn_low = grad_ffn_proj.astype(jnp.bfloat16)
    grad_normed_mid = jnp.zeros((resident_rows, tokens.shape[1]), jnp.float32)
    gate_shares = []
    up_shares = []
    down_shares = []
    for part_number in range(part_count):
        back_ffn = ffn_weights(part_number)
        w_gate, w_up, w_down = back_ffn
        grad_mixed = jnp.dot(grad_ffn_low, w_down, preferred_element_type=jnp.float32) * scale_down
        _, geglu_pull = jax.vjp(geglu, gate_store[part_number], up_store[part_number])
        grad_gate_lin, grad_up_lin = geglu_pull(grad_mixed)
        grad_gate_low = grad_gate_lin.astype(jnp.bfloat16)
        grad_up_low = grad_up_lin.astype(jnp.bfloat16)
        grad_normed_mid = (
            grad_normed_mid
            + (times_transposed(grad_gate_low, w_gate) + times_transposed(grad_up_low, w_up))
            * scale_in
        )
        gate_share, up_share, down_share = reduce_terms(
            (
                cross_rows(normed_mid, grad_gate_low),
                cross_rows(normed_mid, grad_up_low),
                cross_rows(grad_ffn_low, mixed_store[part_number]),
            )
        )
        gate_shares.append(gate_share)
        up_shares.append(up_share)
        down_shares.append(down_share)
    _, mid_pull = jax.vjp(norm_gain, middle, gain_ffw_in)
    grad_middle_part, grad_gain_three = mid_pull(grad_normed_mid)
    grad_middle = upstream + grad_middle_part
    _, attn_pull = jax.vjp(norm_gain, attn_proj, gain_attn_out)
    grad_attn_proj, grad_gain_two = attn_pull(grad_middle)
    grad_proj_low = grad_attn_proj.astype(jnp.bfloat16)
    back_attn = attention_weights()
    back_query, back_key, back_value, back_out = back_attn
    grad_attended = jnp.dot(grad_proj_low, back_out, preferred_element_type=jnp.float32) * scale_out
    gradient_attention_narrow = grad_attended.astype(jnp.bfloat16)
    head_gradients = gradient_attention_narrow.reshape(
        resident_rows, KEY_VALUE_HEADS, heads_per_group, HEAD_SIZE
    )
    deltas = jnp.sum(
        gradient_attention_narrow.astype(jnp.float32)
        .reshape(resident_rows, KEY_VALUE_HEADS, heads_per_group, HEAD_SIZE)
        .transpose(1, 2, 0, 3)
        * attn_heads,
        axis=-1,
    )
    block_of_keys = lax.all_gather(rows_of_keys, "seq", axis=0, tiled=True)
    block_of_values = lax.all_gather(rows_of_values, "seq", axis=0, tiled=True)
    rows_per_block = block_of_keys.shape[0]
    heads_of_keys = block_of_keys.reshape(rows_per_block, KEY_VALUE_HEADS, HEAD_SIZE)
    heads_of_values = block_of_values.reshape(rows_per_block, KEY_VALUE_HEADS, HEAD_SIZE)
    key_index = jnp.arange(rows_per_block, dtype=jnp.int32)
    grad_raw, probs_low = score_grads(
        heads_of_queries,
        head_gradients,
        log_totals,
        deltas,
        local_index,
        local_start,
        heads_of_keys,
        heads_of_values,
        key_index,
    )
    grad_query_heads = (
        jnp.einsum("kgtr,rkd->tkgd", grad_raw, heads_of_keys, preferred_element_type=jnp.float32)
        * head_scale
    )
    resident_keys = rows_of_keys.reshape(resident_rows, KEY_VALUE_HEADS, HEAD_SIZE)
    resident_values = rows_of_values.reshape(resident_rows, KEY_VALUE_HEADS, HEAD_SIZE)
    block_of_queries = lax.all_gather(
        rows_of_queries.astype(jnp.float32), "seq", axis=0, tiled=True
    )
    block_gradient = lax.all_gather(
        gradient_attention_narrow.astype(jnp.float32), "seq", axis=0, tiled=True
    )
    lse_block = lax.all_gather(log_totals.transpose(2, 0, 1), "seq", axis=0, tiled=True)
    delta_block = lax.all_gather(deltas.transpose(2, 0, 1), "seq", axis=0, tiled=True)
    rows_per_block = block_of_queries.shape[0]
    foreign_queries = block_of_queries.astype(jnp.bfloat16).reshape(
        rows_per_block, KEY_VALUE_HEADS, heads_per_group, HEAD_SIZE
    )
    foreign_gradients = block_gradient.astype(jnp.bfloat16).reshape(
        rows_per_block, KEY_VALUE_HEADS, heads_per_group, HEAD_SIZE
    )
    remote_index, remote_start = doc_layout(lengths, jnp.int32(0), rows_per_block)
    grad_raw, probs_low = score_grads(
        foreign_queries,
        foreign_gradients,
        lse_block.transpose(1, 2, 0),
        delta_block.transpose(1, 2, 0),
        remote_index,
        remote_start,
        resident_keys,
        resident_values,
        local_index,
    )
    key_gradients = (
        jnp.einsum("kgtr,tkgd->rkd", grad_raw, foreign_queries, preferred_element_type=jnp.float32)
        * head_scale
    )
    value_gradients = jnp.einsum(
        "kgtr,tkgd->rkd", probs_low, foreign_gradients, preferred_element_type=jnp.float32
    )
    grad_query_lin = (
        inverse_rotary(
            grad_query_heads.reshape(resident_rows, QUERY_HEADS, HEAD_SIZE),
            cosine_table,
            sine_table,
        )
        .reshape(resident_rows, QUERY_HEADS * HEAD_SIZE)
        .astype(jnp.bfloat16)
    )
    grad_key_lin = (
        inverse_rotary(key_gradients, cosine_table, sine_table)
        .reshape(resident_rows, KEY_VALUE_HEADS * HEAD_SIZE)
        .astype(jnp.bfloat16)
    )
    value_linear_gradient = value_gradients.reshape(
        resident_rows, KEY_VALUE_HEADS * HEAD_SIZE
    ).astype(jnp.bfloat16)
    grad_normed_in = (
        times_transposed(grad_query_lin, back_query) + times_transposed(grad_key_lin, back_key)
    ) * scale_qk + times_transposed(value_linear_gradient, back_value) * scale_in
    _, in_pull = jax.vjp(norm_gain, tokens, gain_attn_in)
    grad_tokens_part, grad_gain_one = in_pull(grad_normed_in)
    grad_input = grad_middle + grad_tokens_part
    attn_shares = reduce_terms(
        (
            cross_rows(normed_in, grad_query_lin),
            cross_rows(normed_in, grad_key_lin),
            cross_rows(normed_in, value_linear_gradient),
            cross_rows(grad_proj_low, attended),
            grad_gain_one,
            grad_gain_two,
            grad_gain_three,
            grad_gain_four,
        )
    )
    return (
        block_out[None],
        grad_input[None],
        attn_shares[4],
        attn_shares[5],
        attn_shares[6],
        attn_shares[7],
        attn_shares[0],
        attn_shares[1],
        attn_shares[2],
        attn_shares[3],
        jnp.concatenate(gate_shares, axis=1),
        jnp.concatenate(up_shares, axis=1),
        jnp.concatenate(down_shares, axis=1),
    )


def seq_swap(block, bit):
    return lax.ppermute(block, "seq", [(place, place ^ bit) for place in range(8)])


def row_swap(block, bit):
    return lax.ppermute(block, "row", [(place, place ^ bit) for place in range(4)])


def bf(values):
    return values.astype(jnp.bfloat16)


def wide(values):
    return values.astype(jnp.float32)


RELATIVE = (0, 2, 4, 6, 1, 3, 5, 7)


def gather_row(block):
    half = block.shape[0] // 2
    from_x = seq_swap(block, 2)
    from_y = seq_swap(block, 4)
    far_first = seq_swap(from_y[:half], 2)
    far_last = seq_swap(from_x[half:], 4)
    mine = jnp.concatenate([block, from_x, from_y, far_first, far_last])
    return jnp.concatenate([mine, seq_swap(mine, 1)])


def other_core(rows):
    middle = rows.shape[0] // 2
    theirs = seq_swap(rows, 1)
    return jnp.concatenate([theirs[middle:], theirs[:middle]])


def scatter_row(partial_rows, row_count):
    middle = row_count // 2
    unit = row_count // 8
    half = unit // 2
    theirs = seq_swap(bf(partial_rows(middle, row_count)), 1)
    mine = partial_rows(0, middle) + wide(theirs)
    here, by_x, by_y, far = (mine[i * unit : (i + 1) * unit] for i in range(4))
    from_x = seq_swap(bf(jnp.concatenate([by_x[:half], far[:half]])), 2)
    from_y = seq_swap(bf(jnp.concatenate([by_y[half:], far[half:]])), 4)
    last_y = seq_swap(bf(by_y[:half] + wide(from_x[half:])), 4)
    last_x = seq_swap(bf(by_x[half:] + wide(from_y[half:])), 2)
    return jnp.concatenate(
        [
            here[:half] + wide(from_x[:half]) + wide(last_y),
            here[half:] + wide(from_y[:half]) + wide(last_x),
        ]
    )


def spread_columns(code_rows):
    rows, columns = code_rows.shape
    blocks = code_rows.reshape(rows, 8, columns // 8).transpose(1, 0, 2)
    return lax.all_to_all(blocks, "seq", 0, 0, tiled=True).reshape(rows * 8, columns // 8)


def spread_rows(gradient):
    rows, columns = gradient.shape
    blocks = lax.all_to_all(
        bf(gradient).reshape(8, rows // 8, columns), "seq", 0, 0, tiled=True
    )
    return wide(blocks.transpose(1, 0, 2).reshape(rows // 8, columns * 8))


def dot(left, right):
    return jnp.dot(left, right, preferred_element_type=jnp.float32)


def turn(values, cosine, sine):
    half = values.shape[-1] // 2
    first, last = values[..., :half], values[..., half:]
    return jnp.concatenate([first * cosine - last * sine, last * cosine + first * sine], axis=-1)


def norm_back(values, gain, upstream):
    scale = rms_scale(values)
    lifted = upstream * gain
    shared = jnp.mean(lifted * values, axis=-1, keepdims=True)
    gradient = scale * lifted - values * (scale * scale * scale) * shared
    return gradient, jnp.sum(upstream * values * scale, axis=0)


def geglu_back(gate, up, grad_mixed):
    mixed, pull = jax.vjp(geglu, gate, up)
    grad_gate, grad_up = pull(grad_mixed)
    return bf(mixed), bf(grad_gate), bf(grad_up)


def plane_body(
    hidden_in,
    cotangent,
    doc_lengths,
    gain_attn_in,
    gain_attn_out,
    gain_ffw_in,
    gain_ffw_out,
    query_codes,
    key_integer_codes,
    value_integer_codes,
    out_codes,
    gate_codes,
    up_codes,
    down_codes,
):
    lengths = doc_lengths[0]
    block_rows, width = hidden_in.shape[1:]
    row_length = block_rows * 8
    place = lax.axis_index("seq")
    core = place % 2
    head = HEAD_SIZE
    half = head // 2
    scale_qk = key_unit * MODEL_WIDTH ** (-0.5)
    scale_in = code_unit * MODEL_WIDTH ** (-0.5)
    scale_out = code_unit * (QUERY_HEADS * HEAD_SIZE) ** (-0.5)
    scale_down = code_unit * FF ** (-0.5)
    head_scale = HEAD_SIZE ** (-0.5)

    model_rows = query_codes.shape[0]
    attn_blocks = jnp.concatenate(
        [
            codes_eight(codes).reshape(model_rows, 8, codes.shape[1] // 8)
            for codes in (query_codes, key_integer_codes, value_integer_codes, out_codes)
        ],
        axis=2,
    )
    attn_weights = spread_columns(attn_blocks.reshape(model_rows, -1))
    w_attn_in = attn_weights[:, : 2 * head]
    w_out = attn_weights[:, 2 * head :]
    w_gate = spread_columns(codes_four(gate_codes))
    w_up = spread_columns(codes_four(up_codes))
    w_down = spread_columns(codes_two(down_codes))

    token_blocks = [(place ^ k) * block_rows + jnp.arange(block_rows) for k in RELATIVE]
    token_index = jnp.concatenate(token_blocks).astype(jnp.int32)
    ends = jnp.cumsum(lengths)
    past = token_index[:, None] >= ends[None, :]
    doc_start = jnp.max(jnp.where(past, ends[None, :], 0), axis=1)
    cosine, sine = rotary_tables(token_index - doc_start, head)
    visible = (token_index[None, :] <= token_index[:, None]) & (
        token_index[None, :] >= doc_start[:, None]
    )

    tokens = wide(hidden_in[0])
    upstream = wide(cotangent[0])
    row_tokens = gather_row(hidden_in[0])
    normed_in = bf(norm_gain(wide(row_tokens), gain_attn_in))
    linear = dot(normed_in, w_attn_in)
    query = bf(turn(linear[:, :head] * scale_qk, cosine, sine))
    key_half = linear[:, head : head + half] * scale_qk
    value_half = bf(linear[:, head + half :] * scale_in)
    key_other = other_core(key_half)
    value_other = other_core(value_half)

    def pair(own, other):
        return jnp.where(
            core == 0,
            jnp.concatenate([own, other], axis=-1),
            jnp.concatenate([other, own], axis=-1),
        )

    key = bf(turn(pair(key_half, key_other), cosine, sine))
    value = pair(value_half, value_other)
    bend = jnp.tanh(times_transposed(query, key) * (head_scale / SOFTCAP))
    weights = jnp.where(visible, jnp.exp(SOFTCAP * bend), 0.0)
    totals = jnp.sum(weights, axis=-1, keepdims=True)
    attended_wide = dot(bf(weights), value) / totals
    attended = bf(attended_wide)
    attn_proj = scale_out * scatter_row(
        lambda a, b: times_transposed(attended[a:b], w_out), row_length
    )
    middle = tokens + norm_gain(attn_proj, gain_attn_out)
    normed_mid = bf(norm_gain(middle, gain_ffw_in))

    row_mid = gather_row(normed_mid)
    gate = dot(row_mid, w_gate) * scale_in
    up = dot(row_mid, w_up) * scale_in
    mixed = bf(geglu(gate, up))
    ffn_proj = scale_down * scatter_row(
        lambda a, b: times_transposed(mixed[a:b], w_down), row_length
    )
    block_out = bf(middle + norm_gain(ffn_proj, gain_ffw_out))
    grad_ffn, grad_gain_four = norm_back(ffn_proj, gain_ffw_out, upstream)
    grad_ffn_low = bf(grad_ffn)

    others_mid = gather_row(jnp.concatenate([row_swap(normed_mid, bit) for bit in (1, 2, 3)]))
    others_ffn = gather_row(jnp.concatenate([row_swap(grad_ffn_low, bit) for bit in (1, 2, 3)]))

    row_ffn = gather_row(grad_ffn_low)
    grad_mixed = dot(row_ffn, w_down) * scale_down
    _, grad_gate, grad_up = geglu_back(gate, up, grad_mixed)
    grad_mid = scale_in * scatter_row(
        lambda a, b: times_transposed(grad_gate[a:b], w_gate)
        + times_transposed(grad_up[a:b], w_up),
        row_length,
    )
    grad_middle_part, grad_gain_three = norm_back(middle, gain_ffw_in, grad_mid)
    grad_middle = upstream + grad_middle_part
    grad_proj, grad_gain_two = norm_back(attn_proj, gain_attn_out, grad_middle)

    row_proj = gather_row(bf(grad_proj))
    grad_attended = bf(dot(row_proj, w_out) * scale_out)
    delta = jnp.sum(wide(grad_attended) * attended_wide, axis=-1, keepdims=True)
    probs = weights / totals
    grad_probs = times_transposed(grad_attended, value)
    grad_raw = bf(probs * (grad_probs - delta) * (1.0 - bend * bend))
    grad_query = bf(turn(dot(grad_raw, key) * head_scale, cosine, -sine))
    key_part = cross_rows(grad_raw, query) * head_scale
    value_part = cross_rows(bf(probs), grad_attended)

    def own_half(values, side):
        return lax.dynamic_slice_in_dim(values, side * half, half, axis=1)

    key_sum = key_part + other_core(key_part)
    grad_key = bf(own_half(turn(key_sum, cosine, -sine), core))
    grad_value = bf(own_half(value_part, core) + other_core(own_half(value_part, 1 - core)))
    grad_linear = jnp.concatenate([grad_query, grad_key, grad_value], axis=1)
    scaled_linear = (grad_linear[:, : head + half], grad_linear[:, head + half :])
    grad_in = scatter_row(
        lambda a, b: scale_qk * times_transposed(scaled_linear[0][a:b], w_attn_in[:, : head + half])
        + scale_in * times_transposed(scaled_linear[1][a:b], w_attn_in[:, head + half :]),
        row_length,
    )
    grad_tokens, grad_gain_one = norm_back(tokens, gain_attn_in, grad_in)
    grad_input = grad_middle + grad_tokens

    other_gate = dot(others_mid, w_gate) * scale_in
    other_up = dot(others_mid, w_up) * scale_in
    other_grad = dot(others_ffn, w_down) * scale_down
    other_mixed, other_grad_gate, other_grad_up = geglu_back(other_gate, other_up, other_grad)
    grad_w_down = spread_rows(cross_rows(row_ffn, mixed) + cross_rows(others_ffn, other_mixed))
    grad_w_gate = spread_rows(
        cross_rows(row_mid, grad_gate) + cross_rows(others_mid, other_grad_gate)
    )
    grad_w_up = spread_rows(cross_rows(row_mid, grad_up) + cross_rows(others_mid, other_grad_up))

    own_part = jnp.concatenate(
        [cross_rows(normed_in, grad_linear), cross_rows(row_proj, attended)], axis=1
    )
    columns = own_part.shape[1]
    quarter = model_rows // 4
    row_place = lax.axis_index("row")
    low_bit, high_bit = row_place % 2, row_place // 2
    quarters = bf(own_part).reshape(8, 2, 2, quarter, columns)

    def halve(terms, bit, axis, side):
        kept = lax.dynamic_index_in_dim(terms, side, axis, keepdims=False)
        sent = lax.dynamic_index_in_dim(terms, 1 - side, axis, keepdims=False)
        return bf(wide(kept) + wide(row_swap(sent, bit)))

    summed = halve(halve(quarters, 1, 2, low_bit), 2, 1, high_bit)
    blocks = lax.all_to_all(summed, "seq", 0, 0, tiled=True).transpose(1, 0, 2)
    blocks = wide(lax.all_gather(blocks, "row", axis=0, tiled=True))
    cuts = (0, head, head + half, 2 * head, 3 * head)
    attn_grads = [
        blocks[:, :, a:b].reshape(model_rows, 8 * (b - a)) for a, b in zip(cuts, cuts[1:])
    ]

    gain_terms = jnp.stack(
        [grad_gain_one, grad_gain_two, grad_gain_three, grad_gain_four], axis=1
    )
    gains = lax.psum(
        lax.psum_scatter(gain_terms, "seq", scatter_dimension=0, tiled=True), "row"
    )
    return (
        block_out[None],
        grad_input[None],
        gains[:, 0],
        gains[:, 1],
        gains[:, 2],
        gains[:, 3],
        attn_grads[0],
        attn_grads[1],
        attn_grads[2],
        attn_grads[3],
        grad_w_gate,
        grad_w_up,
        grad_w_down,
    )


def solution(mesh):
    body = plane_body if dict(mesh.shape) == {"seq": 8, "row": 4} else token_body
    return jax.shard_map(
        body,
        mesh=mesh,
        in_specs=(
            P("row", "seq", None),
            P("row", "seq", None),
            P("row", None),
            P(),
            P(),
            P(),
            P(),
            P("seq", None),
            P("seq", None),
            P("seq", None),
            P("seq", None),
            P("seq", None),
            P("seq", None),
            P("seq", None),
        ),
        out_specs=(
            P("row", "seq", None),
            P("row", "seq", None),
            P("seq"),
            P("seq"),
            P("seq"),
            P("seq"),
            P("seq", None),
            P("seq", None),
            P("seq", None),
            P("seq", None),
            P("seq", None),
            P("seq", None),
            P("seq", None),
        ),
        check_vma=False,
    )
```

```python
import functools

import jax
import jax.numpy as jnp
from jax import lax
from jax.experimental import pallas as pl
from jax.experimental.pallas import tpu as pltpu
from jax.sharding import PartitionSpec as P

MODEL_WIDTH = 2304
QUERY_HEADS = 8
KEY_VALUE_HEADS = 4
HEAD_SIZE = 256
FF = 9216
SOFTCAP = 15


epsilon = 1e-06
code_unit = 1.0 / 72.0
key_unit = 1.0 / 44.0
large_negative_fill = -1e30


def codes_eight(code_block):
    return code_block.astype(jnp.bfloat16)


def codes_four(code_block):
    return (code_block // 16 * 16 + 8).astype(jnp.bfloat16)


def codes_two(code_block):
    return (code_block // 64 * 64 + 32).astype(jnp.bfloat16)


def rms_scale(values):
    return lax.rsqrt(jnp.mean(values * values, axis=-1, keepdims=True) + epsilon)


def norm_gain(values, gain_vector):
    return values * rms_scale(values) * gain_vector


def geglu(gate_values, up_values):
    return jax.nn.gelu(gate_values, approximate=True) * up_values


def cross_rows(left_side, right_side):
    return lax.dot_general(
        left_side, right_side, (((0,), (0,)), ((), ())), preferred_element_type=jnp.float32
    )


def times_transposed(left_side, right_side):
    return lax.dot_general(
        left_side, right_side, (((1,), (1,)), ((), ())), preferred_element_type=jnp.float32
    )


def doc_layout(lengths, first_index, row_count):
    doc_ends = jnp.cumsum(lengths)
    starts = doc_ends - lengths
    token_index = first_index + jnp.arange(row_count, dtype=jnp.int32)
    doc_number = jnp.sum((token_index[:, None] >= doc_ends[None, :]).astype(jnp.int32), axis=1)
    picked = doc_number[:, None] == jnp.arange(lengths.shape[0], dtype=jnp.int32)[None, :]
    doc_start = jnp.sum(jnp.where(picked, starts[None, :], 0), axis=1)
    return (token_index, doc_start)


def rotary_tables(positions, head_size):
    half_size = head_size // 2
    frequencies = 10000.0 ** (-(2.0 * jnp.arange(half_size, dtype=jnp.float32)) / head_size)
    angles = positions.astype(jnp.float32)[:, None] * frequencies[None, :]
    return (jnp.cos(angles), jnp.sin(angles))


def apply_rotary(values, cosine_table, sine_table):
    half_size = values.shape[-1] // 2
    first_half = values[..., :half_size]
    second_half = values[..., half_size:]
    cos_wide = cosine_table[:, None, :]
    sin_wide = sine_table[:, None, :]
    return jnp.concatenate(
        [
            first_half * cos_wide - second_half * sin_wide,
            second_half * cos_wide + first_half * sin_wide,
        ],
        axis=-1,
    )


def inverse_rotary(value_gradients, cosine_table, sine_table):
    half_size = value_gradients.shape[-1] // 2
    first_half = value_gradients[..., :half_size]
    second_half = value_gradients[..., half_size:]
    cos_wide = cosine_table[:, None, :]
    sin_wide = sine_table[:, None, :]
    return jnp.concatenate(
        [
            first_half * cos_wide + second_half * sin_wide,
            second_half * cos_wide - first_half * sin_wide,
        ],
        axis=-1,
    )


def score_grads(
    heads_of_queries,
    head_gradients,
    log_totals,
    deltas,
    query_index,
    query_start,
    heads_of_keys,
    heads_of_values,
    key_index,
):
    head_scale = HEAD_SIZE ** (-0.5)
    raw_scores = (
        jnp.einsum(
            "tkgd,rkd->kgtr", heads_of_queries, heads_of_keys, preferred_element_type=jnp.float32
        )
        * head_scale
    )
    capped = SOFTCAP * jnp.tanh(raw_scores / SOFTCAP)
    visible = (key_index[None, :] <= query_index[:, None]) & (
        key_index[None, :] >= query_start[:, None]
    )
    probs = jnp.where(visible, jnp.exp(capped - log_totals[..., None]), 0.0)
    grad_probs = jnp.einsum(
        "tkgd,rkd->kgtr", head_gradients, heads_of_values, preferred_element_type=jnp.float32
    )
    grad_capped = probs * (grad_probs - deltas[..., None])
    grad_raw = (grad_capped * (1.0 - (capped / SOFTCAP) ** 2)).astype(jnp.bfloat16)
    return (grad_raw, probs.astype(jnp.bfloat16))


def reduce_terms(grad_terms):
    shares = lax.psum_scatter(grad_terms, "seq", scatter_dimension=0, tiled=True)
    return lax.psum(shares, "row")


def token_body(
    hidden_in,
    cotangent,
    doc_lengths,
    gain_attn_in,
    gain_attn_out,
    gain_ffw_in,
    gain_ffw_out,
    query_codes,
    key_integer_codes,
    value_integer_codes,
    out_codes,
    gate_codes,
    up_codes,
    down_codes,
):
    tokens = hidden_in[0].astype(jnp.float32)
    upstream = cotangent[0].astype(jnp.float32)
    lengths = doc_lengths[0]
    resident_rows = tokens.shape[0]
    heads_per_group = QUERY_HEADS // KEY_VALUE_HEADS
    head_scale = HEAD_SIZE ** (-0.5)
    scale_qk = key_unit * MODEL_WIDTH ** (-0.5)
    scale_in = code_unit * MODEL_WIDTH ** (-0.5)
    scale_out = code_unit * (QUERY_HEADS * HEAD_SIZE) ** (-0.5)
    scale_down = code_unit * FF ** (-0.5)
    part_count = 8
    part_width = gate_codes.shape[1] // part_count
    first_row = lax.axis_index("seq") * resident_rows
    local_index, local_start = doc_layout(lengths, first_row, resident_rows)
    cosine_table, sine_table = rotary_tables(local_index - local_start, HEAD_SIZE)

    def attention_weights():
        return (
            lax.all_gather(codes_eight(query_codes), "seq", axis=0, tiled=True),
            lax.all_gather(codes_eight(key_integer_codes), "seq", axis=0, tiled=True),
            lax.all_gather(codes_eight(value_integer_codes), "seq", axis=0, tiled=True),
            lax.all_gather(codes_eight(out_codes), "seq", axis=0, tiled=True),
        )

    def ffn_weights(part_number):
        column_start = part_number * part_width
        column_end = column_start + part_width
        return (
            lax.all_gather(
                codes_four(gate_codes[:, column_start:column_end]), "seq", axis=0, tiled=True
            ),
            lax.all_gather(
                codes_four(up_codes[:, column_start:column_end]), "seq", axis=0, tiled=True
            ),
            lax.all_gather(
                codes_two(down_codes[:, column_start:column_end]), "seq", axis=0, tiled=True
            ),
        )

    attn_set = attention_weights()
    w_query, w_key, w_value, w_out = attn_set
    normed_in = norm_gain(tokens, gain_attn_in).astype(jnp.bfloat16)
    query_lin = jnp.dot(normed_in, w_query, preferred_element_type=jnp.float32) * scale_qk
    key_linear = jnp.dot(normed_in, w_key, preferred_element_type=jnp.float32) * scale_qk
    value_linear = jnp.dot(normed_in, w_value, preferred_element_type=jnp.float32) * scale_in
    rows_of_queries = (
        apply_rotary(
            query_lin.reshape(resident_rows, QUERY_HEADS, HEAD_SIZE), cosine_table, sine_table
        )
        .astype(jnp.bfloat16)
        .reshape(resident_rows, QUERY_HEADS * HEAD_SIZE)
    )
    rows_of_keys = (
        apply_rotary(
            key_linear.reshape(resident_rows, KEY_VALUE_HEADS, HEAD_SIZE), cosine_table, sine_table
        )
        .astype(jnp.bfloat16)
        .reshape(resident_rows, KEY_VALUE_HEADS * HEAD_SIZE)
    )
    rows_of_values = value_linear.astype(jnp.bfloat16)
    heads_of_queries = rows_of_queries.reshape(
        resident_rows, KEY_VALUE_HEADS, heads_per_group, HEAD_SIZE
    )
    running_maximum = jnp.full(
        (KEY_VALUE_HEADS, heads_per_group, resident_rows), large_negative_fill, jnp.float32
    )
    block_of_keys = lax.all_gather(rows_of_keys, "seq", axis=0, tiled=True)
    block_of_values = lax.all_gather(rows_of_values, "seq", axis=0, tiled=True)
    rows_per_block = block_of_keys.shape[0]
    heads_of_keys = block_of_keys.reshape(rows_per_block, KEY_VALUE_HEADS, HEAD_SIZE)
    heads_of_values = block_of_values.reshape(rows_per_block, KEY_VALUE_HEADS, HEAD_SIZE)
    key_index = jnp.arange(rows_per_block, dtype=jnp.int32)
    raw_scores = (
        jnp.einsum(
            "tkgd,rkd->kgtr", heads_of_queries, heads_of_keys, preferred_element_type=jnp.float32
        )
        * head_scale
    )
    capped = SOFTCAP * jnp.tanh(raw_scores / SOFTCAP)
    visible = (key_index[None, :] <= local_index[:, None]) & (
        key_index[None, :] >= local_start[:, None]
    )
    masked = jnp.where(visible, capped, large_negative_fill)
    new_max = jnp.maximum(running_maximum, jnp.max(masked, axis=-1))
    weights = jnp.where(visible, jnp.exp(masked - new_max[..., None]), 0.0)
    run_total = jnp.sum(weights, axis=-1)
    weighted = jnp.einsum(
        "kgtr,rkd->kgtd",
        weights.astype(jnp.bfloat16),
        heads_of_values,
        preferred_element_type=jnp.float32,
    )
    weighted, running_maximum, run_total = (weighted, new_max, run_total)
    attn_heads = weighted / run_total[..., None]
    log_totals = running_maximum + jnp.log(run_total)
    attended = (
        attn_heads.transpose(2, 0, 1, 3)
        .reshape(resident_rows, QUERY_HEADS * HEAD_SIZE)
        .astype(jnp.bfloat16)
    )
    attn_proj = times_transposed(attended, w_out) * scale_out
    middle = tokens + norm_gain(attn_proj, gain_attn_out)
    normed_mid = norm_gain(middle, gain_ffw_in).astype(jnp.bfloat16)
    ffn_proj = jnp.zeros((resident_rows, tokens.shape[1]), jnp.float32)
    gate_store = []
    up_store = []
    mixed_store = []
    ffn_sets = []
    for part_number in range(part_count):
        ffn_set = ffn_weights(part_number)
        w_gate, w_up, w_down = ffn_set
        gate_lin = jnp.dot(normed_mid, w_gate, preferred_element_type=jnp.float32) * scale_in
        up_lin = jnp.dot(normed_mid, w_up, preferred_element_type=jnp.float32) * scale_in
        mixed_rows = geglu(gate_lin, up_lin).astype(jnp.bfloat16)
        ffn_proj = ffn_proj + times_transposed(mixed_rows, w_down) * scale_down
        gate_store.append(gate_lin)
        up_store.append(up_lin)
        mixed_store.append(mixed_rows)
        ffn_sets.append(ffn_set)
    block_out = (middle + norm_gain(ffn_proj, gain_ffw_out)).astype(jnp.bfloat16)
    _, post_pull = jax.vjp(norm_gain, ffn_proj, gain_ffw_out)
    grad_ffn_proj, grad_gain_four = post_pull(upstream)
    grad_ffn_low = grad_ffn_proj.astype(jnp.bfloat16)
    grad_normed_mid = jnp.zeros((resident_rows, tokens.shape[1]), jnp.float32)
    gate_shares = []
    up_shares = []
    down_shares = []
    for part_number in range(part_count):
        back_ffn = ffn_weights(part_number)
        w_gate, w_up, w_down = back_ffn
        grad_mixed = jnp.dot(grad_ffn_low, w_down, preferred_element_type=jnp.float32) * scale_down
        _, geglu_pull = jax.vjp(geglu, gate_store[part_number], up_store[part_number])
        grad_gate_lin, grad_up_lin = geglu_pull(grad_mixed)
        grad_gate_low = grad_gate_lin.astype(jnp.bfloat16)
        grad_up_low = grad_up_lin.astype(jnp.bfloat16)
        grad_normed_mid = (
            grad_normed_mid
            + (times_transposed(grad_gate_low, w_gate) + times_transposed(grad_up_low, w_up))
            * scale_in
        )
        gate_share, up_share, down_share = reduce_terms(
            (
                cross_rows(normed_mid, grad_gate_low),
                cross_rows(normed_mid, grad_up_low),
                cross_rows(grad_ffn_low, mixed_store[part_number]),
            )
        )
        gate_shares.append(gate_share)
        up_shares.append(up_share)
        down_shares.append(down_share)
    _, mid_pull = jax.vjp(norm_gain, middle, gain_ffw_in)
    grad_middle_part, grad_gain_three = mid_pull(grad_normed_mid)
    grad_middle = upstream + grad_middle_part
    _, attn_pull = jax.vjp(norm_gain, attn_proj, gain_attn_out)
    grad_attn_proj, grad_gain_two = attn_pull(grad_middle)
    grad_proj_low = grad_attn_proj.astype(jnp.bfloat16)
    back_attn = attention_weights()
    back_query, back_key, back_value, back_out = back_attn
    grad_attended = jnp.dot(grad_proj_low, back_out, preferred_element_type=jnp.float32) * scale_out
    gradient_attention_narrow = grad_attended.astype(jnp.bfloat16)
    head_gradients = gradient_attention_narrow.reshape(
        resident_rows, KEY_VALUE_HEADS, heads_per_group, HEAD_SIZE
    )
    deltas = jnp.sum(
        gradient_attention_narrow.astype(jnp.float32)
        .reshape(resident_rows, KEY_VALUE_HEADS, heads_per_group, HEAD_SIZE)
        .transpose(1, 2, 0, 3)
        * attn_heads,
        axis=-1,
    )
    block_of_keys = lax.all_gather(rows_of_keys, "seq", axis=0, tiled=True)
    block_of_values = lax.all_gather(rows_of_values, "seq", axis=0, tiled=True)
    rows_per_block = block_of_keys.shape[0]
    heads_of_keys = block_of_keys.reshape(rows_per_block, KEY_VALUE_HEADS, HEAD_SIZE)
    heads_of_values = block_of_values.reshape(rows_per_block, KEY_VALUE_HEADS, HEAD_SIZE)
    key_index = jnp.arange(rows_per_block, dtype=jnp.int32)
    grad_raw, probs_low = score_grads(
        heads_of_queries,
        head_gradients,
        log_totals,
        deltas,
        local_index,
        local_start,
        heads_of_keys,
        heads_of_values,
        key_index,
    )
    grad_query_heads = (
        jnp.einsum("kgtr,rkd->tkgd", grad_raw, heads_of_keys, preferred_element_type=jnp.float32)
        * head_scale
    )
    resident_keys = rows_of_keys.reshape(resident_rows, KEY_VALUE_HEADS, HEAD_SIZE)
    resident_values = rows_of_values.reshape(resident_rows, KEY_VALUE_HEADS, HEAD_SIZE)
    block_of_queries = lax.all_gather(
        rows_of_queries.astype(jnp.float32), "seq", axis=0, tiled=True
    )
    block_gradient = lax.all_gather(
        gradient_attention_narrow.astype(jnp.float32), "seq", axis=0, tiled=True
    )
    lse_block = lax.all_gather(log_totals.transpose(2, 0, 1), "seq", axis=0, tiled=True)
    delta_block = lax.all_gather(deltas.transpose(2, 0, 1), "seq", axis=0, tiled=True)
    rows_per_block = block_of_queries.shape[0]
    foreign_queries = block_of_queries.astype(jnp.bfloat16).reshape(
        rows_per_block, KEY_VALUE_HEADS, heads_per_group, HEAD_SIZE
    )
    foreign_gradients = block_gradient.astype(jnp.bfloat16).reshape(
        rows_per_block, KEY_VALUE_HEADS, heads_per_group, HEAD_SIZE
    )
    remote_index, remote_start = doc_layout(lengths, jnp.int32(0), rows_per_block)
    grad_raw, probs_low = score_grads(
        foreign_queries,
        foreign_gradients,
        lse_block.transpose(1, 2, 0),
        delta_block.transpose(1, 2, 0),
        remote_index,
        remote_start,
        resident_keys,
        resident_values,
        local_index,
    )
    key_gradients = (
        jnp.einsum("kgtr,tkgd->rkd", grad_raw, foreign_queries, preferred_element_type=jnp.float32)
        * head_scale
    )
    value_gradients = jnp.einsum(
        "kgtr,tkgd->rkd", probs_low, foreign_gradients, preferred_element_type=jnp.float32
    )
    grad_query_lin = (
        inverse_rotary(
            grad_query_heads.reshape(resident_rows, QUERY_HEADS, HEAD_SIZE),
            cosine_table,
            sine_table,
        )
        .reshape(resident_rows, QUERY_HEADS * HEAD_SIZE)
        .astype(jnp.bfloat16)
    )
    grad_key_lin = (
        inverse_rotary(key_gradients, cosine_table, sine_table)
        .reshape(resident_rows, KEY_VALUE_HEADS * HEAD_SIZE)
        .astype(jnp.bfloat16)
    )
    value_linear_gradient = value_gradients.reshape(
        resident_rows, KEY_VALUE_HEADS * HEAD_SIZE
    ).astype(jnp.bfloat16)
    grad_normed_in = (
        times_transposed(grad_query_lin, back_query) + times_transposed(grad_key_lin, back_key)
    ) * scale_qk + times_transposed(value_linear_gradient, back_value) * scale_in
    _, in_pull = jax.vjp(norm_gain, tokens, gain_attn_in)
    grad_tokens_part, grad_gain_one = in_pull(grad_normed_in)
    grad_input = grad_middle + grad_tokens_part
    attn_shares = reduce_terms(
        (
            cross_rows(normed_in, grad_query_lin),
            cross_rows(normed_in, grad_key_lin),
            cross_rows(normed_in, value_linear_gradient),
            cross_rows(grad_proj_low, attended),
            grad_gain_one,
            grad_gain_two,
            grad_gain_three,
            grad_gain_four,
        )
    )
    return (
        block_out[None],
        grad_input[None],
        attn_shares[4],
        attn_shares[5],
        attn_shares[6],
        attn_shares[7],
        attn_shares[0],
        attn_shares[1],
        attn_shares[2],
        attn_shares[3],
        jnp.concatenate(gate_shares, axis=1),
        jnp.concatenate(up_shares, axis=1),
        jnp.concatenate(down_shares, axis=1),
    )


VMEM_BYTES = 56 * 1024 * 1024
TILE_VMEM_BYTES = 28 * 1024 * 1024
CROSS_VMEM_BYTES = 40 * 1024 * 1024
GELU_RATE = 0.7978845608028654
TILE = 512
CHUNK = 768


def seq_swap(block, bit):
    return lax.ppermute(block, "seq", [(place, place ^ bit) for place in range(8)])


def row_swap(block, bit):
    return lax.ppermute(block, "row", [(place, place ^ bit) for place in range(4)])


def row_shift(block, step):
    return lax.ppermute(
        block, "row", [(place, place + step) for place in range(4) if 0 <= place + step < 4]
    )


def join_kernel(place_ref, own, *refs):
    below, above, (out_ref, sems) = refs[:3], refs[3:6], refs[6:]

    def join(place):
        copies = [
            pltpu.make_async_copy(
                own if q == place else below[place - q - 1] if q < place else above[q - place - 1],
                out_ref.at[:, q],
                sems.at[q],
            )
            for q in range(4)
        ]
        for copy in copies:
            copy.start()
        for copy in copies:
            copy.wait()

    for place in range(4):
        pl.when(place_ref[0] == place)(functools.partial(join, place))


def ordered_quarters(own, below, above):
    _, rows, columns = own.shape
    joined = pl.pallas_call(
        join_kernel,
        in_specs=[pl.BlockSpec(memory_space=pltpu.SMEM)] + [pl.BlockSpec(memory_space=pl.ANY)] * 7,
        out_specs=pl.BlockSpec(memory_space=pltpu.VMEM),
        out_shape=jax.ShapeDtypeStruct((8, 4, rows, columns), own.dtype),
        scratch_shapes=[pltpu.SemaphoreType.DMA((4,))],
        compiler_params=pltpu.CompilerParams(vmem_limit_bytes=TILE_VMEM_BYTES),
        cost_estimate=pl.CostEstimate(flops=1, bytes_accessed=1, transcendentals=0),
    )(jnp.full((1,), lax.axis_index("row"), jnp.int32), own, *below, *above)
    return joined.reshape(32 * rows, columns)


def bf(values):
    return values.astype(jnp.bfloat16)


def wide(values):
    return values.astype(jnp.float32)


RELATIVE = (0, 2, 4, 6, 1, 3, 5, 7)


def pin(*values):
    return lax.optimization_barrier(values)


def gather_near(block):
    return block, seq_swap(block, 2), seq_swap(block, 4)


def gather_far(block, from_x, from_y):
    half = block.shape[0] // 2
    far_first = seq_swap(from_y[:half], 2)
    far_last = seq_swap(from_x[half:], 4)
    return jnp.concatenate([block, from_x, from_y, far_first, far_last])


def gather_row(block):
    mine = gather_far(*gather_near(block))
    return mine, seq_swap(mine, 1)


def other_core(rows):
    middle = rows.shape[0] // 2
    theirs = seq_swap(rows, 1)
    return jnp.concatenate([theirs[middle:], theirs[:middle]])


def scatter_core(partial_half):
    theirs = seq_swap(partial_half(1, jnp.bfloat16), 1)
    return partial_half(0, jnp.float32) + wide(theirs)


def scatter_near(mine):
    unit = mine.shape[0] // 4
    half = unit // 2
    here, by_x, by_y, far = (mine[i * unit : (i + 1) * unit] for i in range(4))
    from_x = seq_swap(bf(jnp.concatenate([by_x[:half], far[:half]])), 2)
    from_y = seq_swap(bf(jnp.concatenate([by_y[half:], far[half:]])), 4)
    return here, by_x[half:], by_y[:half], from_x, from_y


def scatter_far(here, by_x, by_y, from_x, from_y):
    half = here.shape[0] // 2
    last_y = seq_swap(bf(by_y + wide(from_x[half:])), 4)
    last_x = seq_swap(bf(by_x + wide(from_y[half:])), 2)
    return jnp.concatenate(
        [
            here[:half] + wide(from_x[:half]) + wide(last_y),
            here[half:] + wide(from_y[:half]) + wide(last_x),
        ]
    )


def scatter_row(partial_half):
    return scatter_far(*scatter_near(scatter_core(partial_half)))


def pack_kernel(decoders, place_ref, *refs):
    codes, outs = refs[: len(decoders)], refs[len(decoders) :]
    rows = [bf(wide(decode(code_ref[...]))) for decode, code_ref in zip(decoders, codes)]
    if len(outs) == 1:
        column = 0
        for part in rows:
            outs[0][0, :, column : column + part.shape[1]] = part
            column += part.shape[1]
    else:
        column = 0
        for out_ref in outs:
            out_ref[0] = rows[0][:, column : column + out_ref.shape[2]]
            column += out_ref.shape[2]


def exact_eight(codes):
    return codes


def exact_four(codes):
    return (codes & -16) + 8


def exact_two(codes):
    return (codes & -64) + 32


def pack_codes(code_arrays, decoders, parts, part, widths=None):
    rows = code_arrays[0].shape[0] // parts
    columns = [codes.shape[1] // 8 for codes in code_arrays]
    widths = widths or [sum(columns)]
    found = pl.pallas_call(
        functools.partial(pack_kernel, decoders),
        grid_spec=pltpu.PrefetchScalarGridSpec(
            num_scalar_prefetch=1,
            grid=(8,),
            in_specs=[pl.BlockSpec((rows, c), lambda j, p: (p[0], j)) for c in columns],
            out_specs=[pl.BlockSpec((1, rows, w), lambda j, p: (j, 0, 0)) for w in widths],
        ),
        out_shape=[jax.ShapeDtypeStruct((8, rows, w), jnp.bfloat16) for w in widths],
        compiler_params=pltpu.CompilerParams(vmem_limit_bytes=VMEM_BYTES),
        cost_estimate=pl.CostEstimate(
            flops=0, bytes_accessed=rows * sum(columns) * 48, transcendentals=0
        ),
    )(jnp.full((1,), part, jnp.int32), *code_arrays)
    return found if len(widths) > 1 else found[0]


def unpack_kernel(block_ref, *out_refs):
    rows = block_ref.shape[2]
    column = 0
    for out_ref in out_refs:
        end = column + out_ref.shape[1]
        for part in range(block_ref.shape[0]):
            out_ref[part * rows : (part + 1) * rows, :] = wide(block_ref[part, 0, :, column:end])
        column = end


def unpack_blocks(blocks, widths):
    parts, _, rows, columns = blocks.shape
    return pl.pallas_call(
        unpack_kernel,
        grid=(8,),
        in_specs=[pl.BlockSpec((parts, 1, rows, columns), lambda j: (0, j, 0, 0))],
        out_specs=[pl.BlockSpec((parts * rows, w), lambda j: (0, j)) for w in widths],
        out_shape=[jax.ShapeDtypeStruct((parts * rows, 8 * w), jnp.float32) for w in widths],
        compiler_params=pltpu.CompilerParams(vmem_limit_bytes=VMEM_BYTES),
        cost_estimate=pl.CostEstimate(flops=0, bytes_accessed=6 * blocks.size, transcendentals=0),
    )(blocks)


def trade(blocks):
    return lax.all_to_all(blocks, "seq", 0, 0, tiled=True)


def dot(left, right):
    return jnp.dot(left, right, preferred_element_type=jnp.float32)


def turn(values, cosine, sine):
    half = values.shape[-1] // 2
    first, last = values[..., :half], values[..., half:]
    return jnp.concatenate([first * cosine - last * sine, last * cosine + first * sine], axis=-1)


def norm_back(values, gain, upstream):
    scale = rms_scale(values)
    lifted = upstream * gain
    shared = jnp.mean(lifted * values, axis=-1, keepdims=True)
    gradient = scale * lifted - values * (scale * scale * scale) * shared
    return gradient, jnp.sum(upstream * values * scale, axis=0)


def gelu_parts(values):
    inner = GELU_RATE * (values + 0.044715 * values * values * values)
    bent = jnp.tanh(inner)
    slope = 0.5 * (1.0 + bent) + 0.5 * values * (1.0 - bent * bent) * GELU_RATE * (
        1.0 + 3.0 * 0.044715 * values * values
    )
    return 0.5 * values * (1.0 + bent), slope


def whole_spec(weight):
    return pl.BlockSpec(memory_space=pltpu.VMEM)


def tile_calls(kernel, grid, in_specs, arrays, out_specs, out_shape, scratch=()):
    return pl.pallas_call(
        kernel,
        grid=grid,
        in_specs=in_specs,
        out_specs=out_specs,
        out_shape=out_shape,
        scratch_shapes=scratch,
        compiler_params=pltpu.CompilerParams(vmem_limit_bytes=TILE_VMEM_BYTES),
        cost_estimate=pl.CostEstimate(flops=1, bytes_accessed=1, transcendentals=0),
    )(*arrays)


def source_specs(count, tile, columns, steps):
    specs = [
        pl.BlockSpec((tile, columns), lambda i: (jnp.minimum(i, steps - 1), 0)),
        pl.BlockSpec((tile, columns), lambda i: (jnp.maximum(i - steps, 0), 0)),
    ]
    return specs[:count]


def on_source(steps, sources, action):
    if len(sources) == 1:
        action(sources[0][...])
    else:
        pl.when(pl.program_id(0) < steps)(lambda: action(sources[0][...]))
        pl.when(pl.program_id(0) >= steps)(lambda: action(sources[1][...]))


def up_kernel(steps, scale, *refs):
    *sources, w_gate, w_up, mixed_ref, to_gate_ref, to_up_ref = refs

    def action(rows):
        gate = dot(rows, w_gate[...]) * scale
        up = dot(rows, w_up[...]) * scale
        value, slope = gelu_parts(gate)
        mixed_ref[...] = bf(value * up)
        to_gate_ref[...] = bf(slope * up)
        to_up_ref[...] = bf(value)

    on_source(steps, sources, action)


def up_project(halves, w_gate, w_up, scale):
    rows, columns = halves[0].shape
    hidden = w_gate.shape[1]
    steps = rows // TILE
    return tile_calls(
        functools.partial(up_kernel, steps, scale),
        (len(halves) * steps,),
        source_specs(len(halves), TILE, columns, steps) + [whole_spec(w_gate), whole_spec(w_up)],
        (*halves, w_gate, w_up),
        [pl.BlockSpec((TILE, hidden), lambda i: (i, 0))] * 3,
        [jax.ShapeDtypeStruct((len(halves) * rows, hidden), jnp.bfloat16)] * 3,
    )


def back_kernel(steps, scale, *refs):
    *sources, w_down, to_gate_ref, to_up_ref, gate_ref, up_ref = refs

    def action(rows):
        grad_mixed = dot(rows, w_down[...]) * scale
        gate_ref[...] = bf(grad_mixed * wide(to_gate_ref[...]))
        up_ref[...] = bf(grad_mixed * wide(to_up_ref[...]))

    on_source(steps, sources, action)


def back_project(halves, w_down, factors, scale):
    rows, columns = halves[0].shape
    hidden = w_down.shape[1]
    steps = rows // TILE
    part = pl.BlockSpec((TILE, hidden), lambda i: (i, 0))
    return tile_calls(
        functools.partial(back_kernel, steps, scale),
        (len(halves) * steps,),
        source_specs(len(halves), TILE, columns, steps) + [whole_spec(w_down), part, part],
        (*halves, w_down, *factors),
        [part] * 2,
        [jax.ShapeDtypeStruct((len(halves) * rows, hidden), jnp.bfloat16)] * 2,
    )


def cross_kernel(steps, n_left, n_right, *refs):
    lefts, rights = refs[:n_left], refs[n_left : n_left + n_right]
    out_ref, left_buf, right_buf, total, sems = refs[n_left + n_right :]

    def copies(step):
        slot = step % 2
        found = []
        at = 0
        for left, left_row, right, right_row, count in steps[step]:
            found.append(
                pltpu.make_async_copy(
                    lefts[left].at[pl.ds(left_row, count)],
                    left_buf.at[slot, pl.ds(at, count)],
                    sems.at[slot, len(found)],
                )
            )
            found.append(
                pltpu.make_async_copy(
                    rights[right].at[pl.ds(right_row, count)],
                    right_buf.at[slot, pl.ds(at, count)],
                    sems.at[slot, len(found)],
                )
            )
            at += count
        return found

    for copy in copies(0):
        copy.start()
    chunk = out_ref.shape[2]
    for step in range(len(steps)):
        slot = step % 2
        if step + 1 < len(steps):
            for copy in copies(step + 1):
                copy.start()
        for copy in copies(step):
            copy.wait()

        @pl.loop(0, total.shape[0] // CHUNK)
        def _(m):
            columns = pl.ds(pl.multiple_of(m * CHUNK, CHUNK), CHUNK)
            term = cross_rows(left_buf[slot, :, columns], right_buf[slot])
            if step > 0:
                term = term + total[columns, :]
            total[columns, :] = term

    for place in range(8):
        for part in range(out_ref.shape[0]):
            start = (place * out_ref.shape[0] + part) * chunk
            out_ref[part, place] = bf(total[start : start + chunk, :])


def cross_products(lefts, rights, steps, parts=1):
    wide_rows, columns = lefts[0].shape[1], rights[0].shape[1]
    depth = max(sum(piece[4] for piece in step) for step in steps)
    pieces = max(2 * len(step) for step in steps)
    return pl.pallas_call(
        functools.partial(cross_kernel, steps, len(lefts), len(rights)),
        in_specs=[pl.BlockSpec(memory_space=pl.ANY)] * (len(lefts) + len(rights)),
        out_shape=jax.ShapeDtypeStruct((parts, 8, wide_rows // 8 // parts, columns), jnp.bfloat16),
        scratch_shapes=[
            pltpu.VMEM((2, depth, wide_rows), jnp.bfloat16),
            pltpu.VMEM((2, depth, columns), jnp.bfloat16),
            pltpu.VMEM((wide_rows, columns), jnp.float32),
            pltpu.SemaphoreType.DMA((2, pieces)),
        ],
        compiler_params=pltpu.CompilerParams(vmem_limit_bytes=CROSS_VMEM_BYTES),
        cost_estimate=pl.CostEstimate(flops=1, bytes_accessed=1, transcendentals=0),
    )(*lefts, *rights)


def partial_kernel(*refs):
    out_ref, pairs = refs[-1], refs[:-1]
    total = times_transposed(pairs[0][...], pairs[1][...])
    for left, right in zip(pairs[2::2], pairs[3::2]):
        total = total + times_transposed(left[...], right[...])
    out_ref[...] = total.astype(out_ref.dtype)


def partial_product(pairs, side, kind):
    rows, hidden = pairs[0][0].shape
    columns = pairs[0][1].shape[0]
    half = rows // 2
    left_spec = pl.BlockSpec((half, hidden), lambda i: (side, 0))
    return tile_calls(
        partial_kernel,
        (1,),
        [spec for pair in pairs for spec in (left_spec, whole_spec(pair[1]))],
        [array for pair in pairs for array in pair],
        pl.BlockSpec((half, columns), lambda i: (0, 0)),
        jax.ShapeDtypeStruct((half, columns), kind),
    )


def plane_body(
    hidden_in,
    cotangent,
    doc_lengths,
    gain_attn_in,
    gain_attn_out,
    gain_ffw_in,
    gain_ffw_out,
    query_codes,
    key_integer_codes,
    value_integer_codes,
    out_codes,
    gate_codes,
    up_codes,
    down_codes,
):
    lengths = doc_lengths[0]
    block_rows, width = hidden_in.shape[1:]
    row_length = block_rows * 8
    place = lax.axis_index("seq")
    core = place % 2
    head = HEAD_SIZE
    half = head // 2
    scale_qk = key_unit * MODEL_WIDTH ** (-0.5)
    scale_in = code_unit * MODEL_WIDTH ** (-0.5)
    scale_out = code_unit * (QUERY_HEADS * HEAD_SIZE) ** (-0.5)
    scale_down = code_unit * FF ** (-0.5)
    head_scale = HEAD_SIZE ** (-0.5)

    row_place = lax.axis_index("row")
    model_rows = query_codes.shape[0]
    hidden_part = gate_codes.shape[1] // 8

    def both_ways(below, above):
        return row_shift(below, 1), row_shift(above, -1)

    near_tokens = gather_near(hidden_in[0])
    down_blocks = pack_codes([down_codes], [exact_two], 4, row_place)
    near_tokens, down_blocks = pin(near_tokens, down_blocks)
    own_down = trade(down_blocks)
    attn_blocks = pack_codes(
        [query_codes, key_integer_codes, value_integer_codes, out_codes], [exact_eight] * 4, 1, 0
    )
    attn_blocks, own_down = pin(attn_blocks, own_down)
    attn_weights, gate_blocks, up_blocks, down_one = pin(
        trade(attn_blocks).reshape(width, 3 * head),
        pack_codes([gate_codes], [exact_four], 1, 0),
        pack_codes([up_codes], [exact_four], 1, 0),
        both_ways(own_down, own_down),
    )
    gate_rows = trade(gate_blocks)
    w_attn_in = attn_weights[:, : 2 * head]
    w_out = attn_weights[:, 2 * head :]

    token_blocks = [(place ^ k) * block_rows + jnp.arange(block_rows) for k in RELATIVE]
    token_index = jnp.concatenate(token_blocks).astype(jnp.int32)
    ends = jnp.cumsum(lengths)
    past = token_index[:, None] >= ends[None, :]
    doc_start = jnp.max(jnp.where(past, ends[None, :], 0), axis=1)
    cosine, sine = rotary_tables(token_index - doc_start, head)
    visible = (token_index[None, :] <= token_index[:, None]) & (
        token_index[None, :] >= doc_start[:, None]
    )

    tokens = wide(hidden_in[0])
    upstream = wide(cotangent[0])
    tokens_mine = gather_far(*near_tokens)
    row_tokens = jnp.concatenate([tokens_mine, seq_swap(tokens_mine, 1)])
    normed_in = bf(norm_gain(wide(row_tokens), gain_attn_in))
    linear = dot(normed_in, w_attn_in)
    query = bf(turn(linear[:, :head] * scale_qk, cosine, sine))
    key_half = linear[:, head : head + half] * scale_qk
    value_half = bf(linear[:, head + half :] * scale_in)
    key_other = other_core(key_half)
    value_other = other_core(value_half)

    def pair(own, other):
        return jnp.where(
            core == 0,
            jnp.concatenate([own, other], axis=-1),
            jnp.concatenate([other, own], axis=-1),
        )

    key = bf(turn(pair(key_half, key_other), cosine, sine))
    value = pair(value_half, value_other)
    bend = jnp.tanh(times_transposed(query, key) * (head_scale / SOFTCAP))
    weights = jnp.where(visible, jnp.exp(SOFTCAP * bend), 0.0)
    totals = jnp.sum(weights, axis=-1, keepdims=True)
    attended_wide = dot(bf(weights), value) / totals
    attended = bf(attended_wide)
    attended, down_two = pin(attended, both_ways(*down_one))
    near_half = row_length // 2
    attn_core = scatter_core(
        lambda side, kind: times_transposed(
            attended[side * near_half :][:near_half], w_out
        ).astype(kind)
    )
    attn_core, gate_rows = pin(attn_core, gate_rows)
    attn_near, down_three = pin(scatter_near(attn_core), both_ways(*down_two))
    attn_proj, up_blocks = pin(scale_out * scatter_far(*attn_near), up_blocks)
    up_rows = trade(up_blocks)
    middle = tokens + norm_gain(attn_proj, gain_attn_out)
    normed_mid = bf(norm_gain(middle, gain_ffw_in))

    mid_near, up_rows, mid_one, mid_two, mid_three = pin(
        gather_near(normed_mid),
        up_rows,
        row_swap(normed_mid, 1),
        row_swap(normed_mid, 2),
        row_swap(normed_mid, 3),
    )
    mid_mine = gather_far(*mid_near)
    mid_mine, mid_theirs, w_down = pin(
        mid_mine,
        seq_swap(mid_mine, 1),
        ordered_quarters(own_down, *zip(down_one, down_two, down_three)),
    )
    w_gate, w_up = gate_rows.reshape(width, hidden_part), up_rows.reshape(width, hidden_part)

    def up_again(*halves):
        return up_project(halves, w_gate, w_up, scale_in)

    def back_again(halves, factors):
        return back_project(halves, w_down, factors, scale_down)

    (mixed, *factors), pair_mid_near = pin(
        up_again(mid_mine, mid_theirs), gather_near(jnp.concatenate([mid_one, mid_two]))
    )
    ffn_core, pair_mid_mine = pin(
        scatter_core(lambda side, kind: partial_product([(mixed, w_down)], side, kind)),
        gather_far(*pair_mid_near),
    )
    ffn_near, pair_mid_theirs = pin(scatter_near(ffn_core), seq_swap(pair_mid_mine, 1))
    ffn_proj, third_mid_near = pin(scale_down * scatter_far(*ffn_near), gather_near(mid_three))
    block_out = bf(middle + norm_gain(ffn_proj, gain_ffw_out))
    grad_ffn, grad_gain_four = norm_back(ffn_proj, gain_ffw_out, upstream)
    grad_ffn_low = bf(grad_ffn)
    grad_near, grad_one, third_mid_mine, (mine_mixed, *mine_factors) = pin(
        gather_near(grad_ffn_low),
        row_swap(grad_ffn_low, 1),
        gather_far(*third_mid_near),
        up_again(pair_mid_mine),
    )
    grad_mine = gather_far(*grad_near)
    grad_mine, grad_theirs, grad_two, third_mid_theirs, (theirs_mixed, *theirs_factors) = pin(
        grad_mine,
        seq_swap(grad_mine, 1),
        row_swap(grad_ffn_low, 2),
        seq_swap(third_mid_mine, 1),
        up_again(pair_mid_theirs),
    )
    grads_hidden, pair_grad_near = pin(
        back_again((grad_mine, grad_theirs), factors),
        gather_near(jnp.concatenate([grad_one, grad_two])),
    )
    pairs = list(zip(grads_hidden, (w_gate, w_up)))
    mid_core, pair_grad_mine, grad_three = pin(
        scatter_core(lambda side, kind: partial_product(pairs, side, kind)),
        gather_far(*pair_grad_near),
        row_swap(grad_ffn_low, 3),
    )
    sum_near, third_grad_near, (third_mixed, *third_factors), pair_grad_theirs, mine_hidden = pin(
        scatter_near(mid_core),
        gather_near(grad_three),
        up_again(third_mid_mine, third_mid_theirs),
        seq_swap(pair_grad_mine, 1),
        back_again((pair_grad_mine,), mine_factors),
    )
    third_grad_mine = gather_far(*third_grad_near)
    grad_mid, third_grad_mine, third_grad_theirs, theirs_hidden = pin(
        scale_in * scatter_far(*sum_near),
        third_grad_mine,
        seq_swap(third_grad_mine, 1),
        back_again((pair_grad_theirs,), theirs_factors),
    )
    grad_middle_part, grad_gain_three = norm_back(middle, gain_ffw_in, grad_mid)
    grad_middle = upstream + grad_middle_part
    grad_proj, grad_gain_two = norm_back(attn_proj, gain_attn_out, grad_middle)

    row_half = row_length // 2
    mids = (mid_mine, mid_theirs, pair_mid_mine, pair_mid_theirs, third_mid_mine, third_mid_theirs)
    outs = (
        grad_mine,
        grad_theirs,
        pair_grad_mine,
        pair_grad_theirs,
        third_grad_mine,
        third_grad_theirs,
    )
    steps = (
        ((0, 0, 0, 0, row_half), (1, 0, 0, row_half, row_half)),
        ((2, 0, 1, 0, row_length),),
        ((3, 0, 2, 0, row_length),),
        ((4, 0, 3, 0, row_half), (5, 0, 3, row_half, row_half)),
    )
    proj_near, down_blocks, third_grads = pin(
        gather_near(bf(grad_proj)),
        cross_products(outs, (mixed, mine_mixed, theirs_mixed, third_mixed), steps),
        (third_grad_mine, third_grad_theirs),
    )
    proj_mine, down_blocks = pin(gather_far(*proj_near), down_blocks)
    down_blocks = trade(down_blocks[0])
    row_proj = jnp.concatenate([proj_mine, seq_swap(proj_mine, 1)])

    def halve(terms, bit, axis, side):
        kept = lax.dynamic_index_in_dim(terms, side, axis, keepdims=False)
        sent = lax.dynamic_index_in_dim(terms, 1 - side, axis, keepdims=False)
        return bf(wide(kept) + wide(row_swap(sent, bit)))

    def quarters_of(part):
        return bf(part).reshape(8, 2, 2, model_rows // 4, part.shape[1])

    low_bit, high_bit = row_place % 2, row_place // 2

    grad_attended = bf(dot(row_proj, w_out) * scale_out)
    delta = jnp.sum(wide(grad_attended) * attended_wide, axis=-1, keepdims=True)
    probs = weights / totals
    grad_probs = times_transposed(grad_attended, value)
    grad_raw = bf(probs * (grad_probs - delta) * (1.0 - bend * bend))
    grad_raw, third_grads = pin(grad_raw, third_grads)
    third_hidden = back_again(third_grads, third_factors)
    gate_terms, up_terms = zip(grads_hidden, mine_hidden, theirs_hidden, third_hidden)
    grad_query = bf(turn(dot(grad_raw, key) * head_scale, cosine, -sine))
    key_part = cross_rows(grad_raw, query) * head_scale
    value_part = cross_rows(bf(probs), grad_attended)

    def own_half(values, side):
        return lax.dynamic_slice_in_dim(values, side * half, half, axis=1)

    key_sum = key_part + other_core(key_part)
    grad_key = bf(own_half(turn(key_sum, cosine, -sine), core))
    grad_value = bf(own_half(value_part, core) + other_core(own_half(value_part, 1 - core)))
    grad_linear = jnp.concatenate([grad_query, grad_key, grad_value], axis=1)
    grad_linear, down_blocks, gate_blocks, up_terms = pin(
        grad_linear, down_blocks, cross_products(mids, gate_terms, steps), up_terms
    )
    gate_blocks = trade(gate_blocks[0])

    def grad_in_half(side, kind):
        rows = grad_linear[side * near_half :][:near_half]
        total = scale_qk * times_transposed(
            rows[:, : head + half], w_attn_in[:, : head + half]
        ) + scale_in * times_transposed(rows[:, head + half :], w_attn_in[:, head + half :])
        return total.astype(kind)

    in_core, in_sum, out_sum, up_terms = pin(
        scatter_core(grad_in_half),
        halve(quarters_of(cross_rows(normed_in, grad_linear)), 1, 2, low_bit),
        halve(quarters_of(cross_rows(row_proj, attended)), 1, 2, low_bit),
        up_terms,
    )
    in_sum, out_sum, up_blocks, gate_blocks, in_near = pin(
        halve(in_sum, 2, 1, high_bit),
        halve(out_sum, 2, 1, high_bit),
        cross_products(mids, up_terms, steps),
        gate_blocks,
        scatter_near(in_core),
    )
    grad_in, sums = pin(
        scatter_far(*in_near), trade(jnp.concatenate([in_sum, out_sum], axis=2))
    )
    grad_tokens, grad_gain_one = norm_back(tokens, gain_attn_in, grad_in)
    grad_input = grad_middle + grad_tokens
    gain_terms = jnp.stack([grad_gain_one, grad_gain_two, grad_gain_three, grad_gain_four])
    gain_blocks = trade(gain_terms.reshape(4, 8, model_rows).transpose(1, 0, 2))
    gain_blocks, up_blocks = pin(gain_blocks, up_blocks)
    up_blocks = trade(up_blocks[0])

    def double(blocks, bit, side):
        both_sides = jnp.stack([blocks, row_swap(blocks, bit)])
        return jnp.where(side == 0, both_sides, both_sides[::-1])

    gains = jnp.sum(gain_blocks, axis=0)
    gains = gains + row_swap(gains, 1)
    blocks, gains = pin(double(sums, 2, high_bit), gains + row_swap(gains, 2))
    blocks = double(blocks, 1, low_bit).transpose(1, 0, 2, 3, 4)
    attn_grads = unpack_blocks(blocks.reshape(4, *sums.shape), [head, half, half, head])
    grad_w_gate, grad_w_up, grad_w_down = (
        unpack_blocks(blocks, [hidden_part])[0]
        for blocks in (gate_blocks[None], up_blocks[None], down_blocks[None])
    )

    return (
        block_out[None],
        grad_input[None],
        gains[0],
        gains[1],
        gains[2],
        gains[3],
        attn_grads[0],
        attn_grads[1],
        attn_grads[2],
        attn_grads[3],
        grad_w_gate,
        grad_w_up,
        grad_w_down,
    )


def solution(mesh):
    body = plane_body if dict(mesh.shape) == {"seq": 8, "row": 4} else token_body
    return jax.shard_map(
        body,
        mesh=mesh,
        in_specs=(
            P("row", "seq", None),
            P("row", "seq", None),
            P("row", None),
            P(),
            P(),
            P(),
            P(),
            P("seq", None),
            P("seq", None),
            P("seq", None),
            P("seq", None),
            P("seq", None),
            P("seq", None),
            P("seq", None),
        ),
        out_specs=(
            P("row", "seq", None),
            P("row", "seq", None),
            P("seq"),
            P("seq"),
            P("seq"),
            P("seq"),
            P("seq", None),
            P("seq", None),
            P("seq", None),
            P("seq", None),
            P("seq", None),
            P("seq", None),
            P("seq", None),
        ),
        check_vma=False,
    )
```

```python
import functools

import jax
import jax.numpy as jnp
from jax import lax
from jax.experimental import pallas as pl
from jax.experimental.pallas import tpu as pltpu
from jax.sharding import PartitionSpec as P

MODEL_WIDTH = 2304
QUERY_HEADS = 8
KEY_VALUE_HEADS = 4
HEAD_SIZE = 256
FF = 9216
SOFTCAP = 15


epsilon = 1e-06
code_unit = 1.0 / 72.0
key_unit = 1.0 / 44.0
large_negative_fill = -1e30


def codes_eight(code_block):
    return code_block.astype(jnp.bfloat16)


def codes_four(code_block):
    return (code_block // 16 * 16 + 8).astype(jnp.bfloat16)


def codes_two(code_block):
    return (code_block // 64 * 64 + 32).astype(jnp.bfloat16)


def rms_scale(values):
    return lax.rsqrt(jnp.mean(values * values, axis=-1, keepdims=True) + epsilon)


def norm_gain(values, gain_vector):
    return values * rms_scale(values) * gain_vector


def geglu(gate_values, up_values):
    return jax.nn.gelu(gate_values, approximate=True) * up_values


def cross_rows(left_side, right_side):
    return lax.dot_general(
        left_side, right_side, (((0,), (0,)), ((), ())), preferred_element_type=jnp.float32
    )


def times_transposed(left_side, right_side):
    return lax.dot_general(
        left_side, right_side, (((1,), (1,)), ((), ())), preferred_element_type=jnp.float32
    )


def doc_layout(lengths, first_index, row_count):
    doc_ends = jnp.cumsum(lengths)
    starts = doc_ends - lengths
    token_index = first_index + jnp.arange(row_count, dtype=jnp.int32)
    doc_number = jnp.sum((token_index[:, None] >= doc_ends[None, :]).astype(jnp.int32), axis=1)
    picked = doc_number[:, None] == jnp.arange(lengths.shape[0], dtype=jnp.int32)[None, :]
    doc_start = jnp.sum(jnp.where(picked, starts[None, :], 0), axis=1)
    return (token_index, doc_start)


def rotary_tables(positions, head_size):
    half_size = head_size // 2
    frequencies = 10000.0 ** (-(2.0 * jnp.arange(half_size, dtype=jnp.float32)) / head_size)
    angles = positions.astype(jnp.float32)[:, None] * frequencies[None, :]
    return (jnp.cos(angles), jnp.sin(angles))


def apply_rotary(values, cosine_table, sine_table):
    half_size = values.shape[-1] // 2
    first_half = values[..., :half_size]
    second_half = values[..., half_size:]
    cos_wide = cosine_table[:, None, :]
    sin_wide = sine_table[:, None, :]
    return jnp.concatenate(
        [
            first_half * cos_wide - second_half * sin_wide,
            second_half * cos_wide + first_half * sin_wide,
        ],
        axis=-1,
    )


def inverse_rotary(value_gradients, cosine_table, sine_table):
    half_size = value_gradients.shape[-1] // 2
    first_half = value_gradients[..., :half_size]
    second_half = value_gradients[..., half_size:]
    cos_wide = cosine_table[:, None, :]
    sin_wide = sine_table[:, None, :]
    return jnp.concatenate(
        [
            first_half * cos_wide + second_half * sin_wide,
            second_half * cos_wide - first_half * sin_wide,
        ],
        axis=-1,
    )


def score_grads(
    heads_of_queries,
    head_gradients,
    log_totals,
    deltas,
    query_index,
    query_start,
    heads_of_keys,
    heads_of_values,
    key_index,
):
    head_scale = HEAD_SIZE ** (-0.5)
    raw_scores = (
        jnp.einsum(
            "tkgd,rkd->kgtr", heads_of_queries, heads_of_keys, preferred_element_type=jnp.float32
        )
        * head_scale
    )
    capped = SOFTCAP * jnp.tanh(raw_scores / SOFTCAP)
    visible = (key_index[None, :] <= query_index[:, None]) & (
        key_index[None, :] >= query_start[:, None]
    )
    probs = jnp.where(visible, jnp.exp(capped - log_totals[..., None]), 0.0)
    grad_probs = jnp.einsum(
        "tkgd,rkd->kgtr", head_gradients, heads_of_values, preferred_element_type=jnp.float32
    )
    grad_capped = probs * (grad_probs - deltas[..., None])
    grad_raw = (grad_capped * (1.0 - (capped / SOFTCAP) ** 2)).astype(jnp.bfloat16)
    return (grad_raw, probs.astype(jnp.bfloat16))


def reduce_terms(grad_terms):
    shares = lax.psum_scatter(grad_terms, "seq", scatter_dimension=0, tiled=True)
    return lax.psum(shares, "row")


def token_body(
    hidden_in,
    cotangent,
    doc_lengths,
    gain_attn_in,
    gain_attn_out,
    gain_ffw_in,
    gain_ffw_out,
    query_codes,
    key_integer_codes,
    value_integer_codes,
    out_codes,
    gate_codes,
    up_codes,
    down_codes,
):
    tokens = hidden_in[0].astype(jnp.float32)
    upstream = cotangent[0].astype(jnp.float32)
    lengths = doc_lengths[0]
    resident_rows = tokens.shape[0]
    heads_per_group = QUERY_HEADS // KEY_VALUE_HEADS
    head_scale = HEAD_SIZE ** (-0.5)
    scale_qk = key_unit * MODEL_WIDTH ** (-0.5)
    scale_in = code_unit * MODEL_WIDTH ** (-0.5)
    scale_out = code_unit * (QUERY_HEADS * HEAD_SIZE) ** (-0.5)
    scale_down = code_unit * FF ** (-0.5)
    part_count = 8
    part_width = gate_codes.shape[1] // part_count
    first_row = lax.axis_index("seq") * resident_rows
    local_index, local_start = doc_layout(lengths, first_row, resident_rows)
    cosine_table, sine_table = rotary_tables(local_index - local_start, HEAD_SIZE)

    def attention_weights():
        return (
            lax.all_gather(codes_eight(query_codes), "seq", axis=0, tiled=True),
            lax.all_gather(codes_eight(key_integer_codes), "seq", axis=0, tiled=True),
            lax.all_gather(codes_eight(value_integer_codes), "seq", axis=0, tiled=True),
            lax.all_gather(codes_eight(out_codes), "seq", axis=0, tiled=True),
        )

    def ffn_weights(part_number):
        column_start = part_number * part_width
        column_end = column_start + part_width
        return (
            lax.all_gather(
                codes_four(gate_codes[:, column_start:column_end]), "seq", axis=0, tiled=True
            ),
            lax.all_gather(
                codes_four(up_codes[:, column_start:column_end]), "seq", axis=0, tiled=True
            ),
            lax.all_gather(
                codes_two(down_codes[:, column_start:column_end]), "seq", axis=0, tiled=True
            ),
        )

    attn_set = attention_weights()
    w_query, w_key, w_value, w_out = attn_set
    normed_in = norm_gain(tokens, gain_attn_in).astype(jnp.bfloat16)
    query_lin = jnp.dot(normed_in, w_query, preferred_element_type=jnp.float32) * scale_qk
    key_linear = jnp.dot(normed_in, w_key, preferred_element_type=jnp.float32) * scale_qk
    value_linear = jnp.dot(normed_in, w_value, preferred_element_type=jnp.float32) * scale_in
    rows_of_queries = (
        apply_rotary(
            query_lin.reshape(resident_rows, QUERY_HEADS, HEAD_SIZE), cosine_table, sine_table
        )
        .astype(jnp.bfloat16)
        .reshape(resident_rows, QUERY_HEADS * HEAD_SIZE)
    )
    rows_of_keys = (
        apply_rotary(
            key_linear.reshape(resident_rows, KEY_VALUE_HEADS, HEAD_SIZE), cosine_table, sine_table
        )
        .astype(jnp.bfloat16)
        .reshape(resident_rows, KEY_VALUE_HEADS * HEAD_SIZE)
    )
    rows_of_values = value_linear.astype(jnp.bfloat16)
    heads_of_queries = rows_of_queries.reshape(
        resident_rows, KEY_VALUE_HEADS, heads_per_group, HEAD_SIZE
    )
    running_maximum = jnp.full(
        (KEY_VALUE_HEADS, heads_per_group, resident_rows), large_negative_fill, jnp.float32
    )
    block_of_keys = lax.all_gather(rows_of_keys, "seq", axis=0, tiled=True)
    block_of_values = lax.all_gather(rows_of_values, "seq", axis=0, tiled=True)
    rows_per_block = block_of_keys.shape[0]
    heads_of_keys = block_of_keys.reshape(rows_per_block, KEY_VALUE_HEADS, HEAD_SIZE)
    heads_of_values = block_of_values.reshape(rows_per_block, KEY_VALUE_HEADS, HEAD_SIZE)
    key_index = jnp.arange(rows_per_block, dtype=jnp.int32)
    raw_scores = (
        jnp.einsum(
            "tkgd,rkd->kgtr", heads_of_queries, heads_of_keys, preferred_element_type=jnp.float32
        )
        * head_scale
    )
    capped = SOFTCAP * jnp.tanh(raw_scores / SOFTCAP)
    visible = (key_index[None, :] <= local_index[:, None]) & (
        key_index[None, :] >= local_start[:, None]
    )
    masked = jnp.where(visible, capped, large_negative_fill)
    new_max = jnp.maximum(running_maximum, jnp.max(masked, axis=-1))
    weights = jnp.where(visible, jnp.exp(masked - new_max[..., None]), 0.0)
    run_total = jnp.sum(weights, axis=-1)
    weighted = jnp.einsum(
        "kgtr,rkd->kgtd",
        weights.astype(jnp.bfloat16),
        heads_of_values,
        preferred_element_type=jnp.float32,
    )
    weighted, running_maximum, run_total = (weighted, new_max, run_total)
    attn_heads = weighted / run_total[..., None]
    log_totals = running_maximum + jnp.log(run_total)
    attended = (
        attn_heads.transpose(2, 0, 1, 3)
        .reshape(resident_rows, QUERY_HEADS * HEAD_SIZE)
        .astype(jnp.bfloat16)
    )
    attn_proj = times_transposed(attended, w_out) * scale_out
    middle = tokens + norm_gain(attn_proj, gain_attn_out)
    normed_mid = norm_gain(middle, gain_ffw_in).astype(jnp.bfloat16)
    ffn_proj = jnp.zeros((resident_rows, tokens.shape[1]), jnp.float32)
    gate_store = []
    up_store = []
    mixed_store = []
    ffn_sets = []
    for part_number in range(part_count):
        ffn_set = ffn_weights(part_number)
        w_gate, w_up, w_down = ffn_set
        gate_lin = jnp.dot(normed_mid, w_gate, preferred_element_type=jnp.float32) * scale_in
        up_lin = jnp.dot(normed_mid, w_up, preferred_element_type=jnp.float32) * scale_in
        mixed_rows = geglu(gate_lin, up_lin).astype(jnp.bfloat16)
        ffn_proj = ffn_proj + times_transposed(mixed_rows, w_down) * scale_down
        gate_store.append(gate_lin)
        up_store.append(up_lin)
        mixed_store.append(mixed_rows)
        ffn_sets.append(ffn_set)
    block_out = (middle + norm_gain(ffn_proj, gain_ffw_out)).astype(jnp.bfloat16)
    _, post_pull = jax.vjp(norm_gain, ffn_proj, gain_ffw_out)
    grad_ffn_proj, grad_gain_four = post_pull(upstream)
    grad_ffn_low = grad_ffn_proj.astype(jnp.bfloat16)
    grad_normed_mid = jnp.zeros((resident_rows, tokens.shape[1]), jnp.float32)
    gate_shares = []
    up_shares = []
    down_shares = []
    for part_number in range(part_count):
        back_ffn = ffn_weights(part_number)
        w_gate, w_up, w_down = back_ffn
        grad_mixed = jnp.dot(grad_ffn_low, w_down, preferred_element_type=jnp.float32) * scale_down
        _, geglu_pull = jax.vjp(geglu, gate_store[part_number], up_store[part_number])
        grad_gate_lin, grad_up_lin = geglu_pull(grad_mixed)
        grad_gate_low = grad_gate_lin.astype(jnp.bfloat16)
        grad_up_low = grad_up_lin.astype(jnp.bfloat16)
        grad_normed_mid = (
            grad_normed_mid
            + (times_transposed(grad_gate_low, w_gate) + times_transposed(grad_up_low, w_up))
            * scale_in
        )
        gate_share, up_share, down_share = reduce_terms(
            (
                cross_rows(normed_mid, grad_gate_low),
                cross_rows(normed_mid, grad_up_low),
                cross_rows(grad_ffn_low, mixed_store[part_number]),
            )
        )
        gate_shares.append(gate_share)
        up_shares.append(up_share)
        down_shares.append(down_share)
    _, mid_pull = jax.vjp(norm_gain, middle, gain_ffw_in)
    grad_middle_part, grad_gain_three = mid_pull(grad_normed_mid)
    grad_middle = upstream + grad_middle_part
    _, attn_pull = jax.vjp(norm_gain, attn_proj, gain_attn_out)
    grad_attn_proj, grad_gain_two = attn_pull(grad_middle)
    grad_proj_low = grad_attn_proj.astype(jnp.bfloat16)
    back_attn = attention_weights()
    back_query, back_key, back_value, back_out = back_attn
    grad_attended = jnp.dot(grad_proj_low, back_out, preferred_element_type=jnp.float32) * scale_out
    gradient_attention_narrow = grad_attended.astype(jnp.bfloat16)
    head_gradients = gradient_attention_narrow.reshape(
        resident_rows, KEY_VALUE_HEADS, heads_per_group, HEAD_SIZE
    )
    deltas = jnp.sum(
        gradient_attention_narrow.astype(jnp.float32)
        .reshape(resident_rows, KEY_VALUE_HEADS, heads_per_group, HEAD_SIZE)
        .transpose(1, 2, 0, 3)
        * attn_heads,
        axis=-1,
    )
    block_of_keys = lax.all_gather(rows_of_keys, "seq", axis=0, tiled=True)
    block_of_values = lax.all_gather(rows_of_values, "seq", axis=0, tiled=True)
    rows_per_block = block_of_keys.shape[0]
    heads_of_keys = block_of_keys.reshape(rows_per_block, KEY_VALUE_HEADS, HEAD_SIZE)
    heads_of_values = block_of_values.reshape(rows_per_block, KEY_VALUE_HEADS, HEAD_SIZE)
    key_index = jnp.arange(rows_per_block, dtype=jnp.int32)
    grad_raw, probs_low = score_grads(
        heads_of_queries,
        head_gradients,
        log_totals,
        deltas,
        local_index,
        local_start,
        heads_of_keys,
        heads_of_values,
        key_index,
    )
    grad_query_heads = (
        jnp.einsum("kgtr,rkd->tkgd", grad_raw, heads_of_keys, preferred_element_type=jnp.float32)
        * head_scale
    )
    resident_keys = rows_of_keys.reshape(resident_rows, KEY_VALUE_HEADS, HEAD_SIZE)
    resident_values = rows_of_values.reshape(resident_rows, KEY_VALUE_HEADS, HEAD_SIZE)
    block_of_queries = lax.all_gather(
        rows_of_queries.astype(jnp.float32), "seq", axis=0, tiled=True
    )
    block_gradient = lax.all_gather(
        gradient_attention_narrow.astype(jnp.float32), "seq", axis=0, tiled=True
    )
    lse_block = lax.all_gather(log_totals.transpose(2, 0, 1), "seq", axis=0, tiled=True)
    delta_block = lax.all_gather(deltas.transpose(2, 0, 1), "seq", axis=0, tiled=True)
    rows_per_block = block_of_queries.shape[0]
    foreign_queries = block_of_queries.astype(jnp.bfloat16).reshape(
        rows_per_block, KEY_VALUE_HEADS, heads_per_group, HEAD_SIZE
    )
    foreign_gradients = block_gradient.astype(jnp.bfloat16).reshape(
        rows_per_block, KEY_VALUE_HEADS, heads_per_group, HEAD_SIZE
    )
    remote_index, remote_start = doc_layout(lengths, jnp.int32(0), rows_per_block)
    grad_raw, probs_low = score_grads(
        foreign_queries,
        foreign_gradients,
        lse_block.transpose(1, 2, 0),
        delta_block.transpose(1, 2, 0),
        remote_index,
        remote_start,
        resident_keys,
        resident_values,
        local_index,
    )
    key_gradients = (
        jnp.einsum("kgtr,tkgd->rkd", grad_raw, foreign_queries, preferred_element_type=jnp.float32)
        * head_scale
    )
    value_gradients = jnp.einsum(
        "kgtr,tkgd->rkd", probs_low, foreign_gradients, preferred_element_type=jnp.float32
    )
    grad_query_lin = (
        inverse_rotary(
            grad_query_heads.reshape(resident_rows, QUERY_HEADS, HEAD_SIZE),
            cosine_table,
            sine_table,
        )
        .reshape(resident_rows, QUERY_HEADS * HEAD_SIZE)
        .astype(jnp.bfloat16)
    )
    grad_key_lin = (
        inverse_rotary(key_gradients, cosine_table, sine_table)
        .reshape(resident_rows, KEY_VALUE_HEADS * HEAD_SIZE)
        .astype(jnp.bfloat16)
    )
    value_linear_gradient = value_gradients.reshape(
        resident_rows, KEY_VALUE_HEADS * HEAD_SIZE
    ).astype(jnp.bfloat16)
    grad_normed_in = (
        times_transposed(grad_query_lin, back_query) + times_transposed(grad_key_lin, back_key)
    ) * scale_qk + times_transposed(value_linear_gradient, back_value) * scale_in
    _, in_pull = jax.vjp(norm_gain, tokens, gain_attn_in)
    grad_tokens_part, grad_gain_one = in_pull(grad_normed_in)
    grad_input = grad_middle + grad_tokens_part
    attn_shares = reduce_terms(
        (
            cross_rows(normed_in, grad_query_lin),
            cross_rows(normed_in, grad_key_lin),
            cross_rows(normed_in, value_linear_gradient),
            cross_rows(grad_proj_low, attended),
            grad_gain_one,
            grad_gain_two,
            grad_gain_three,
            grad_gain_four,
        )
    )
    return (
        block_out[None],
        grad_input[None],
        attn_shares[4],
        attn_shares[5],
        attn_shares[6],
        attn_shares[7],
        attn_shares[0],
        attn_shares[1],
        attn_shares[2],
        attn_shares[3],
        jnp.concatenate(gate_shares, axis=1),
        jnp.concatenate(up_shares, axis=1),
        jnp.concatenate(down_shares, axis=1),
    )


VMEM_BYTES = 56 * 1024 * 1024
TILE_VMEM_BYTES = 18 * 1024 * 1024
CROSS_VMEM_BYTES = 38 * 1024 * 1024
GELU_RATE = 0.7978845608028654
TILE = 256
CHUNK = 768


def seq_swap(block, bit):
    return lax.ppermute(block, "seq", [(place, place ^ bit) for place in range(8)])


def row_swap(block, bit):
    return lax.ppermute(block, "row", [(place, place ^ bit) for place in range(4)])


def row_shift(block, step):
    return lax.ppermute(
        block, "row", [(place, place + step) for place in range(4) if 0 <= place + step < 4]
    )


def join_kernel(place_ref, own, *refs):
    below, above, (out_ref, sems) = refs[:3], refs[3:6], refs[6:]

    def join(place):
        copies = [
            pltpu.make_async_copy(
                own if q == place else below[place - q - 1] if q < place else above[q - place - 1],
                out_ref.at[:, q],
                sems.at[q],
            )
            for q in range(4)
        ]
        for copy in copies:
            copy.start()
        for copy in copies:
            copy.wait()

    for place in range(4):
        pl.when(place_ref[0] == place)(functools.partial(join, place))


def ordered_quarters(own, below, above):
    _, rows, columns = own.shape
    joined = pl.pallas_call(
        join_kernel,
        in_specs=[pl.BlockSpec(memory_space=pltpu.SMEM)] + [pl.BlockSpec(memory_space=pl.ANY)] * 7,
        out_specs=pl.BlockSpec(memory_space=pltpu.VMEM),
        out_shape=jax.ShapeDtypeStruct((8, 4, rows, columns), own.dtype),
        scratch_shapes=[pltpu.SemaphoreType.DMA((4,))],
        compiler_params=pltpu.CompilerParams(vmem_limit_bytes=TILE_VMEM_BYTES),
        cost_estimate=pl.CostEstimate(flops=1, bytes_accessed=1, transcendentals=0),
    )(jnp.full((1,), lax.axis_index("row"), jnp.int32), own, *below, *above)
    return joined.reshape(32 * rows, columns)


def bf(values):
    return values.astype(jnp.bfloat16)


def wide(values):
    return values.astype(jnp.float32)


RELATIVE = (0, 2, 4, 6, 1, 3, 5, 7)


def pin(*values):
    return lax.optimization_barrier(values)


def gather_near(block):
    return block, seq_swap(block, 2), seq_swap(block, 4)


def gather_far(block, from_x, from_y):
    half = block.shape[0] // 2
    far_first = seq_swap(from_y[:half], 2)
    far_last = seq_swap(from_x[half:], 4)
    return jnp.concatenate([block, from_x, from_y, far_first, far_last])


def gather_row(block):
    mine = gather_far(*gather_near(block))
    return mine, seq_swap(mine, 1)


def other_core(rows):
    middle = rows.shape[0] // 2
    theirs = seq_swap(rows, 1)
    return jnp.concatenate([theirs[middle:], theirs[:middle]])


def scatter_core(partial_half):
    theirs = seq_swap(partial_half(1, jnp.bfloat16), 1)
    return scatter_parts(partial_half(0, jnp.float32) + wide(theirs))


def scatter_parts(mine):
    unit = mine.shape[0] // 4
    half = unit // 2
    here, by_x, by_y, far = (mine[i * unit : (i + 1) * unit] for i in range(4))
    to_x = bf(jnp.concatenate([by_x[:half], far[:half]]))
    to_y = bf(jnp.concatenate([by_y[half:], far[half:]]))
    return here, by_x[half:], by_y[:half], to_x, to_y


def scatter_near(here, by_x, by_y, to_x, to_y):
    return here, by_x, by_y, seq_swap(to_x, 2), seq_swap(to_y, 4)


def scatter_far(here, by_x, by_y, from_x, from_y):
    half = here.shape[0] // 2
    last_y = seq_swap(bf(by_y + wide(from_x[half:])), 4)
    last_x = seq_swap(bf(by_x + wide(from_y[half:])), 2)
    return jnp.concatenate(
        [
            here[:half] + wide(from_x[:half]) + wide(last_y),
            here[half:] + wide(from_y[:half]) + wide(last_x),
        ]
    )


def scatter_row(partial_half):
    return scatter_far(*scatter_near(*scatter_core(partial_half)))


def pack_kernel(decoders, place_ref, *refs):
    codes, outs = refs[: len(decoders)], refs[len(decoders) :]
    rows = [bf(wide(decode(code_ref[...]))) for decode, code_ref in zip(decoders, codes)]
    if len(outs) == 1:
        column = 0
        for part in rows:
            outs[0][0, :, column : column + part.shape[1]] = part
            column += part.shape[1]
    else:
        column = 0
        for out_ref in outs:
            out_ref[0] = rows[0][:, column : column + out_ref.shape[2]]
            column += out_ref.shape[2]


def exact_eight(codes):
    return codes


def exact_four(codes):
    return (codes & -16) + 8


def exact_two(codes):
    return (codes & -64) + 32


def pack_codes(code_arrays, decoders, parts, part, widths=None):
    rows = code_arrays[0].shape[0] // parts
    columns = [codes.shape[1] // 8 for codes in code_arrays]
    widths = widths or [sum(columns)]
    found = pl.pallas_call(
        functools.partial(pack_kernel, decoders),
        grid_spec=pltpu.PrefetchScalarGridSpec(
            num_scalar_prefetch=1,
            grid=(8,),
            in_specs=[pl.BlockSpec((rows, c), lambda j, p: (p[0], j)) for c in columns],
            out_specs=[pl.BlockSpec((1, rows, w), lambda j, p: (j, 0, 0)) for w in widths],
        ),
        out_shape=[jax.ShapeDtypeStruct((8, rows, w), jnp.bfloat16) for w in widths],
        compiler_params=pltpu.CompilerParams(vmem_limit_bytes=VMEM_BYTES),
        cost_estimate=pl.CostEstimate(
            flops=0, bytes_accessed=rows * sum(columns) * 48, transcendentals=0
        ),
    )(jnp.full((1,), part, jnp.int32), *code_arrays)
    return found if len(widths) > 1 else found[0]


def unpack_kernel(block_ref, *out_refs):
    rows = block_ref.shape[2]
    column = 0
    for out_ref in out_refs:
        end = column + out_ref.shape[1]
        for part in range(block_ref.shape[0]):
            out_ref[part * rows : (part + 1) * rows, :] = wide(block_ref[part, 0, :, column:end])
        column = end


def unpack_blocks(blocks, widths):
    parts, _, rows, columns = blocks.shape
    return pl.pallas_call(
        unpack_kernel,
        grid=(8,),
        in_specs=[pl.BlockSpec((parts, 1, rows, columns), lambda j: (0, j, 0, 0))],
        out_specs=[pl.BlockSpec((parts * rows, w), lambda j: (0, j)) for w in widths],
        out_shape=[jax.ShapeDtypeStruct((parts * rows, 8 * w), jnp.float32) for w in widths],
        compiler_params=pltpu.CompilerParams(vmem_limit_bytes=VMEM_BYTES),
        cost_estimate=pl.CostEstimate(flops=0, bytes_accessed=6 * blocks.size, transcendentals=0),
    )(blocks)


def trade(blocks):
    return lax.all_to_all(blocks, "seq", 0, 0, tiled=True)


def dot(left, right):
    return jnp.dot(left, right, preferred_element_type=jnp.float32)


def turn(values, cosine, sine):
    half = values.shape[-1] // 2
    first, last = values[..., :half], values[..., half:]
    return jnp.concatenate([first * cosine - last * sine, last * cosine + first * sine], axis=-1)


def norm_back(values, gain, upstream):
    scale = rms_scale(values)
    lifted = upstream * gain
    shared = jnp.mean(lifted * values, axis=-1, keepdims=True)
    gradient = scale * lifted - values * (scale * scale * scale) * shared
    return gradient, jnp.sum(upstream * values * scale, axis=0)


def gelu_parts(values):
    inner = GELU_RATE * (values + 0.044715 * values * values * values)
    bent = jnp.tanh(inner)
    slope = 0.5 * (1.0 + bent) + 0.5 * values * (1.0 - bent * bent) * GELU_RATE * (
        1.0 + 3.0 * 0.044715 * values * values
    )
    return 0.5 * values * (1.0 + bent), slope


def whole_spec(weight):
    return pl.BlockSpec(memory_space=pltpu.VMEM)


def tile_calls(kernel, grid, in_specs, arrays, out_specs, out_shape, scratch=()):
    return pl.pallas_call(
        kernel,
        grid=grid,
        in_specs=in_specs,
        out_specs=out_specs,
        out_shape=out_shape,
        scratch_shapes=scratch,
        compiler_params=pltpu.CompilerParams(vmem_limit_bytes=TILE_VMEM_BYTES),
        cost_estimate=pl.CostEstimate(flops=1, bytes_accessed=1, transcendentals=0),
    )(*arrays)


def source_specs(count, tile, columns, steps):
    specs = [
        pl.BlockSpec((tile, columns), lambda i: (jnp.minimum(i, steps - 1), 0)),
        pl.BlockSpec((tile, columns), lambda i: (jnp.maximum(i - steps, 0), 0)),
    ]
    return specs[:count]


def on_source(steps, sources, action):
    if len(sources) == 1:
        action(sources[0][...])
    else:
        pl.when(pl.program_id(0) < steps)(lambda: action(sources[0][...]))
        pl.when(pl.program_id(0) >= steps)(lambda: action(sources[1][...]))


def up_kernel(steps, scale, *refs):
    *sources, w_gate, w_up, mixed_ref, to_gate_ref, to_up_ref = refs

    def action(rows):
        gate = dot(rows, w_gate[...]) * scale
        up = dot(rows, w_up[...]) * scale
        value, slope = gelu_parts(gate)
        mixed_ref[...] = bf(value * up)
        to_gate_ref[...] = bf(slope * up)
        to_up_ref[...] = bf(value)

    on_source(steps, sources, action)


def up_project(halves, w_gate, w_up, scale):
    rows, columns = halves[0].shape
    hidden = w_gate.shape[1]
    steps = rows // TILE
    return tile_calls(
        functools.partial(up_kernel, steps, scale),
        (len(halves) * steps,),
        source_specs(len(halves), TILE, columns, steps) + [whole_spec(w_gate), whole_spec(w_up)],
        (*halves, w_gate, w_up),
        [pl.BlockSpec((TILE, hidden), lambda i: (i, 0))] * 3,
        [jax.ShapeDtypeStruct((len(halves) * rows, hidden), jnp.bfloat16)] * 3,
    )


def back_kernel(steps, scale, *refs):
    *sources, w_down, to_gate_ref, to_up_ref, gate_ref, up_ref = refs

    def action(rows):
        grad_mixed = dot(rows, w_down[...]) * scale
        gate_ref[...] = bf(grad_mixed * wide(to_gate_ref[...]))
        up_ref[...] = bf(grad_mixed * wide(to_up_ref[...]))

    on_source(steps, sources, action)


def back_project(halves, w_down, factors, scale):
    rows, columns = halves[0].shape
    hidden = w_down.shape[1]
    steps = rows // TILE
    part = pl.BlockSpec((TILE, hidden), lambda i: (i, 0))
    return tile_calls(
        functools.partial(back_kernel, steps, scale),
        (len(halves) * steps,),
        source_specs(len(halves), TILE, columns, steps) + [whole_spec(w_down), part, part],
        (*halves, w_down, *factors),
        [part] * 2,
        [jax.ShapeDtypeStruct((len(halves) * rows, hidden), jnp.bfloat16)] * 2,
    )


def cross_kernel(steps, n_left, n_right, *refs):
    lefts, rights = refs[:n_left], refs[n_left : n_left + n_right]
    out_ref, left_buf, right_buf, total, sems = refs[n_left + n_right :]

    def copies(step):
        slot = step % 2
        found = []
        at = 0
        for left, left_row, right, right_row, count in steps[step]:
            found.append(
                pltpu.make_async_copy(
                    lefts[left].at[pl.ds(left_row, count)],
                    left_buf.at[slot, pl.ds(at, count)],
                    sems.at[slot, len(found)],
                )
            )
            found.append(
                pltpu.make_async_copy(
                    rights[right].at[pl.ds(right_row, count)],
                    right_buf.at[slot, pl.ds(at, count)],
                    sems.at[slot, len(found)],
                )
            )
            at += count
        return found

    for copy in copies(0):
        copy.start()
    chunk = out_ref.shape[2]
    for step in range(len(steps)):
        slot = step % 2
        if step + 1 < len(steps):
            for copy in copies(step + 1):
                copy.start()
        for copy in copies(step):
            copy.wait()

        @pl.loop(0, total.shape[0] // CHUNK)
        def _(m):
            columns = pl.ds(pl.multiple_of(m * CHUNK, CHUNK), CHUNK)
            term = cross_rows(left_buf[slot, :, columns], right_buf[slot])
            if step > 0:
                term = term + total[columns, :]
            total[columns, :] = term

    for place in range(8):
        for part in range(out_ref.shape[0]):
            start = (place * out_ref.shape[0] + part) * chunk
            out_ref[part, place] = bf(total[start : start + chunk, :])


def cross_products(lefts, rights, steps, parts=1):
    wide_rows, columns = lefts[0].shape[1], rights[0].shape[1]
    depth = max(sum(piece[4] for piece in step) for step in steps)
    pieces = max(2 * len(step) for step in steps)
    return pl.pallas_call(
        functools.partial(cross_kernel, steps, len(lefts), len(rights)),
        in_specs=[pl.BlockSpec(memory_space=pl.ANY)] * (len(lefts) + len(rights)),
        out_shape=jax.ShapeDtypeStruct((parts, 8, wide_rows // 8 // parts, columns), jnp.bfloat16),
        scratch_shapes=[
            pltpu.VMEM((2, depth, wide_rows), jnp.bfloat16),
            pltpu.VMEM((2, depth, columns), jnp.bfloat16),
            pltpu.VMEM((wide_rows, columns), jnp.float32),
            pltpu.SemaphoreType.DMA((2, pieces)),
        ],
        compiler_params=pltpu.CompilerParams(vmem_limit_bytes=CROSS_VMEM_BYTES),
        cost_estimate=pl.CostEstimate(flops=1, bytes_accessed=1, transcendentals=0),
    )(*lefts, *rights)


def partial_kernel(*refs):
    out_ref, pairs = refs[-1], refs[:-1]
    total = times_transposed(pairs[0][...], pairs[1][...])
    for left, right in zip(pairs[2::2], pairs[3::2]):
        total = total + times_transposed(left[...], right[...])
    out_ref[...] = total.astype(out_ref.dtype)


def partial_product(pairs, side, kind):
    rows, hidden = pairs[0][0].shape
    columns = pairs[0][1].shape[0]
    half = rows // 2
    steps = half // TILE
    left_spec = pl.BlockSpec((TILE, hidden), lambda i: (side * steps + i, 0))
    return tile_calls(
        partial_kernel,
        (steps,),
        [spec for pair in pairs for spec in (left_spec, whole_spec(pair[1]))],
        [array for pair in pairs for array in pair],
        pl.BlockSpec((TILE, columns), lambda i: (i, 0)),
        jax.ShapeDtypeStruct((half, columns), kind),
    )


def plane_body(
    hidden_in,
    cotangent,
    doc_lengths,
    gain_attn_in,
    gain_attn_out,
    gain_ffw_in,
    gain_ffw_out,
    query_codes,
    key_integer_codes,
    value_integer_codes,
    out_codes,
    gate_codes,
    up_codes,
    down_codes,
):
    lengths = doc_lengths[0]
    block_rows, width = hidden_in.shape[1:]
    row_length = block_rows * 8
    place = lax.axis_index("seq")
    core = place % 2
    head = HEAD_SIZE
    half = head // 2
    scale_qk = key_unit * MODEL_WIDTH ** (-0.5)
    scale_in = code_unit * MODEL_WIDTH ** (-0.5)
    scale_out = code_unit * (QUERY_HEADS * HEAD_SIZE) ** (-0.5)
    scale_down = code_unit * FF ** (-0.5)
    head_scale = HEAD_SIZE ** (-0.5)

    row_place = lax.axis_index("row")
    model_rows = query_codes.shape[0]
    hidden_part = gate_codes.shape[1] // 8

    def both_ways(below, above):
        return row_shift(below, 1), row_shift(above, -1)

    near_tokens = gather_near(hidden_in[0])
    down_blocks = pack_codes([down_codes], [exact_two], 4, row_place)
    near_tokens, down_blocks = pin(near_tokens, down_blocks)
    own_down = trade(down_blocks)
    attn_blocks = pack_codes(
        [query_codes, key_integer_codes, value_integer_codes, out_codes], [exact_eight] * 4, 1, 0
    )
    attn_blocks, own_down = pin(attn_blocks, own_down)
    attn_weights, gate_blocks, up_blocks, down_one = pin(
        trade(attn_blocks).reshape(width, 3 * head),
        pack_codes([gate_codes], [exact_four], 1, 0),
        pack_codes([up_codes], [exact_four], 1, 0),
        both_ways(own_down, own_down),
    )
    gate_rows = trade(gate_blocks)
    w_attn_in = attn_weights[:, : 2 * head]
    w_out = attn_weights[:, 2 * head :]

    token_blocks = [(place ^ k) * block_rows + jnp.arange(block_rows) for k in RELATIVE]
    token_index = jnp.concatenate(token_blocks).astype(jnp.int32)
    ends = jnp.cumsum(lengths)
    past = token_index[:, None] >= ends[None, :]
    doc_start = jnp.max(jnp.where(past, ends[None, :], 0), axis=1)
    cosine, sine = rotary_tables(token_index - doc_start, head)
    visible = (token_index[None, :] <= token_index[:, None]) & (
        token_index[None, :] >= doc_start[:, None]
    )

    tokens = wide(hidden_in[0])
    upstream = wide(cotangent[0])
    tokens_mine = gather_far(*near_tokens)
    row_tokens = jnp.concatenate([tokens_mine, seq_swap(tokens_mine, 1)])
    normed_in = bf(norm_gain(wide(row_tokens), gain_attn_in))
    linear = dot(normed_in, w_attn_in)
    query = bf(turn(linear[:, :head] * scale_qk, cosine, sine))
    key_half = linear[:, head : head + half] * scale_qk
    value_half = bf(linear[:, head + half :] * scale_in)
    key_other = other_core(key_half)
    value_other = other_core(value_half)

    def pair(own, other):
        return jnp.where(
            core == 0,
            jnp.concatenate([own, other], axis=-1),
            jnp.concatenate([other, own], axis=-1),
        )

    key = bf(turn(pair(key_half, key_other), cosine, sine))
    value = pair(value_half, value_other)
    bend = jnp.tanh(times_transposed(query, key) * (head_scale / SOFTCAP))
    weights = jnp.where(visible, jnp.exp(SOFTCAP * bend), 0.0)
    totals = jnp.sum(weights, axis=-1, keepdims=True)
    attended_wide = dot(bf(weights), value) / totals
    attended = bf(attended_wide)
    attended, gate_rows, down_two = pin(attended, gate_rows, both_ways(*down_one))
    near_half = row_length // 2
    attn_core = scatter_core(
        lambda side, kind: times_transposed(
            attended[side * near_half :][:near_half], w_out
        ).astype(kind)
    )
    (attn_core,) = pin(attn_core)
    attn_near, down_three = pin(scatter_near(*attn_core), both_ways(*down_two))
    attn_proj, up_blocks = pin(scale_out * scatter_far(*attn_near), up_blocks)
    up_rows = trade(up_blocks)
    middle = tokens + norm_gain(attn_proj, gain_attn_out)
    normed_mid = bf(norm_gain(middle, gain_ffw_in))

    mid_near, up_rows, mid_two, mid_three = pin(
        gather_near(normed_mid), up_rows, row_swap(normed_mid, 2), row_swap(normed_mid, 3)
    )
    mid_mine = gather_far(*mid_near)
    mid_mine, mid_theirs, w_down = pin(
        mid_mine,
        seq_swap(mid_mine, 1),
        ordered_quarters(own_down, *zip(down_one, down_two, down_three)),
    )
    w_gate, w_up = gate_rows.reshape(width, hidden_part), up_rows.reshape(width, hidden_part)

    def up_again(*halves):
        return up_project(halves, w_gate, w_up, scale_in)

    def back_again(halves, factors):
        return back_project(halves, w_down, factors, scale_down)

    def cut(rows):
        return [rows[i * block_rows : (i + 1) * block_rows] for i in range(4)]

    (mixed, *factors), pair_mid_near, mid_cuts = pin(
        up_again(mid_mine, mid_theirs),
        gather_near(jnp.concatenate([mid_two, mid_three])),
        cut(mid_mine),
    )
    ffn_core, pair_mid_mine, third_mid_first = pin(
        scatter_core(lambda side, kind: partial_product([(mixed, w_down)], side, kind)),
        gather_far(*pair_mid_near),
        [row_swap(rows, 1) for rows in mid_cuts[:2]],
    )
    ffn_near, pair_mid_theirs, third_mid_second = pin(
        scatter_near(*ffn_core), seq_swap(pair_mid_mine, 1), row_swap(mid_cuts[2], 1)
    )
    ffn_proj, third_mid_last, pair_mid_mine = pin(
        scale_down * scatter_far(*ffn_near), row_swap(mid_cuts[3], 1), pair_mid_mine
    )
    third_mid_mine = jnp.concatenate([*third_mid_first, third_mid_second, third_mid_last])
    block_out = bf(middle + norm_gain(ffn_proj, gain_ffw_out))
    grad_ffn, grad_gain_four = norm_back(ffn_proj, gain_ffw_out, upstream)
    grad_ffn_low = bf(grad_ffn)
    grad_near, grad_two, (mine_mixed, *mine_factors) = pin(
        gather_near(grad_ffn_low), row_swap(grad_ffn_low, 2), up_again(pair_mid_mine)
    )
    grad_mine = gather_far(*grad_near)
    grad_mine, grad_theirs, grad_three, third_mid_theirs, (theirs_mixed, *theirs_factors) = pin(
        grad_mine,
        seq_swap(grad_mine, 1),
        row_swap(grad_ffn_low, 3),
        seq_swap(third_mid_mine, 1),
        up_again(pair_mid_theirs),
    )
    grad_cuts = cut(grad_mine)
    grads_hidden, pair_grad_near, third_grad_first = pin(
        back_again((grad_mine, grad_theirs), factors),
        gather_near(jnp.concatenate([grad_two, grad_three])),
        [row_swap(rows, 1) for rows in grad_cuts[:2]],
    )
    pairs = list(zip(grads_hidden, (w_gate, w_up)))
    mid_core, pair_grad_mine, third_grad_last = pin(
        scatter_core(lambda side, kind: partial_product(pairs, side, kind)),
        gather_far(*pair_grad_near),
        [row_swap(rows, 1) for rows in grad_cuts[2:]],
    )
    third_grad_mine = jnp.concatenate([*third_grad_first, *third_grad_last])
    sum_near, pair_grad_theirs, third_grad_theirs, (third_mixed, *third_factors), mine_hidden = pin(
        scatter_near(*mid_core),
        seq_swap(pair_grad_mine, 1),
        seq_swap(third_grad_mine, 1),
        up_again(third_mid_mine, third_mid_theirs),
        back_again((pair_grad_mine,), mine_factors),
    )
    grad_mid, theirs_hidden = pin(
        scale_in * scatter_far(*sum_near), back_again((pair_grad_theirs,), theirs_factors)
    )
    grad_middle_part, grad_gain_three = norm_back(middle, gain_ffw_in, grad_mid)
    grad_middle = upstream + grad_middle_part
    grad_proj, grad_gain_two = norm_back(attn_proj, gain_attn_out, grad_middle)

    row_half = row_length // 2
    mids = (mid_mine, mid_theirs, pair_mid_mine, pair_mid_theirs, third_mid_mine, third_mid_theirs)
    outs = (
        grad_mine,
        grad_theirs,
        pair_grad_mine,
        pair_grad_theirs,
        third_grad_mine,
        third_grad_theirs,
    )
    steps = (
        ((0, 0, 0, 0, row_half), (1, 0, 0, row_half, row_half)),
        ((2, 0, 1, 0, row_length),),
        ((3, 0, 2, 0, row_length),),
        ((4, 0, 3, 0, row_half), (5, 0, 3, row_half, row_half)),
    )
    proj_near, down_blocks, third_grads = pin(
        gather_near(bf(grad_proj)),
        cross_products(outs, (mixed, mine_mixed, theirs_mixed, third_mixed), steps),
        (third_grad_mine, third_grad_theirs),
    )
    proj_mine, down_blocks = pin(gather_far(*proj_near), down_blocks)
    down_blocks = trade(down_blocks[0])
    row_proj = jnp.concatenate([proj_mine, seq_swap(proj_mine, 1)])

    def halve(terms, bit, axis, side):
        kept = lax.dynamic_index_in_dim(terms, side, axis, keepdims=False)
        sent = lax.dynamic_index_in_dim(terms, 1 - side, axis, keepdims=False)
        return bf(wide(kept) + wide(row_swap(sent, bit)))

    def quarters_of(part):
        return bf(part).reshape(8, 2, 2, model_rows // 4, part.shape[1])

    low_bit, high_bit = row_place % 2, row_place // 2

    grad_attended = bf(dot(row_proj, w_out) * scale_out)
    delta = jnp.sum(wide(grad_attended) * attended_wide, axis=-1, keepdims=True)
    probs = weights / totals
    grad_probs = times_transposed(grad_attended, value)
    grad_raw = bf(probs * (grad_probs - delta) * (1.0 - bend * bend))
    grad_query = bf(turn(dot(grad_raw, key) * head_scale, cosine, -sine))
    key_part = cross_rows(grad_raw, query) * head_scale
    value_part = cross_rows(bf(probs), grad_attended)

    def own_half(values, side):
        return lax.dynamic_slice_in_dim(values, side * half, half, axis=1)

    key_sum = key_part + other_core(key_part)
    grad_key = bf(own_half(turn(key_sum, cosine, -sine), core))
    grad_value = bf(own_half(value_part, core) + other_core(own_half(value_part, 1 - core)))
    grad_linear = jnp.concatenate([grad_query, grad_key, grad_value], axis=1)
    grad_linear, out_sum, third_grads = pin(
        grad_linear,
        halve(quarters_of(cross_rows(row_proj, attended)), 1, 2, low_bit),
        third_grads,
    )

    def grad_in_half(side, kind):
        rows = grad_linear[side * near_half :][:near_half]
        total = scale_qk * times_transposed(
            rows[:, : head + half], w_attn_in[:, : head + half]
        ) + scale_in * times_transposed(rows[:, head + half :], w_attn_in[:, head + half :])
        return total.astype(kind)

    in_core, in_terms, out_sum, third_grads = pin(
        scatter_core(grad_in_half),
        quarters_of(cross_rows(normed_in, grad_linear)),
        halve(out_sum, 2, 1, high_bit),
        third_grads,
    )
    third_hidden = back_again(third_grads, third_factors)
    gate_terms, up_terms = zip(grads_hidden, mine_hidden, theirs_hidden, third_hidden)
    in_near, in_sum, gate_blocks, up_terms, down_blocks = pin(
        scatter_near(*in_core),
        halve(in_terms, 1, 2, low_bit),
        cross_products(mids, gate_terms, steps),
        up_terms,
        down_blocks,
    )
    gate_blocks = trade(gate_blocks[0])
    in_sum, grad_in, up_blocks, gate_blocks = pin(
        halve(in_sum, 2, 1, high_bit),
        scatter_far(*in_near),
        cross_products(mids, up_terms, steps),
        gate_blocks,
    )
    grad_tokens, grad_gain_one = norm_back(tokens, gain_attn_in, grad_in)
    grad_input = grad_middle + grad_tokens
    gain_terms = jnp.stack([grad_gain_one, grad_gain_two, grad_gain_three, grad_gain_four])
    gain_blocks = trade(gain_terms.reshape(4, 8, model_rows).transpose(1, 0, 2))
    sums, gain_blocks, up_blocks = pin(
        trade(jnp.concatenate([in_sum, out_sum], axis=2)), gain_blocks, up_blocks
    )
    up_blocks = trade(up_blocks[0])

    def double(blocks, bit, side):
        both_sides = jnp.stack([blocks, row_swap(blocks, bit)])
        return jnp.where(side == 0, both_sides, both_sides[::-1])

    gains = jnp.sum(gain_blocks, axis=0)
    gains = gains + row_swap(gains, 1)
    blocks, gains = pin(double(sums, 2, high_bit), gains + row_swap(gains, 2))
    blocks = double(blocks, 1, low_bit).transpose(1, 0, 2, 3, 4)
    grad_w_gate, grad_w_up, grad_w_down = (
        unpack_blocks(blocks, [hidden_part])[0]
        for blocks in (gate_blocks[None], up_blocks[None], down_blocks[None])
    )
    blocks, grad_w_up = pin(blocks, grad_w_up)
    attn_grads = unpack_blocks(blocks.reshape(4, *sums.shape), [head, half, half, head])

    return (
        block_out[None],
        grad_input[None],
        gains[0],
        gains[1],
        gains[2],
        gains[3],
        attn_grads[0],
        attn_grads[1],
        attn_grads[2],
        attn_grads[3],
        grad_w_gate,
        grad_w_up,
        grad_w_down,
    )


def solution(mesh):
    body = plane_body if dict(mesh.shape) == {"seq": 8, "row": 4} else token_body
    return jax.shard_map(
        body,
        mesh=mesh,
        in_specs=(
            P("row", "seq", None),
            P("row", "seq", None),
            P("row", None),
            P(),
            P(),
            P(),
            P(),
            P("seq", None),
            P("seq", None),
            P("seq", None),
            P("seq", None),
            P("seq", None),
            P("seq", None),
            P("seq", None),
        ),
        out_specs=(
            P("row", "seq", None),
            P("row", "seq", None),
            P("seq"),
            P("seq"),
            P("seq"),
            P("seq"),
            P("seq", None),
            P("seq", None),
            P("seq", None),
            P("seq", None),
            P("seq", None),
            P("seq", None),
            P("seq", None),
        ),
        check_vma=False,
    )
```

```python
import functools

import jax
import jax.numpy as jnp
from jax import lax
from jax.experimental import pallas as pl
from jax.experimental.pallas import tpu as pltpu
from jax.sharding import PartitionSpec as P

MODEL_WIDTH = 2304
QUERY_HEADS = 8
KEY_VALUE_HEADS = 4
HEAD_SIZE = 256
FF = 9216
SOFTCAP = 15


epsilon = 1e-06
code_unit = 1.0 / 72.0
key_unit = 1.0 / 44.0
large_negative_fill = -1e30


def codes_eight(code_block):
    return code_block.astype(jnp.bfloat16)


def codes_four(code_block):
    return (code_block // 16 * 16 + 8).astype(jnp.bfloat16)


def codes_two(code_block):
    return (code_block // 64 * 64 + 32).astype(jnp.bfloat16)


def rms_scale(values):
    return lax.rsqrt(jnp.mean(values * values, axis=-1, keepdims=True) + epsilon)


def norm_gain(values, gain_vector):
    return values * rms_scale(values) * gain_vector


def geglu(gate_values, up_values):
    return jax.nn.gelu(gate_values, approximate=True) * up_values


def cross_rows(left_side, right_side):
    return lax.dot_general(
        left_side, right_side, (((0,), (0,)), ((), ())), preferred_element_type=jnp.float32
    )


def times_transposed(left_side, right_side):
    return lax.dot_general(
        left_side, right_side, (((1,), (1,)), ((), ())), preferred_element_type=jnp.float32
    )


def doc_layout(lengths, first_index, row_count):
    doc_ends = jnp.cumsum(lengths)
    starts = doc_ends - lengths
    token_index = first_index + jnp.arange(row_count, dtype=jnp.int32)
    doc_number = jnp.sum((token_index[:, None] >= doc_ends[None, :]).astype(jnp.int32), axis=1)
    picked = doc_number[:, None] == jnp.arange(lengths.shape[0], dtype=jnp.int32)[None, :]
    doc_start = jnp.sum(jnp.where(picked, starts[None, :], 0), axis=1)
    return (token_index, doc_start)


def rotary_tables(positions, head_size):
    half_size = head_size // 2
    frequencies = 10000.0 ** (-(2.0 * jnp.arange(half_size, dtype=jnp.float32)) / head_size)
    angles = positions.astype(jnp.float32)[:, None] * frequencies[None, :]
    return (jnp.cos(angles), jnp.sin(angles))


def apply_rotary(values, cosine_table, sine_table):
    half_size = values.shape[-1] // 2
    first_half = values[..., :half_size]
    second_half = values[..., half_size:]
    cos_wide = cosine_table[:, None, :]
    sin_wide = sine_table[:, None, :]
    return jnp.concatenate(
        [
            first_half * cos_wide - second_half * sin_wide,
            second_half * cos_wide + first_half * sin_wide,
        ],
        axis=-1,
    )


def inverse_rotary(value_gradients, cosine_table, sine_table):
    half_size = value_gradients.shape[-1] // 2
    first_half = value_gradients[..., :half_size]
    second_half = value_gradients[..., half_size:]
    cos_wide = cosine_table[:, None, :]
    sin_wide = sine_table[:, None, :]
    return jnp.concatenate(
        [
            first_half * cos_wide + second_half * sin_wide,
            second_half * cos_wide - first_half * sin_wide,
        ],
        axis=-1,
    )


def score_grads(
    heads_of_queries,
    head_gradients,
    log_totals,
    deltas,
    query_index,
    query_start,
    heads_of_keys,
    heads_of_values,
    key_index,
):
    head_scale = HEAD_SIZE ** (-0.5)
    raw_scores = (
        jnp.einsum(
            "tkgd,rkd->kgtr", heads_of_queries, heads_of_keys, preferred_element_type=jnp.float32
        )
        * head_scale
    )
    capped = SOFTCAP * jnp.tanh(raw_scores / SOFTCAP)
    visible = (key_index[None, :] <= query_index[:, None]) & (
        key_index[None, :] >= query_start[:, None]
    )
    probs = jnp.where(visible, jnp.exp(capped - log_totals[..., None]), 0.0)
    grad_probs = jnp.einsum(
        "tkgd,rkd->kgtr", head_gradients, heads_of_values, preferred_element_type=jnp.float32
    )
    grad_capped = probs * (grad_probs - deltas[..., None])
    grad_raw = (grad_capped * (1.0 - (capped / SOFTCAP) ** 2)).astype(jnp.bfloat16)
    return (grad_raw, probs.astype(jnp.bfloat16))


def reduce_terms(grad_terms):
    shares = lax.psum_scatter(grad_terms, "seq", scatter_dimension=0, tiled=True)
    return lax.psum(shares, "row")


def token_body(
    hidden_in,
    cotangent,
    doc_lengths,
    gain_attn_in,
    gain_attn_out,
    gain_ffw_in,
    gain_ffw_out,
    query_codes,
    key_integer_codes,
    value_integer_codes,
    out_codes,
    gate_codes,
    up_codes,
    down_codes,
):
    tokens = hidden_in[0].astype(jnp.float32)
    upstream = cotangent[0].astype(jnp.float32)
    lengths = doc_lengths[0]
    resident_rows = tokens.shape[0]
    heads_per_group = QUERY_HEADS // KEY_VALUE_HEADS
    head_scale = HEAD_SIZE ** (-0.5)
    scale_qk = key_unit * MODEL_WIDTH ** (-0.5)
    scale_in = code_unit * MODEL_WIDTH ** (-0.5)
    scale_out = code_unit * (QUERY_HEADS * HEAD_SIZE) ** (-0.5)
    scale_down = code_unit * FF ** (-0.5)
    part_count = 8
    part_width = gate_codes.shape[1] // part_count
    first_row = lax.axis_index("seq") * resident_rows
    local_index, local_start = doc_layout(lengths, first_row, resident_rows)
    cosine_table, sine_table = rotary_tables(local_index - local_start, HEAD_SIZE)

    def attention_weights():
        return (
            lax.all_gather(codes_eight(query_codes), "seq", axis=0, tiled=True),
            lax.all_gather(codes_eight(key_integer_codes), "seq", axis=0, tiled=True),
            lax.all_gather(codes_eight(value_integer_codes), "seq", axis=0, tiled=True),
            lax.all_gather(codes_eight(out_codes), "seq", axis=0, tiled=True),
        )

    def ffn_weights(part_number):
        column_start = part_number * part_width
        column_end = column_start + part_width
        return (
            lax.all_gather(
                codes_four(gate_codes[:, column_start:column_end]), "seq", axis=0, tiled=True
            ),
            lax.all_gather(
                codes_four(up_codes[:, column_start:column_end]), "seq", axis=0, tiled=True
            ),
            lax.all_gather(
                codes_two(down_codes[:, column_start:column_end]), "seq", axis=0, tiled=True
            ),
        )

    attn_set = attention_weights()
    w_query, w_key, w_value, w_out = attn_set
    normed_in = norm_gain(tokens, gain_attn_in).astype(jnp.bfloat16)
    query_lin = jnp.dot(normed_in, w_query, preferred_element_type=jnp.float32) * scale_qk
    key_linear = jnp.dot(normed_in, w_key, preferred_element_type=jnp.float32) * scale_qk
    value_linear = jnp.dot(normed_in, w_value, preferred_element_type=jnp.float32) * scale_in
    rows_of_queries = (
        apply_rotary(
            query_lin.reshape(resident_rows, QUERY_HEADS, HEAD_SIZE), cosine_table, sine_table
        )
        .astype(jnp.bfloat16)
        .reshape(resident_rows, QUERY_HEADS * HEAD_SIZE)
    )
    rows_of_keys = (
        apply_rotary(
            key_linear.reshape(resident_rows, KEY_VALUE_HEADS, HEAD_SIZE), cosine_table, sine_table
        )
        .astype(jnp.bfloat16)
        .reshape(resident_rows, KEY_VALUE_HEADS * HEAD_SIZE)
    )
    rows_of_values = value_linear.astype(jnp.bfloat16)
    heads_of_queries = rows_of_queries.reshape(
        resident_rows, KEY_VALUE_HEADS, heads_per_group, HEAD_SIZE
    )
    running_maximum = jnp.full(
        (KEY_VALUE_HEADS, heads_per_group, resident_rows), large_negative_fill, jnp.float32
    )
    block_of_keys = lax.all_gather(rows_of_keys, "seq", axis=0, tiled=True)
    block_of_values = lax.all_gather(rows_of_values, "seq", axis=0, tiled=True)
    rows_per_block = block_of_keys.shape[0]
    heads_of_keys = block_of_keys.reshape(rows_per_block, KEY_VALUE_HEADS, HEAD_SIZE)
    heads_of_values = block_of_values.reshape(rows_per_block, KEY_VALUE_HEADS, HEAD_SIZE)
    key_index = jnp.arange(rows_per_block, dtype=jnp.int32)
    raw_scores = (
        jnp.einsum(
            "tkgd,rkd->kgtr", heads_of_queries, heads_of_keys, preferred_element_type=jnp.float32
        )
        * head_scale
    )
    capped = SOFTCAP * jnp.tanh(raw_scores / SOFTCAP)
    visible = (key_index[None, :] <= local_index[:, None]) & (
        key_index[None, :] >= local_start[:, None]
    )
    masked = jnp.where(visible, capped, large_negative_fill)
    new_max = jnp.maximum(running_maximum, jnp.max(masked, axis=-1))
    weights = jnp.where(visible, jnp.exp(masked - new_max[..., None]), 0.0)
    run_total = jnp.sum(weights, axis=-1)
    weighted = jnp.einsum(
        "kgtr,rkd->kgtd",
        weights.astype(jnp.bfloat16),
        heads_of_values,
        preferred_element_type=jnp.float32,
    )
    weighted, running_maximum, run_total = (weighted, new_max, run_total)
    attn_heads = weighted / run_total[..., None]
    log_totals = running_maximum + jnp.log(run_total)
    attended = (
        attn_heads.transpose(2, 0, 1, 3)
        .reshape(resident_rows, QUERY_HEADS * HEAD_SIZE)
        .astype(jnp.bfloat16)
    )
    attn_proj = times_transposed(attended, w_out) * scale_out
    middle = tokens + norm_gain(attn_proj, gain_attn_out)
    normed_mid = norm_gain(middle, gain_ffw_in).astype(jnp.bfloat16)
    ffn_proj = jnp.zeros((resident_rows, tokens.shape[1]), jnp.float32)
    gate_store = []
    up_store = []
    mixed_store = []
    ffn_sets = []
    for part_number in range(part_count):
        ffn_set = ffn_weights(part_number)
        w_gate, w_up, w_down = ffn_set
        gate_lin = jnp.dot(normed_mid, w_gate, preferred_element_type=jnp.float32) * scale_in
        up_lin = jnp.dot(normed_mid, w_up, preferred_element_type=jnp.float32) * scale_in
        mixed_rows = geglu(gate_lin, up_lin).astype(jnp.bfloat16)
        ffn_proj = ffn_proj + times_transposed(mixed_rows, w_down) * scale_down
        gate_store.append(gate_lin)
        up_store.append(up_lin)
        mixed_store.append(mixed_rows)
        ffn_sets.append(ffn_set)
    block_out = (middle + norm_gain(ffn_proj, gain_ffw_out)).astype(jnp.bfloat16)
    _, post_pull = jax.vjp(norm_gain, ffn_proj, gain_ffw_out)
    grad_ffn_proj, grad_gain_four = post_pull(upstream)
    grad_ffn_low = grad_ffn_proj.astype(jnp.bfloat16)
    grad_normed_mid = jnp.zeros((resident_rows, tokens.shape[1]), jnp.float32)
    gate_shares = []
    up_shares = []
    down_shares = []
    for part_number in range(part_count):
        back_ffn = ffn_weights(part_number)
        w_gate, w_up, w_down = back_ffn
        grad_mixed = jnp.dot(grad_ffn_low, w_down, preferred_element_type=jnp.float32) * scale_down
        _, geglu_pull = jax.vjp(geglu, gate_store[part_number], up_store[part_number])
        grad_gate_lin, grad_up_lin = geglu_pull(grad_mixed)
        grad_gate_low = grad_gate_lin.astype(jnp.bfloat16)
        grad_up_low = grad_up_lin.astype(jnp.bfloat16)
        grad_normed_mid = (
            grad_normed_mid
            + (times_transposed(grad_gate_low, w_gate) + times_transposed(grad_up_low, w_up))
            * scale_in
        )
        gate_share, up_share, down_share = reduce_terms(
            (
                cross_rows(normed_mid, grad_gate_low),
                cross_rows(normed_mid, grad_up_low),
                cross_rows(grad_ffn_low, mixed_store[part_number]),
            )
        )
        gate_shares.append(gate_share)
        up_shares.append(up_share)
        down_shares.append(down_share)
    _, mid_pull = jax.vjp(norm_gain, middle, gain_ffw_in)
    grad_middle_part, grad_gain_three = mid_pull(grad_normed_mid)
    grad_middle = upstream + grad_middle_part
    _, attn_pull = jax.vjp(norm_gain, attn_proj, gain_attn_out)
    grad_attn_proj, grad_gain_two = attn_pull(grad_middle)
    grad_proj_low = grad_attn_proj.astype(jnp.bfloat16)
    back_attn = attention_weights()
    back_query, back_key, back_value, back_out = back_attn
    grad_attended = jnp.dot(grad_proj_low, back_out, preferred_element_type=jnp.float32) * scale_out
    gradient_attention_narrow = grad_attended.astype(jnp.bfloat16)
    head_gradients = gradient_attention_narrow.reshape(
        resident_rows, KEY_VALUE_HEADS, heads_per_group, HEAD_SIZE
    )
    deltas = jnp.sum(
        gradient_attention_narrow.astype(jnp.float32)
        .reshape(resident_rows, KEY_VALUE_HEADS, heads_per_group, HEAD_SIZE)
        .transpose(1, 2, 0, 3)
        * attn_heads,
        axis=-1,
    )
    block_of_keys = lax.all_gather(rows_of_keys, "seq", axis=0, tiled=True)
    block_of_values = lax.all_gather(rows_of_values, "seq", axis=0, tiled=True)
    rows_per_block = block_of_keys.shape[0]
    heads_of_keys = block_of_keys.reshape(rows_per_block, KEY_VALUE_HEADS, HEAD_SIZE)
    heads_of_values = block_of_values.reshape(rows_per_block, KEY_VALUE_HEADS, HEAD_SIZE)
    key_index = jnp.arange(rows_per_block, dtype=jnp.int32)
    grad_raw, probs_low = score_grads(
        heads_of_queries,
        head_gradients,
        log_totals,
        deltas,
        local_index,
        local_start,
        heads_of_keys,
        heads_of_values,
        key_index,
    )
    grad_query_heads = (
        jnp.einsum("kgtr,rkd->tkgd", grad_raw, heads_of_keys, preferred_element_type=jnp.float32)
        * head_scale
    )
    resident_keys = rows_of_keys.reshape(resident_rows, KEY_VALUE_HEADS, HEAD_SIZE)
    resident_values = rows_of_values.reshape(resident_rows, KEY_VALUE_HEADS, HEAD_SIZE)
    block_of_queries = lax.all_gather(
        rows_of_queries.astype(jnp.float32), "seq", axis=0, tiled=True
    )
    block_gradient = lax.all_gather(
        gradient_attention_narrow.astype(jnp.float32), "seq", axis=0, tiled=True
    )
    lse_block = lax.all_gather(log_totals.transpose(2, 0, 1), "seq", axis=0, tiled=True)
    delta_block = lax.all_gather(deltas.transpose(2, 0, 1), "seq", axis=0, tiled=True)
    rows_per_block = block_of_queries.shape[0]
    foreign_queries = block_of_queries.astype(jnp.bfloat16).reshape(
        rows_per_block, KEY_VALUE_HEADS, heads_per_group, HEAD_SIZE
    )
    foreign_gradients = block_gradient.astype(jnp.bfloat16).reshape(
        rows_per_block, KEY_VALUE_HEADS, heads_per_group, HEAD_SIZE
    )
    remote_index, remote_start = doc_layout(lengths, jnp.int32(0), rows_per_block)
    grad_raw, probs_low = score_grads(
        foreign_queries,
        foreign_gradients,
        lse_block.transpose(1, 2, 0),
        delta_block.transpose(1, 2, 0),
        remote_index,
        remote_start,
        resident_keys,
        resident_values,
        local_index,
    )
    key_gradients = (
        jnp.einsum("kgtr,tkgd->rkd", grad_raw, foreign_queries, preferred_element_type=jnp.float32)
        * head_scale
    )
    value_gradients = jnp.einsum(
        "kgtr,tkgd->rkd", probs_low, foreign_gradients, preferred_element_type=jnp.float32
    )
    grad_query_lin = (
        inverse_rotary(
            grad_query_heads.reshape(resident_rows, QUERY_HEADS, HEAD_SIZE),
            cosine_table,
            sine_table,
        )
        .reshape(resident_rows, QUERY_HEADS * HEAD_SIZE)
        .astype(jnp.bfloat16)
    )
    grad_key_lin = (
        inverse_rotary(key_gradients, cosine_table, sine_table)
        .reshape(resident_rows, KEY_VALUE_HEADS * HEAD_SIZE)
        .astype(jnp.bfloat16)
    )
    value_linear_gradient = value_gradients.reshape(
        resident_rows, KEY_VALUE_HEADS * HEAD_SIZE
    ).astype(jnp.bfloat16)
    grad_normed_in = (
        times_transposed(grad_query_lin, back_query) + times_transposed(grad_key_lin, back_key)
    ) * scale_qk + times_transposed(value_linear_gradient, back_value) * scale_in
    _, in_pull = jax.vjp(norm_gain, tokens, gain_attn_in)
    grad_tokens_part, grad_gain_one = in_pull(grad_normed_in)
    grad_input = grad_middle + grad_tokens_part
    attn_shares = reduce_terms(
        (
            cross_rows(normed_in, grad_query_lin),
            cross_rows(normed_in, grad_key_lin),
            cross_rows(normed_in, value_linear_gradient),
            cross_rows(grad_proj_low, attended),
            grad_gain_one,
            grad_gain_two,
            grad_gain_three,
            grad_gain_four,
        )
    )
    return (
        block_out[None],
        grad_input[None],
        attn_shares[4],
        attn_shares[5],
        attn_shares[6],
        attn_shares[7],
        attn_shares[0],
        attn_shares[1],
        attn_shares[2],
        attn_shares[3],
        jnp.concatenate(gate_shares, axis=1),
        jnp.concatenate(up_shares, axis=1),
        jnp.concatenate(down_shares, axis=1),
    )


VMEM_BYTES = 56 * 1024 * 1024
TILE_VMEM_BYTES = 16 * 1024 * 1024
CROSS_VMEM_BYTES = 36 * 1024 * 1024
GELU_RATE = 0.7978845608028654
TILE = 256
CHUNK = 768


def seq_swap(block, bit):
    return lax.ppermute(block, "seq", [(place, place ^ bit) for place in range(8)])


def row_swap(block, bit):
    return lax.ppermute(block, "row", [(place, place ^ bit) for place in range(4)])


def row_shift(block, step):
    return lax.ppermute(
        block, "row", [(place, place + step) for place in range(4) if 0 <= place + step < 4]
    )


def join_kernel(place_ref, own, *refs):
    below, above, (out_ref, sems) = refs[:3], refs[3:6], refs[6:]

    def join(place):
        copies = [
            pltpu.make_async_copy(
                own if q == place else below[place - q - 1] if q < place else above[q - place - 1],
                out_ref.at[:, q],
                sems.at[q],
            )
            for q in range(4)
        ]
        for copy in copies:
            copy.start()
        for copy in copies:
            copy.wait()

    for place in range(4):
        pl.when(place_ref[0] == place)(functools.partial(join, place))


def ordered_quarters(own, below, above):
    _, rows, columns = own.shape
    joined = pl.pallas_call(
        join_kernel,
        in_specs=[pl.BlockSpec(memory_space=pltpu.SMEM)] + [pl.BlockSpec(memory_space=pl.ANY)] * 7,
        out_specs=pl.BlockSpec(memory_space=pltpu.VMEM),
        out_shape=jax.ShapeDtypeStruct((8, 4, rows, columns), own.dtype),
        scratch_shapes=[pltpu.SemaphoreType.DMA((4,))],
        compiler_params=pltpu.CompilerParams(vmem_limit_bytes=TILE_VMEM_BYTES),
        cost_estimate=pl.CostEstimate(flops=1, bytes_accessed=1, transcendentals=0),
    )(jnp.full((1,), lax.axis_index("row"), jnp.int32), own, *below, *above)
    return joined.reshape(32 * rows, columns)


def bf(values):
    return values.astype(jnp.bfloat16)


def wide(values):
    return values.astype(jnp.float32)


RELATIVE = (0, 2, 4, 6, 1, 3, 5, 7)


def pin(*values):
    return lax.optimization_barrier(values)


def gather_near(block):
    return block, seq_swap(block, 2), seq_swap(block, 4)


def gather_far(block, from_x, from_y):
    half = block.shape[0] // 2
    far_first = seq_swap(from_y[:half], 2)
    far_last = seq_swap(from_x[half:], 4)
    return jnp.concatenate([block, from_x, from_y, far_first, far_last])


def gather_row(block):
    mine = gather_far(*gather_near(block))
    return mine, seq_swap(mine, 1)


def other_core(rows):
    middle = rows.shape[0] // 2
    theirs = seq_swap(rows, 1)
    return jnp.concatenate([theirs[middle:], theirs[:middle]])


def scatter_core(partial_half):
    theirs = seq_swap(partial_half(1, jnp.bfloat16), 1)
    return scatter_parts(partial_half(0, jnp.float32) + wide(theirs))


def scatter_parts(mine):
    unit = mine.shape[0] // 4
    half = unit // 2
    here, by_x, by_y, far = (mine[i * unit : (i + 1) * unit] for i in range(4))
    to_x = bf(jnp.concatenate([by_x[:half], far[:half]]))
    to_y = bf(jnp.concatenate([by_y[half:], far[half:]]))
    return here, by_x[half:], by_y[:half], to_x, to_y


def scatter_near(here, by_x, by_y, to_x, to_y):
    return here, by_x, by_y, seq_swap(to_x, 2), seq_swap(to_y, 4)


def scatter_far(here, by_x, by_y, from_x, from_y):
    half = here.shape[0] // 2
    last_y = seq_swap(bf(by_y + wide(from_x[half:])), 4)
    last_x = seq_swap(bf(by_x + wide(from_y[half:])), 2)
    return jnp.concatenate(
        [
            here[:half] + wide(from_x[:half]) + wide(last_y),
            here[half:] + wide(from_y[:half]) + wide(last_x),
        ]
    )


def scatter_row(partial_half):
    return scatter_far(*scatter_near(*scatter_core(partial_half)))


def pack_kernel(decoders, place_ref, *refs):
    codes, outs = refs[: len(decoders)], refs[len(decoders) :]
    rows = [bf(wide(decode(code_ref[...]))) for decode, code_ref in zip(decoders, codes)]
    if len(outs) == 1:
        column = 0
        for part in rows:
            outs[0][0, :, column : column + part.shape[1]] = part
            column += part.shape[1]
    else:
        column = 0
        for out_ref in outs:
            out_ref[0] = rows[0][:, column : column + out_ref.shape[2]]
            column += out_ref.shape[2]


def exact_eight(codes):
    return codes


def exact_four(codes):
    return (codes & -16) + 8


def exact_two(codes):
    return (codes & -64) + 32


def pack_codes(code_arrays, decoders, parts, part, widths=None):
    rows = code_arrays[0].shape[0] // parts
    columns = [codes.shape[1] // 8 for codes in code_arrays]
    widths = widths or [sum(columns)]
    found = pl.pallas_call(
        functools.partial(pack_kernel, decoders),
        grid_spec=pltpu.PrefetchScalarGridSpec(
            num_scalar_prefetch=1,
            grid=(8,),
            in_specs=[pl.BlockSpec((rows, c), lambda j, p: (p[0], j)) for c in columns],
            out_specs=[pl.BlockSpec((1, rows, w), lambda j, p: (j, 0, 0)) for w in widths],
        ),
        out_shape=[jax.ShapeDtypeStruct((8, rows, w), jnp.bfloat16) for w in widths],
        compiler_params=pltpu.CompilerParams(vmem_limit_bytes=VMEM_BYTES),
        cost_estimate=pl.CostEstimate(
            flops=0, bytes_accessed=rows * sum(columns) * 48, transcendentals=0
        ),
    )(jnp.full((1,), part, jnp.int32), *code_arrays)
    return found if len(widths) > 1 else found[0]


def unpack_kernel(block_ref, *out_refs):
    rows = block_ref.shape[2]
    column = 0
    for out_ref in out_refs:
        end = column + out_ref.shape[1]
        for part in range(block_ref.shape[0]):
            out_ref[part * rows : (part + 1) * rows, :] = wide(block_ref[part, 0, :, column:end])
        column = end


def unpack_blocks(blocks, widths):
    parts, _, rows, columns = blocks.shape
    return pl.pallas_call(
        unpack_kernel,
        grid=(8,),
        in_specs=[pl.BlockSpec((parts, 1, rows, columns), lambda j: (0, j, 0, 0))],
        out_specs=[pl.BlockSpec((parts * rows, w), lambda j: (0, j)) for w in widths],
        out_shape=[jax.ShapeDtypeStruct((parts * rows, 8 * w), jnp.float32) for w in widths],
        compiler_params=pltpu.CompilerParams(vmem_limit_bytes=VMEM_BYTES),
        cost_estimate=pl.CostEstimate(flops=0, bytes_accessed=6 * blocks.size, transcendentals=0),
    )(blocks)


def trade(blocks):
    return lax.all_to_all(blocks, "seq", 0, 0, tiled=True)


def dot(left, right):
    return jnp.dot(left, right, preferred_element_type=jnp.float32)


def turn(values, cosine, sine):
    half = values.shape[-1] // 2
    first, last = values[..., :half], values[..., half:]
    return jnp.concatenate([first * cosine - last * sine, last * cosine + first * sine], axis=-1)


def norm_back(values, gain, upstream):
    scale = rms_scale(values)
    lifted = upstream * gain
    shared = jnp.mean(lifted * values, axis=-1, keepdims=True)
    gradient = scale * lifted - values * (scale * scale * scale) * shared
    return gradient, jnp.sum(upstream * values * scale, axis=0)


def gelu_parts(values):
    inner = GELU_RATE * (values + 0.044715 * values * values * values)
    bent = jnp.tanh(inner)
    slope = 0.5 * (1.0 + bent) + 0.5 * values * (1.0 - bent * bent) * GELU_RATE * (
        1.0 + 3.0 * 0.044715 * values * values
    )
    return 0.5 * values * (1.0 + bent), slope


def whole_spec(weight):
    return pl.BlockSpec(memory_space=pltpu.VMEM)


def tile_calls(kernel, grid, in_specs, arrays, out_specs, out_shape, scratch=()):
    return pl.pallas_call(
        kernel,
        grid=grid,
        in_specs=in_specs,
        out_specs=out_specs,
        out_shape=out_shape,
        scratch_shapes=scratch,
        compiler_params=pltpu.CompilerParams(vmem_limit_bytes=TILE_VMEM_BYTES),
        cost_estimate=pl.CostEstimate(flops=1, bytes_accessed=1, transcendentals=0),
    )(*arrays)


def source_specs(count, tile, columns, steps):
    specs = [
        pl.BlockSpec((tile, columns), lambda i: (jnp.minimum(i, steps - 1), 0)),
        pl.BlockSpec((tile, columns), lambda i: (jnp.maximum(i - steps, 0), 0)),
    ]
    return specs[:count]


def on_source(steps, sources, action):
    if len(sources) == 1:
        action(sources[0][...])
    else:
        pl.when(pl.program_id(0) < steps)(lambda: action(sources[0][...]))
        pl.when(pl.program_id(0) >= steps)(lambda: action(sources[1][...]))


def up_kernel(steps, scale, *refs):
    *sources, w_gate, w_up, mixed_ref, to_gate_ref, to_up_ref = refs

    def action(rows):
        gate = dot(rows, w_gate[...]) * scale
        up = dot(rows, w_up[...]) * scale
        value, slope = gelu_parts(gate)
        mixed_ref[...] = bf(value * up)
        to_gate_ref[...] = bf(slope * up)
        to_up_ref[...] = bf(value)

    on_source(steps, sources, action)


def up_project(halves, w_gate, w_up, scale):
    rows, columns = halves[0].shape
    hidden = w_gate.shape[1]
    steps = rows // TILE
    return tile_calls(
        functools.partial(up_kernel, steps, scale),
        (len(halves) * steps,),
        source_specs(len(halves), TILE, columns, steps) + [whole_spec(w_gate), whole_spec(w_up)],
        (*halves, w_gate, w_up),
        [pl.BlockSpec((TILE, hidden), lambda i: (i, 0))] * 3,
        [jax.ShapeDtypeStruct((len(halves) * rows, hidden), jnp.bfloat16)] * 3,
    )


def back_kernel(steps, scale, *refs):
    *sources, w_down, to_gate_ref, to_up_ref, gate_ref, up_ref = refs

    def action(rows):
        grad_mixed = dot(rows, w_down[...]) * scale
        gate_ref[...] = bf(grad_mixed * wide(to_gate_ref[...]))
        up_ref[...] = bf(grad_mixed * wide(to_up_ref[...]))

    on_source(steps, sources, action)


def back_project(halves, w_down, factors, scale):
    rows, columns = halves[0].shape
    hidden = w_down.shape[1]
    steps = rows // TILE
    part = pl.BlockSpec((TILE, hidden), lambda i: (i, 0))
    return tile_calls(
        functools.partial(back_kernel, steps, scale),
        (len(halves) * steps,),
        source_specs(len(halves), TILE, columns, steps) + [whole_spec(w_down), part, part],
        (*halves, w_down, *factors),
        [part] * 2,
        [jax.ShapeDtypeStruct((len(halves) * rows, hidden), jnp.bfloat16)] * 2,
    )


def cross_kernel(steps, n_left, n_right, *refs):
    lefts, rights = refs[:n_left], refs[n_left : n_left + n_right]
    out_ref, left_buf, right_buf, total, sems = refs[n_left + n_right :]

    def copies(step):
        slot = step % 2
        found = []
        at = 0
        for left, left_row, right, right_row, count in steps[step]:
            found.append(
                pltpu.make_async_copy(
                    lefts[left].at[pl.ds(left_row, count)],
                    left_buf.at[slot, pl.ds(at, count)],
                    sems.at[slot, len(found)],
                )
            )
            found.append(
                pltpu.make_async_copy(
                    rights[right].at[pl.ds(right_row, count)],
                    right_buf.at[slot, pl.ds(at, count)],
                    sems.at[slot, len(found)],
                )
            )
            at += count
        return found

    for copy in copies(0):
        copy.start()
    chunk = out_ref.shape[2]
    for step in range(len(steps)):
        slot = step % 2
        if step + 1 < len(steps):
            for copy in copies(step + 1):
                copy.start()
        for copy in copies(step):
            copy.wait()

        @pl.loop(0, total.shape[0] // CHUNK)
        def _(m):
            columns = pl.ds(pl.multiple_of(m * CHUNK, CHUNK), CHUNK)
            term = cross_rows(left_buf[slot, :, columns], right_buf[slot])
            if step > 0:
                term = term + total[columns, :]
            total[columns, :] = term

    for place in range(8):
        for part in range(out_ref.shape[0]):
            start = (place * out_ref.shape[0] + part) * chunk
            out_ref[part, place] = bf(total[start : start + chunk, :])


def cross_products(lefts, rights, steps, parts=1):
    wide_rows, columns = lefts[0].shape[1], rights[0].shape[1]
    depth = max(sum(piece[4] for piece in step) for step in steps)
    pieces = max(2 * len(step) for step in steps)
    return pl.pallas_call(
        functools.partial(cross_kernel, steps, len(lefts), len(rights)),
        in_specs=[pl.BlockSpec(memory_space=pl.ANY)] * (len(lefts) + len(rights)),
        out_shape=jax.ShapeDtypeStruct((parts, 8, wide_rows // 8 // parts, columns), jnp.bfloat16),
        scratch_shapes=[
            pltpu.VMEM((2, depth, wide_rows), jnp.bfloat16),
            pltpu.VMEM((2, depth, columns), jnp.bfloat16),
            pltpu.VMEM((wide_rows, columns), jnp.float32),
            pltpu.SemaphoreType.DMA((2, pieces)),
        ],
        compiler_params=pltpu.CompilerParams(vmem_limit_bytes=CROSS_VMEM_BYTES),
        cost_estimate=pl.CostEstimate(flops=1, bytes_accessed=1, transcendentals=0),
    )(*lefts, *rights)


def partial_kernel(*refs):
    out_ref, pairs = refs[-1], refs[:-1]
    total = times_transposed(pairs[0][...], pairs[1][...])
    for left, right in zip(pairs[2::2], pairs[3::2]):
        total = total + times_transposed(left[...], right[...])
    out_ref[...] = total.astype(out_ref.dtype)


def partial_product(pairs, side, kind):
    rows, hidden = pairs[0][0].shape
    columns = pairs[0][1].shape[0]
    half = rows // 2
    steps = half // TILE
    left_spec = pl.BlockSpec((TILE, hidden), lambda i: (side * steps + i, 0))
    return tile_calls(
        partial_kernel,
        (steps,),
        [spec for pair in pairs for spec in (left_spec, whole_spec(pair[1]))],
        [array for pair in pairs for array in pair],
        pl.BlockSpec((TILE, columns), lambda i: (i, 0)),
        jax.ShapeDtypeStruct((half, columns), kind),
    )


def plane_body(
    hidden_in,
    cotangent,
    doc_lengths,
    gain_attn_in,
    gain_attn_out,
    gain_ffw_in,
    gain_ffw_out,
    query_codes,
    key_integer_codes,
    value_integer_codes,
    out_codes,
    gate_codes,
    up_codes,
    down_codes,
):
    lengths = doc_lengths[0]
    block_rows, width = hidden_in.shape[1:]
    row_length = block_rows * 8
    place = lax.axis_index("seq")
    core = place % 2
    head = HEAD_SIZE
    half = head // 2
    scale_qk = key_unit * MODEL_WIDTH ** (-0.5)
    scale_in = code_unit * MODEL_WIDTH ** (-0.5)
    scale_out = code_unit * (QUERY_HEADS * HEAD_SIZE) ** (-0.5)
    scale_down = code_unit * FF ** (-0.5)
    head_scale = HEAD_SIZE ** (-0.5)

    row_place = lax.axis_index("row")
    model_rows = query_codes.shape[0]
    hidden_part = gate_codes.shape[1] // 8

    def both_ways(below, above):
        return row_shift(below, 1), row_shift(above, -1)

    near_tokens = gather_near(hidden_in[0])
    down_blocks = pack_codes([down_codes], [exact_two], 4, row_place)
    near_tokens, down_blocks = pin(near_tokens, down_blocks)
    own_down = trade(down_blocks)
    attn_blocks = pack_codes(
        [query_codes, key_integer_codes, value_integer_codes, out_codes], [exact_eight] * 4, 1, 0
    )
    attn_blocks, own_down = pin(attn_blocks, own_down)
    attn_weights, gate_blocks, up_blocks, down_one = pin(
        trade(attn_blocks).reshape(width, 3 * head),
        pack_codes([gate_codes], [exact_four], 1, 0),
        pack_codes([up_codes], [exact_four], 1, 0),
        both_ways(own_down, own_down),
    )
    gate_rows = trade(gate_blocks)
    w_attn_in = attn_weights[:, : 2 * head]
    w_out = attn_weights[:, 2 * head :]

    token_blocks = [(place ^ k) * block_rows + jnp.arange(block_rows) for k in RELATIVE]
    token_index = jnp.concatenate(token_blocks).astype(jnp.int32)
    ends = jnp.cumsum(lengths)
    past = token_index[:, None] >= ends[None, :]
    doc_start = jnp.max(jnp.where(past, ends[None, :], 0), axis=1)
    cosine, sine = rotary_tables(token_index - doc_start, head)
    visible = (token_index[None, :] <= token_index[:, None]) & (
        token_index[None, :] >= doc_start[:, None]
    )

    tokens = wide(hidden_in[0])
    upstream = wide(cotangent[0])
    tokens_mine = gather_far(*near_tokens)
    row_tokens = jnp.concatenate([tokens_mine, seq_swap(tokens_mine, 1)])
    normed_in = bf(norm_gain(wide(row_tokens), gain_attn_in))
    linear = dot(normed_in, w_attn_in)
    query = bf(turn(linear[:, :head] * scale_qk, cosine, sine))
    key_half = linear[:, head : head + half] * scale_qk
    value_half = bf(linear[:, head + half :] * scale_in)
    key_other = other_core(key_half)
    value_other = other_core(value_half)

    def pair(own, other):
        return jnp.where(
            core == 0,
            jnp.concatenate([own, other], axis=-1),
            jnp.concatenate([other, own], axis=-1),
        )

    key = bf(turn(pair(key_half, key_other), cosine, sine))
    value = pair(value_half, value_other)
    bend = jnp.tanh(times_transposed(query, key) * (head_scale / SOFTCAP))
    weights = jnp.where(visible, jnp.exp(SOFTCAP * bend), 0.0)
    totals = jnp.sum(weights, axis=-1, keepdims=True)
    attended_wide = dot(bf(weights), value) / totals
    attended = bf(attended_wide)
    attended, gate_rows, down_two = pin(attended, gate_rows, both_ways(*down_one))
    near_half = row_length // 2
    attn_core = scatter_core(
        lambda side, kind: times_transposed(
            attended[side * near_half :][:near_half], w_out
        ).astype(kind)
    )
    (attn_core,) = pin(attn_core)
    attn_near, down_three = pin(scatter_near(*attn_core), both_ways(*down_two))
    attn_proj, up_blocks = pin(scale_out * scatter_far(*attn_near), up_blocks)
    up_rows = trade(up_blocks)
    middle = tokens + norm_gain(attn_proj, gain_attn_out)
    normed_mid = bf(norm_gain(middle, gain_ffw_in))

    mid_near, up_rows, mid_two, mid_three = pin(
        gather_near(normed_mid), up_rows, row_swap(normed_mid, 2), row_swap(normed_mid, 3)
    )
    mid_mine = gather_far(*mid_near)
    mid_mine, mid_theirs, w_down = pin(
        mid_mine,
        seq_swap(mid_mine, 1),
        ordered_quarters(own_down, *zip(down_one, down_two, down_three)),
    )
    w_gate, w_up = gate_rows.reshape(width, hidden_part), up_rows.reshape(width, hidden_part)

    def up_again(*halves):
        return up_project(halves, w_gate, w_up, scale_in)

    def back_again(halves, factors):
        return back_project(halves, w_down, factors, scale_down)

    def cut(rows):
        middle = 2 * block_rows
        return rows[:middle], rows[middle : middle + block_rows], rows[middle + block_rows :]

    (mixed, *factors), pair_mid_near, mid_cuts = pin(
        up_again(mid_mine, mid_theirs),
        gather_near(jnp.concatenate([mid_two, mid_three])),
        cut(mid_mine),
    )
    ffn_core, pair_mid_mine, third_mid_first = pin(
        scatter_core(lambda side, kind: partial_product([(mixed, w_down)], side, kind)),
        gather_far(*pair_mid_near),
        row_swap(mid_cuts[0], 1),
    )
    ffn_near, pair_mid_theirs, third_mid_second = pin(
        scatter_near(*ffn_core), seq_swap(pair_mid_mine, 1), row_swap(mid_cuts[1], 1)
    )
    ffn_proj, third_mid_last, pair_mid_mine = pin(
        scale_down * scatter_far(*ffn_near), row_swap(mid_cuts[2], 1), pair_mid_mine
    )
    third_mid_mine = jnp.concatenate([third_mid_first, third_mid_second, third_mid_last])
    block_out = bf(middle + norm_gain(ffn_proj, gain_ffw_out))
    grad_ffn, grad_gain_four = norm_back(ffn_proj, gain_ffw_out, upstream)
    grad_ffn_low = bf(grad_ffn)
    grad_near, grad_two, (mine_mixed, *mine_factors) = pin(
        gather_near(grad_ffn_low), row_swap(grad_ffn_low, 2), up_again(pair_mid_mine)
    )
    grad_mine = gather_far(*grad_near)
    grad_mine, grad_theirs, grad_three, third_mid_theirs, (theirs_mixed, *theirs_factors) = pin(
        grad_mine,
        seq_swap(grad_mine, 1),
        row_swap(grad_ffn_low, 3),
        seq_swap(third_mid_mine, 1),
        up_again(pair_mid_theirs),
    )
    grad_cuts = grad_mine[: 2 * block_rows], grad_mine[2 * block_rows :]
    grads_hidden, pair_grad_near, third_grad_first = pin(
        back_again((grad_mine, grad_theirs), factors),
        gather_near(jnp.concatenate([grad_two, grad_three])),
        row_swap(grad_cuts[0], 1),
    )
    pairs = list(zip(grads_hidden, (w_gate, w_up)))
    mid_core, pair_grad_mine, third_grad_last = pin(
        scatter_core(lambda side, kind: partial_product(pairs, side, kind)),
        gather_far(*pair_grad_near),
        row_swap(grad_cuts[1], 1),
    )
    third_grad_mine = jnp.concatenate([third_grad_first, third_grad_last])
    sum_near, pair_grad_theirs, third_grad_theirs, (third_mixed, *third_factors), mine_hidden = pin(
        scatter_near(*mid_core),
        seq_swap(pair_grad_mine, 1),
        seq_swap(third_grad_mine, 1),
        up_again(third_mid_mine, third_mid_theirs),
        back_again((pair_grad_mine,), mine_factors),
    )
    grad_mid, theirs_hidden = pin(
        scale_in * scatter_far(*sum_near), back_again((pair_grad_theirs,), theirs_factors)
    )
    grad_middle_part, grad_gain_three = norm_back(middle, gain_ffw_in, grad_mid)
    grad_middle = upstream + grad_middle_part
    grad_proj, grad_gain_two = norm_back(attn_proj, gain_attn_out, grad_middle)

    row_half = row_length // 2
    mids = (mid_mine, mid_theirs, pair_mid_mine, pair_mid_theirs, third_mid_mine, third_mid_theirs)
    outs = (
        grad_mine,
        grad_theirs,
        pair_grad_mine,
        pair_grad_theirs,
        third_grad_mine,
        third_grad_theirs,
    )
    steps = (
        ((0, 0, 0, 0, row_half), (1, 0, 0, row_half, row_half)),
        ((2, 0, 1, 0, row_length),),
        ((3, 0, 2, 0, row_length),),
        ((4, 0, 3, 0, row_half), (5, 0, 3, row_half, row_half)),
    )
    proj_near, down_blocks, third_grads = pin(
        gather_near(bf(grad_proj)),
        cross_products(outs, (mixed, mine_mixed, theirs_mixed, third_mixed), steps),
        (third_grad_mine, third_grad_theirs),
    )
    proj_mine, down_blocks = pin(gather_far(*proj_near), down_blocks)
    down_blocks = trade(down_blocks[0])
    row_proj = jnp.concatenate([proj_mine, seq_swap(proj_mine, 1)])

    def halve(terms, bit, axis, side):
        kept = lax.dynamic_index_in_dim(terms, side, axis, keepdims=False)
        sent = lax.dynamic_index_in_dim(terms, 1 - side, axis, keepdims=False)
        return bf(wide(kept) + wide(row_swap(sent, bit)))

    def quarters_of(part):
        return bf(part).reshape(8, 2, 2, model_rows // 4, part.shape[1])

    low_bit, high_bit = row_place % 2, row_place // 2

    grad_attended = bf(dot(row_proj, w_out) * scale_out)
    delta = jnp.sum(wide(grad_attended) * attended_wide, axis=-1, keepdims=True)
    probs = weights / totals
    grad_probs = times_transposed(grad_attended, value)
    grad_raw = bf(probs * (grad_probs - delta) * (1.0 - bend * bend))
    grad_query = bf(turn(dot(grad_raw, key) * head_scale, cosine, -sine))
    key_part = cross_rows(grad_raw, query) * head_scale
    value_part = cross_rows(bf(probs), grad_attended)

    def own_half(values, side):
        return lax.dynamic_slice_in_dim(values, side * half, half, axis=1)

    key_sum = key_part + other_core(key_part)
    grad_key = bf(own_half(turn(key_sum, cosine, -sine), core))
    grad_value = bf(own_half(value_part, core) + other_core(own_half(value_part, 1 - core)))
    grad_linear = jnp.concatenate([grad_query, grad_key, grad_value], axis=1)
    grad_linear, out_sum, third_grads = pin(
        grad_linear,
        halve(quarters_of(cross_rows(row_proj, attended)), 1, 2, low_bit),
        third_grads,
    )

    def grad_in_half(side, kind):
        rows = grad_linear[side * near_half :][:near_half]
        total = scale_qk * times_transposed(
            rows[:, : head + half], w_attn_in[:, : head + half]
        ) + scale_in * times_transposed(rows[:, head + half :], w_attn_in[:, head + half :])
        return total.astype(kind)

    in_core, in_terms, out_sum, third_grads = pin(
        scatter_core(grad_in_half),
        quarters_of(cross_rows(normed_in, grad_linear)),
        halve(out_sum, 2, 1, high_bit),
        third_grads,
    )
    third_hidden = back_again(third_grads, third_factors)
    gate_terms, up_terms = zip(grads_hidden, mine_hidden, theirs_hidden, third_hidden)
    in_near, in_sum, gate_blocks, up_terms, down_blocks = pin(
        scatter_near(*in_core),
        halve(in_terms, 1, 2, low_bit),
        cross_products(mids, gate_terms, steps),
        up_terms,
        down_blocks,
    )
    gate_blocks = trade(gate_blocks[0])
    in_sum, grad_in, up_blocks, gate_blocks = pin(
        halve(in_sum, 2, 1, high_bit),
        scatter_far(*in_near),
        cross_products(mids, up_terms, steps),
        gate_blocks,
    )
    grad_tokens, grad_gain_one = norm_back(tokens, gain_attn_in, grad_in)
    grad_input = grad_middle + grad_tokens
    gain_terms = jnp.stack([grad_gain_one, grad_gain_two, grad_gain_three, grad_gain_four])
    sums = jnp.concatenate([in_sum, out_sum], axis=2)
    own_rows, columns = sums.shape[1:]
    gain_terms = bf(gain_terms.reshape(4, 8, model_rows).transpose(1, 0, 2)).reshape(8, -1)
    gain_rows = -(-gain_terms.shape[1] // columns // 8) * 8
    gain_terms = jnp.pad(gain_terms, ((0, 0), (0, gain_rows * columns - gain_terms.shape[1])))
    sums = jnp.concatenate([sums, gain_terms.reshape(8, gain_rows, columns)], axis=1)
    sums, up_blocks = pin(trade(sums), up_blocks)
    up_blocks = trade(up_blocks[0])
    gain_blocks = wide(sums[:, own_rows:]).reshape(8, -1)[:, : 4 * model_rows]
    gain_blocks = gain_blocks.reshape(8, 4, model_rows)
    sums = sums[:, :own_rows]

    def double(blocks, received, side):
        both_sides = jnp.stack([blocks, received])
        return jnp.where(side == 0, both_sides, both_sides[::-1])

    gains = jnp.sum(gain_blocks, axis=0)
    gains = gains + row_swap(gains, 1)
    blocks, gains = pin(
        double(sums, row_swap(sums, 2), high_bit), gains + row_swap(gains, 2)
    )
    received = row_swap(blocks, 1)
    grad_w_gate, grad_w_up, grad_w_down = (
        unpack_blocks(blocks, [hidden_part])[0]
        for blocks in (gate_blocks[None], up_blocks[None], down_blocks[None])
    )
    blocks, grad_w_up = pin(blocks, grad_w_up)
    blocks = double(blocks, received, low_bit).transpose(1, 0, 2, 3, 4)
    attn_grads = unpack_blocks(blocks.reshape(4, *sums.shape), [head, half, half, head])

    return (
        block_out[None],
        grad_input[None],
        gains[0],
        gains[1],
        gains[2],
        gains[3],
        attn_grads[0],
        attn_grads[1],
        attn_grads[2],
        attn_grads[3],
        grad_w_gate,
        grad_w_up,
        grad_w_down,
    )


def solution(mesh):
    body = plane_body if dict(mesh.shape) == {"seq": 8, "row": 4} else token_body
    return jax.shard_map(
        body,
        mesh=mesh,
        in_specs=(
            P("row", "seq", None),
            P("row", "seq", None),
            P("row", None),
            P(),
            P(),
            P(),
            P(),
            P("seq", None),
            P("seq", None),
            P("seq", None),
            P("seq", None),
            P("seq", None),
            P("seq", None),
            P("seq", None),
        ),
        out_specs=(
            P("row", "seq", None),
            P("row", "seq", None),
            P("seq"),
            P("seq"),
            P("seq"),
            P("seq"),
            P("seq", None),
            P("seq", None),
            P("seq", None),
            P("seq", None),
            P("seq", None),
            P("seq", None),
            P("seq", None),
        ),
        check_vma=False,
    )
```

```python
import functools

import jax
import jax.numpy as jnp
from jax import lax
from jax.experimental import pallas as pl
from jax.experimental.pallas import tpu as pltpu
from jax.sharding import PartitionSpec as P

MODEL_WIDTH = 2304
QUERY_HEADS = 8
KEY_VALUE_HEADS = 4
HEAD_SIZE = 256
FF = 9216
SOFTCAP = 15


epsilon = 1e-06
code_unit = 1.0 / 72.0
key_unit = 1.0 / 44.0
large_negative_fill = -1e30


def codes_eight(code_block):
    return code_block.astype(jnp.bfloat16)


def codes_four(code_block):
    return (code_block // 16 * 16 + 8).astype(jnp.bfloat16)


def codes_two(code_block):
    return (code_block // 64 * 64 + 32).astype(jnp.bfloat16)


def rms_scale(values):
    return lax.rsqrt(jnp.mean(values * values, axis=-1, keepdims=True) + epsilon)


def norm_gain(values, gain_vector):
    return values * rms_scale(values) * gain_vector


def geglu(gate_values, up_values):
    return jax.nn.gelu(gate_values, approximate=True) * up_values


def cross_rows(left_side, right_side):
    return lax.dot_general(
        left_side, right_side, (((0,), (0,)), ((), ())), preferred_element_type=jnp.float32
    )


def times_transposed(left_side, right_side):
    return lax.dot_general(
        left_side, right_side, (((1,), (1,)), ((), ())), preferred_element_type=jnp.float32
    )


def doc_layout(lengths, first_index, row_count):
    doc_ends = jnp.cumsum(lengths)
    starts = doc_ends - lengths
    token_index = first_index + jnp.arange(row_count, dtype=jnp.int32)
    doc_number = jnp.sum((token_index[:, None] >= doc_ends[None, :]).astype(jnp.int32), axis=1)
    picked = doc_number[:, None] == jnp.arange(lengths.shape[0], dtype=jnp.int32)[None, :]
    doc_start = jnp.sum(jnp.where(picked, starts[None, :], 0), axis=1)
    return (token_index, doc_start)


def rotary_tables(positions, head_size):
    half_size = head_size // 2
    frequencies = 10000.0 ** (-(2.0 * jnp.arange(half_size, dtype=jnp.float32)) / head_size)
    angles = positions.astype(jnp.float32)[:, None] * frequencies[None, :]
    return (jnp.cos(angles), jnp.sin(angles))


def apply_rotary(values, cosine_table, sine_table):
    half_size = values.shape[-1] // 2
    first_half = values[..., :half_size]
    second_half = values[..., half_size:]
    cos_wide = cosine_table[:, None, :]
    sin_wide = sine_table[:, None, :]
    return jnp.concatenate(
        [
            first_half * cos_wide - second_half * sin_wide,
            second_half * cos_wide + first_half * sin_wide,
        ],
        axis=-1,
    )


def inverse_rotary(value_gradients, cosine_table, sine_table):
    half_size = value_gradients.shape[-1] // 2
    first_half = value_gradients[..., :half_size]
    second_half = value_gradients[..., half_size:]
    cos_wide = cosine_table[:, None, :]
    sin_wide = sine_table[:, None, :]
    return jnp.concatenate(
        [
            first_half * cos_wide + second_half * sin_wide,
            second_half * cos_wide - first_half * sin_wide,
        ],
        axis=-1,
    )


def score_grads(
    heads_of_queries,
    head_gradients,
    log_totals,
    deltas,
    query_index,
    query_start,
    heads_of_keys,
    heads_of_values,
    key_index,
):
    head_scale = HEAD_SIZE ** (-0.5)
    raw_scores = (
        jnp.einsum(
            "tkgd,rkd->kgtr", heads_of_queries, heads_of_keys, preferred_element_type=jnp.float32
        )
        * head_scale
    )
    capped = SOFTCAP * jnp.tanh(raw_scores / SOFTCAP)
    visible = (key_index[None, :] <= query_index[:, None]) & (
        key_index[None, :] >= query_start[:, None]
    )
    probs = jnp.where(visible, jnp.exp(capped - log_totals[..., None]), 0.0)
    grad_probs = jnp.einsum(
        "tkgd,rkd->kgtr", head_gradients, heads_of_values, preferred_element_type=jnp.float32
    )
    grad_capped = probs * (grad_probs - deltas[..., None])
    grad_raw = (grad_capped * (1.0 - (capped / SOFTCAP) ** 2)).astype(jnp.bfloat16)
    return (grad_raw, probs.astype(jnp.bfloat16))


def reduce_terms(grad_terms):
    shares = lax.psum_scatter(grad_terms, "seq", scatter_dimension=0, tiled=True)
    return lax.psum(shares, "row")


def token_body(
    hidden_in,
    cotangent,
    doc_lengths,
    gain_attn_in,
    gain_attn_out,
    gain_ffw_in,
    gain_ffw_out,
    query_codes,
    key_integer_codes,
    value_integer_codes,
    out_codes,
    gate_codes,
    up_codes,
    down_codes,
):
    tokens = hidden_in[0].astype(jnp.float32)
    upstream = cotangent[0].astype(jnp.float32)
    lengths = doc_lengths[0]
    resident_rows = tokens.shape[0]
    heads_per_group = QUERY_HEADS // KEY_VALUE_HEADS
    head_scale = HEAD_SIZE ** (-0.5)
    scale_qk = key_unit * MODEL_WIDTH ** (-0.5)
    scale_in = code_unit * MODEL_WIDTH ** (-0.5)
    scale_out = code_unit * (QUERY_HEADS * HEAD_SIZE) ** (-0.5)
    scale_down = code_unit * FF ** (-0.5)
    part_count = 8
    part_width = gate_codes.shape[1] // part_count
    first_row = lax.axis_index("seq") * resident_rows
    local_index, local_start = doc_layout(lengths, first_row, resident_rows)
    cosine_table, sine_table = rotary_tables(local_index - local_start, HEAD_SIZE)

    def attention_weights():
        return (
            lax.all_gather(codes_eight(query_codes), "seq", axis=0, tiled=True),
            lax.all_gather(codes_eight(key_integer_codes), "seq", axis=0, tiled=True),
            lax.all_gather(codes_eight(value_integer_codes), "seq", axis=0, tiled=True),
            lax.all_gather(codes_eight(out_codes), "seq", axis=0, tiled=True),
        )

    def ffn_weights(part_number):
        column_start = part_number * part_width
        column_end = column_start + part_width
        return (
            lax.all_gather(
                codes_four(gate_codes[:, column_start:column_end]), "seq", axis=0, tiled=True
            ),
            lax.all_gather(
                codes_four(up_codes[:, column_start:column_end]), "seq", axis=0, tiled=True
            ),
            lax.all_gather(
                codes_two(down_codes[:, column_start:column_end]), "seq", axis=0, tiled=True
            ),
        )

    attn_set = attention_weights()
    w_query, w_key, w_value, w_out = attn_set
    normed_in = norm_gain(tokens, gain_attn_in).astype(jnp.bfloat16)
    query_lin = jnp.dot(normed_in, w_query, preferred_element_type=jnp.float32) * scale_qk
    key_linear = jnp.dot(normed_in, w_key, preferred_element_type=jnp.float32) * scale_qk
    value_linear = jnp.dot(normed_in, w_value, preferred_element_type=jnp.float32) * scale_in
    rows_of_queries = (
        apply_rotary(
            query_lin.reshape(resident_rows, QUERY_HEADS, HEAD_SIZE), cosine_table, sine_table
        )
        .astype(jnp.bfloat16)
        .reshape(resident_rows, QUERY_HEADS * HEAD_SIZE)
    )
    rows_of_keys = (
        apply_rotary(
            key_linear.reshape(resident_rows, KEY_VALUE_HEADS, HEAD_SIZE), cosine_table, sine_table
        )
        .astype(jnp.bfloat16)
        .reshape(resident_rows, KEY_VALUE_HEADS * HEAD_SIZE)
    )
    rows_of_values = value_linear.astype(jnp.bfloat16)
    heads_of_queries = rows_of_queries.reshape(
        resident_rows, KEY_VALUE_HEADS, heads_per_group, HEAD_SIZE
    )
    running_maximum = jnp.full(
        (KEY_VALUE_HEADS, heads_per_group, resident_rows), large_negative_fill, jnp.float32
    )
    block_of_keys = lax.all_gather(rows_of_keys, "seq", axis=0, tiled=True)
    block_of_values = lax.all_gather(rows_of_values, "seq", axis=0, tiled=True)
    rows_per_block = block_of_keys.shape[0]
    heads_of_keys = block_of_keys.reshape(rows_per_block, KEY_VALUE_HEADS, HEAD_SIZE)
    heads_of_values = block_of_values.reshape(rows_per_block, KEY_VALUE_HEADS, HEAD_SIZE)
    key_index = jnp.arange(rows_per_block, dtype=jnp.int32)
    raw_scores = (
        jnp.einsum(
            "tkgd,rkd->kgtr", heads_of_queries, heads_of_keys, preferred_element_type=jnp.float32
        )
        * head_scale
    )
    capped = SOFTCAP * jnp.tanh(raw_scores / SOFTCAP)
    visible = (key_index[None, :] <= local_index[:, None]) & (
        key_index[None, :] >= local_start[:, None]
    )
    masked = jnp.where(visible, capped, large_negative_fill)
    new_max = jnp.maximum(running_maximum, jnp.max(masked, axis=-1))
    weights = jnp.where(visible, jnp.exp(masked - new_max[..., None]), 0.0)
    run_total = jnp.sum(weights, axis=-1)
    weighted = jnp.einsum(
        "kgtr,rkd->kgtd",
        weights.astype(jnp.bfloat16),
        heads_of_values,
        preferred_element_type=jnp.float32,
    )
    weighted, running_maximum, run_total = (weighted, new_max, run_total)
    attn_heads = weighted / run_total[..., None]
    log_totals = running_maximum + jnp.log(run_total)
    attended = (
        attn_heads.transpose(2, 0, 1, 3)
        .reshape(resident_rows, QUERY_HEADS * HEAD_SIZE)
        .astype(jnp.bfloat16)
    )
    attn_proj = times_transposed(attended, w_out) * scale_out
    middle = tokens + norm_gain(attn_proj, gain_attn_out)
    normed_mid = norm_gain(middle, gain_ffw_in).astype(jnp.bfloat16)
    ffn_proj = jnp.zeros((resident_rows, tokens.shape[1]), jnp.float32)
    gate_store = []
    up_store = []
    mixed_store = []
    ffn_sets = []
    for part_number in range(part_count):
        ffn_set = ffn_weights(part_number)
        w_gate, w_up, w_down = ffn_set
        gate_lin = jnp.dot(normed_mid, w_gate, preferred_element_type=jnp.float32) * scale_in
        up_lin = jnp.dot(normed_mid, w_up, preferred_element_type=jnp.float32) * scale_in
        mixed_rows = geglu(gate_lin, up_lin).astype(jnp.bfloat16)
        ffn_proj = ffn_proj + times_transposed(mixed_rows, w_down) * scale_down
        gate_store.append(gate_lin)
        up_store.append(up_lin)
        mixed_store.append(mixed_rows)
        ffn_sets.append(ffn_set)
    block_out = (middle + norm_gain(ffn_proj, gain_ffw_out)).astype(jnp.bfloat16)
    _, post_pull = jax.vjp(norm_gain, ffn_proj, gain_ffw_out)
    grad_ffn_proj, grad_gain_four = post_pull(upstream)
    grad_ffn_low = grad_ffn_proj.astype(jnp.bfloat16)
    grad_normed_mid = jnp.zeros((resident_rows, tokens.shape[1]), jnp.float32)
    gate_shares = []
    up_shares = []
    down_shares = []
    for part_number in range(part_count):
        back_ffn = ffn_weights(part_number)
        w_gate, w_up, w_down = back_ffn
        grad_mixed = jnp.dot(grad_ffn_low, w_down, preferred_element_type=jnp.float32) * scale_down
        _, geglu_pull = jax.vjp(geglu, gate_store[part_number], up_store[part_number])
        grad_gate_lin, grad_up_lin = geglu_pull(grad_mixed)
        grad_gate_low = grad_gate_lin.astype(jnp.bfloat16)
        grad_up_low = grad_up_lin.astype(jnp.bfloat16)
        grad_normed_mid = (
            grad_normed_mid
            + (times_transposed(grad_gate_low, w_gate) + times_transposed(grad_up_low, w_up))
            * scale_in
        )
        gate_share, up_share, down_share = reduce_terms(
            (
                cross_rows(normed_mid, grad_gate_low),
                cross_rows(normed_mid, grad_up_low),
                cross_rows(grad_ffn_low, mixed_store[part_number]),
            )
        )
        gate_shares.append(gate_share)
        up_shares.append(up_share)
        down_shares.append(down_share)
    _, mid_pull = jax.vjp(norm_gain, middle, gain_ffw_in)
    grad_middle_part, grad_gain_three = mid_pull(grad_normed_mid)
    grad_middle = upstream + grad_middle_part
    _, attn_pull = jax.vjp(norm_gain, attn_proj, gain_attn_out)
    grad_attn_proj, grad_gain_two = attn_pull(grad_middle)
    grad_proj_low = grad_attn_proj.astype(jnp.bfloat16)
    back_attn = attention_weights()
    back_query, back_key, back_value, back_out = back_attn
    grad_attended = jnp.dot(grad_proj_low, back_out, preferred_element_type=jnp.float32) * scale_out
    gradient_attention_narrow = grad_attended.astype(jnp.bfloat16)
    head_gradients = gradient_attention_narrow.reshape(
        resident_rows, KEY_VALUE_HEADS, heads_per_group, HEAD_SIZE
    )
    deltas = jnp.sum(
        gradient_attention_narrow.astype(jnp.float32)
        .reshape(resident_rows, KEY_VALUE_HEADS, heads_per_group, HEAD_SIZE)
        .transpose(1, 2, 0, 3)
        * attn_heads,
        axis=-1,
    )
    block_of_keys = lax.all_gather(rows_of_keys, "seq", axis=0, tiled=True)
    block_of_values = lax.all_gather(rows_of_values, "seq", axis=0, tiled=True)
    rows_per_block = block_of_keys.shape[0]
    heads_of_keys = block_of_keys.reshape(rows_per_block, KEY_VALUE_HEADS, HEAD_SIZE)
    heads_of_values = block_of_values.reshape(rows_per_block, KEY_VALUE_HEADS, HEAD_SIZE)
    key_index = jnp.arange(rows_per_block, dtype=jnp.int32)
    grad_raw, probs_low = score_grads(
        heads_of_queries,
        head_gradients,
        log_totals,
        deltas,
        local_index,
        local_start,
        heads_of_keys,
        heads_of_values,
        key_index,
    )
    grad_query_heads = (
        jnp.einsum("kgtr,rkd->tkgd", grad_raw, heads_of_keys, preferred_element_type=jnp.float32)
        * head_scale
    )
    resident_keys = rows_of_keys.reshape(resident_rows, KEY_VALUE_HEADS, HEAD_SIZE)
    resident_values = rows_of_values.reshape(resident_rows, KEY_VALUE_HEADS, HEAD_SIZE)
    block_of_queries = lax.all_gather(
        rows_of_queries.astype(jnp.float32), "seq", axis=0, tiled=True
    )
    block_gradient = lax.all_gather(
        gradient_attention_narrow.astype(jnp.float32), "seq", axis=0, tiled=True
    )
    lse_block = lax.all_gather(log_totals.transpose(2, 0, 1), "seq", axis=0, tiled=True)
    delta_block = lax.all_gather(deltas.transpose(2, 0, 1), "seq", axis=0, tiled=True)
    rows_per_block = block_of_queries.shape[0]
    foreign_queries = block_of_queries.astype(jnp.bfloat16).reshape(
        rows_per_block, KEY_VALUE_HEADS, heads_per_group, HEAD_SIZE
    )
    foreign_gradients = block_gradient.astype(jnp.bfloat16).reshape(
        rows_per_block, KEY_VALUE_HEADS, heads_per_group, HEAD_SIZE
    )
    remote_index, remote_start = doc_layout(lengths, jnp.int32(0), rows_per_block)
    grad_raw, probs_low = score_grads(
        foreign_queries,
        foreign_gradients,
        lse_block.transpose(1, 2, 0),
        delta_block.transpose(1, 2, 0),
        remote_index,
        remote_start,
        resident_keys,
        resident_values,
        local_index,
    )
    key_gradients = (
        jnp.einsum("kgtr,tkgd->rkd", grad_raw, foreign_queries, preferred_element_type=jnp.float32)
        * head_scale
    )
    value_gradients = jnp.einsum(
        "kgtr,tkgd->rkd", probs_low, foreign_gradients, preferred_element_type=jnp.float32
    )
    grad_query_lin = (
        inverse_rotary(
            grad_query_heads.reshape(resident_rows, QUERY_HEADS, HEAD_SIZE),
            cosine_table,
            sine_table,
        )
        .reshape(resident_rows, QUERY_HEADS * HEAD_SIZE)
        .astype(jnp.bfloat16)
    )
    grad_key_lin = (
        inverse_rotary(key_gradients, cosine_table, sine_table)
        .reshape(resident_rows, KEY_VALUE_HEADS * HEAD_SIZE)
        .astype(jnp.bfloat16)
    )
    value_linear_gradient = value_gradients.reshape(
        resident_rows, KEY_VALUE_HEADS * HEAD_SIZE
    ).astype(jnp.bfloat16)
    grad_normed_in = (
        times_transposed(grad_query_lin, back_query) + times_transposed(grad_key_lin, back_key)
    ) * scale_qk + times_transposed(value_linear_gradient, back_value) * scale_in
    _, in_pull = jax.vjp(norm_gain, tokens, gain_attn_in)
    grad_tokens_part, grad_gain_one = in_pull(grad_normed_in)
    grad_input = grad_middle + grad_tokens_part
    attn_shares = reduce_terms(
        (
            cross_rows(normed_in, grad_query_lin),
            cross_rows(normed_in, grad_key_lin),
            cross_rows(normed_in, value_linear_gradient),
            cross_rows(grad_proj_low, attended),
            grad_gain_one,
            grad_gain_two,
            grad_gain_three,
            grad_gain_four,
        )
    )
    return (
        block_out[None],
        grad_input[None],
        attn_shares[4],
        attn_shares[5],
        attn_shares[6],
        attn_shares[7],
        attn_shares[0],
        attn_shares[1],
        attn_shares[2],
        attn_shares[3],
        jnp.concatenate(gate_shares, axis=1),
        jnp.concatenate(up_shares, axis=1),
        jnp.concatenate(down_shares, axis=1),
    )


VMEM_BYTES = 56 * 1024 * 1024
TILE_VMEM_BYTES = 16 * 1024 * 1024
CROSS_VMEM_BYTES = 42 * 1024 * 1024
GELU_RATE = 0.7978845608028654
TILE = 256
CHUNK = 1152


def seq_swap(block, bit):
    return lax.ppermute(block, "seq", [(place, place ^ bit) for place in range(8)])


def row_swap(block, bit):
    return lax.ppermute(block, "row", [(place, place ^ bit) for place in range(4)])


def row_shift(block, step):
    return lax.ppermute(
        block, "row", [(place, place + step) for place in range(4) if 0 <= place + step < 4]
    )


def join_kernel(place_ref, own, *refs):
    below, above, (out_ref, sems) = refs[:3], refs[3:6], refs[6:]

    def join(place):
        copies = [
            pltpu.make_async_copy(
                own if q == place else below[place - q - 1] if q < place else above[q - place - 1],
                out_ref.at[:, q],
                sems.at[q],
            )
            for q in range(4)
        ]
        for copy in copies:
            copy.start()
        for copy in copies:
            copy.wait()

    for place in range(4):
        pl.when(place_ref[0] == place)(functools.partial(join, place))


def ordered_quarters(own, below, above):
    _, rows, columns = own.shape
    joined = pl.pallas_call(
        join_kernel,
        in_specs=[pl.BlockSpec(memory_space=pltpu.SMEM)] + [pl.BlockSpec(memory_space=pl.ANY)] * 7,
        out_specs=pl.BlockSpec(memory_space=pltpu.VMEM),
        out_shape=jax.ShapeDtypeStruct((8, 4, rows, columns), own.dtype),
        scratch_shapes=[pltpu.SemaphoreType.DMA((4,))],
        compiler_params=pltpu.CompilerParams(vmem_limit_bytes=TILE_VMEM_BYTES),
        cost_estimate=pl.CostEstimate(flops=1, bytes_accessed=1, transcendentals=0),
    )(jnp.full((1,), lax.axis_index("row"), jnp.int32), own, *below, *above)
    return joined.reshape(32 * rows, columns)


def bf(values):
    return values.astype(jnp.bfloat16)


def wide(values):
    return values.astype(jnp.float32)


RELATIVE = (0, 2, 4, 6, 1, 3, 5, 7)


def pin(*values):
    return lax.optimization_barrier(values)


def gather_near(block):
    return block, seq_swap(block, 2), seq_swap(block, 4)


def gather_far(block, from_x, from_y):
    half = block.shape[0] // 2
    far_first = seq_swap(from_y[:half], 2)
    far_last = seq_swap(from_x[half:], 4)
    return jnp.concatenate([block, from_x, from_y, far_first, far_last])


def gather_row(block):
    mine = gather_far(*gather_near(block))
    return mine, seq_swap(mine, 1)


def other_core(rows):
    middle = rows.shape[0] // 2
    theirs = seq_swap(rows, 1)
    return jnp.concatenate([theirs[middle:], theirs[:middle]])


def scatter_core(partial_half):
    theirs = seq_swap(partial_half(1, jnp.bfloat16), 1)
    return scatter_parts(partial_half(0, jnp.float32) + wide(theirs))


def scatter_parts(mine):
    unit = mine.shape[0] // 4
    half = unit // 2
    here, by_x, by_y, far = (mine[i * unit : (i + 1) * unit] for i in range(4))
    to_x = bf(jnp.concatenate([by_x[:half], far[:half]]))
    to_y = bf(jnp.concatenate([by_y[half:], far[half:]]))
    return here, by_x[half:], by_y[:half], to_x, to_y


def scatter_near(here, by_x, by_y, to_x, to_y):
    return here, by_x, by_y, seq_swap(to_x, 2), seq_swap(to_y, 4)


def scatter_far(here, by_x, by_y, from_x, from_y):
    half = here.shape[0] // 2
    last_y = seq_swap(bf(by_y + wide(from_x[half:])), 4)
    last_x = seq_swap(bf(by_x + wide(from_y[half:])), 2)
    return jnp.concatenate(
        [
            here[:half] + wide(from_x[:half]) + wide(last_y),
            here[half:] + wide(from_y[:half]) + wide(last_x),
        ]
    )


def scatter_row(partial_half):
    return scatter_far(*scatter_near(*scatter_core(partial_half)))


def pack_kernel(decoders, place_ref, *refs):
    codes, outs = refs[: len(decoders)], refs[len(decoders) :]
    rows = [bf(wide(decode(code_ref[...]))) for decode, code_ref in zip(decoders, codes)]
    if len(outs) == 1:
        column = 0
        for part in rows:
            outs[0][0, :, column : column + part.shape[1]] = part
            column += part.shape[1]
    else:
        column = 0
        for out_ref in outs:
            out_ref[0] = rows[0][:, column : column + out_ref.shape[2]]
            column += out_ref.shape[2]


def exact_eight(codes):
    return codes


def exact_four(codes):
    return (codes & -16) + 8


def exact_two(codes):
    return (codes & -64) + 32


def pack_codes(code_arrays, decoders, parts, part, widths=None):
    rows = code_arrays[0].shape[0] // parts
    columns = [codes.shape[1] // 8 for codes in code_arrays]
    widths = widths or [sum(columns)]
    found = pl.pallas_call(
        functools.partial(pack_kernel, decoders),
        grid_spec=pltpu.PrefetchScalarGridSpec(
            num_scalar_prefetch=1,
            grid=(8,),
            in_specs=[pl.BlockSpec((rows, c), lambda j, p: (p[0], j)) for c in columns],
            out_specs=[pl.BlockSpec((1, rows, w), lambda j, p: (j, 0, 0)) for w in widths],
        ),
        out_shape=[jax.ShapeDtypeStruct((8, rows, w), jnp.bfloat16) for w in widths],
        compiler_params=pltpu.CompilerParams(vmem_limit_bytes=VMEM_BYTES),
        cost_estimate=pl.CostEstimate(
            flops=0, bytes_accessed=rows * sum(columns) * 48, transcendentals=0
        ),
    )(jnp.full((1,), part, jnp.int32), *code_arrays)
    return found if len(widths) > 1 else found[0]


def unpack_kernel(block_ref, *out_refs):
    rows = block_ref.shape[2]
    column = 0
    for out_ref in out_refs:
        end = column + out_ref.shape[1]
        for part in range(block_ref.shape[0]):
            out_ref[part * rows : (part + 1) * rows, :] = wide(block_ref[part, 0, :, column:end])
        column = end


def unpack_blocks(blocks, widths):
    parts, _, rows, columns = blocks.shape
    return pl.pallas_call(
        unpack_kernel,
        grid=(8,),
        in_specs=[pl.BlockSpec((parts, 1, rows, columns), lambda j: (0, j, 0, 0))],
        out_specs=[pl.BlockSpec((parts * rows, w), lambda j: (0, j)) for w in widths],
        out_shape=[jax.ShapeDtypeStruct((parts * rows, 8 * w), jnp.float32) for w in widths],
        compiler_params=pltpu.CompilerParams(vmem_limit_bytes=VMEM_BYTES),
        cost_estimate=pl.CostEstimate(flops=0, bytes_accessed=6 * blocks.size, transcendentals=0),
    )(blocks)


def trade(blocks):
    return lax.all_to_all(blocks, "seq", 0, 0, tiled=True)


def dot(left, right):
    return jnp.dot(left, right, preferred_element_type=jnp.float32)


def turn(values, cosine, sine):
    half = values.shape[-1] // 2
    first, last = values[..., :half], values[..., half:]
    return jnp.concatenate([first * cosine - last * sine, last * cosine + first * sine], axis=-1)


def norm_back(values, gain, upstream):
    scale = rms_scale(values)
    lifted = upstream * gain
    shared = jnp.mean(lifted * values, axis=-1, keepdims=True)
    gradient = scale * lifted - values * (scale * scale * scale) * shared
    return gradient, jnp.sum(upstream * values * scale, axis=0)


def gelu_parts(values):
    inner = GELU_RATE * (values + 0.044715 * values * values * values)
    bent = jnp.tanh(inner)
    slope = 0.5 * (1.0 + bent) + 0.5 * values * (1.0 - bent * bent) * GELU_RATE * (
        1.0 + 3.0 * 0.044715 * values * values
    )
    return 0.5 * values * (1.0 + bent), slope


def whole_spec(weight):
    return pl.BlockSpec(memory_space=pltpu.VMEM)


def tile_calls(kernel, grid, in_specs, arrays, out_specs, out_shape, scratch=()):
    return pl.pallas_call(
        kernel,
        grid=grid,
        in_specs=in_specs,
        out_specs=out_specs,
        out_shape=out_shape,
        scratch_shapes=scratch,
        compiler_params=pltpu.CompilerParams(vmem_limit_bytes=TILE_VMEM_BYTES),
        cost_estimate=pl.CostEstimate(flops=1, bytes_accessed=1, transcendentals=0),
    )(*arrays)


def source_specs(count, tile, columns, steps):
    specs = [
        pl.BlockSpec((tile, columns), lambda i: (jnp.minimum(i, steps - 1), 0)),
        pl.BlockSpec((tile, columns), lambda i: (jnp.maximum(i - steps, 0), 0)),
    ]
    return specs[:count]


def on_source(steps, sources, action):
    if len(sources) == 1:
        action(sources[0][...])
    else:
        pl.when(pl.program_id(0) < steps)(lambda: action(sources[0][...]))
        pl.when(pl.program_id(0) >= steps)(lambda: action(sources[1][...]))


def up_kernel(steps, scale, *refs):
    *sources, w_gate, w_up, mixed_ref, to_gate_ref, to_up_ref = refs

    def action(rows):
        gate = dot(rows, w_gate[...]) * scale
        up = dot(rows, w_up[...]) * scale
        value, slope = gelu_parts(gate)
        mixed_ref[...] = bf(value * up)
        to_gate_ref[...] = bf(slope * up)
        to_up_ref[...] = bf(value)

    on_source(steps, sources, action)


def up_project(halves, w_gate, w_up, scale):
    rows, columns = halves[0].shape
    hidden = w_gate.shape[1]
    steps = rows // TILE
    return tile_calls(
        functools.partial(up_kernel, steps, scale),
        (len(halves) * steps,),
        source_specs(len(halves), TILE, columns, steps) + [whole_spec(w_gate), whole_spec(w_up)],
        (*halves, w_gate, w_up),
        [pl.BlockSpec((TILE, hidden), lambda i: (i, 0))] * 3,
        [jax.ShapeDtypeStruct((len(halves) * rows, hidden), jnp.bfloat16)] * 3,
    )


def back_kernel(steps, scale, *refs):
    *sources, w_down, to_gate_ref, to_up_ref, gate_ref, up_ref = refs

    def action(rows):
        grad_mixed = dot(rows, w_down[...]) * scale
        gate_ref[...] = bf(grad_mixed * wide(to_gate_ref[...]))
        up_ref[...] = bf(grad_mixed * wide(to_up_ref[...]))

    on_source(steps, sources, action)


def back_project(halves, w_down, factors, scale):
    rows, columns = halves[0].shape
    hidden = w_down.shape[1]
    steps = rows // TILE
    part = pl.BlockSpec((TILE, hidden), lambda i: (i, 0))
    return tile_calls(
        functools.partial(back_kernel, steps, scale),
        (len(halves) * steps,),
        source_specs(len(halves), TILE, columns, steps) + [whole_spec(w_down), part, part],
        (*halves, w_down, *factors),
        [part] * 2,
        [jax.ShapeDtypeStruct((len(halves) * rows, hidden), jnp.bfloat16)] * 2,
    )


def cross_kernel(steps, n_left, n_right, *refs):
    lefts, rights = refs[:n_left], refs[n_left : n_left + n_right]
    out_ref, left_buf, right_buf, total, sems = refs[n_left + n_right :]

    def copies(step):
        slot = step % 2
        found = []
        at = 0
        for left, left_row, right, right_row, count in steps[step]:
            found.append(
                pltpu.make_async_copy(
                    lefts[left].at[pl.ds(left_row, count)],
                    left_buf.at[slot, pl.ds(at, count)],
                    sems.at[slot, len(found)],
                )
            )
            found.append(
                pltpu.make_async_copy(
                    rights[right].at[pl.ds(right_row, count)],
                    right_buf.at[slot, pl.ds(at, count)],
                    sems.at[slot, len(found)],
                )
            )
            at += count
        return found

    for copy in copies(0):
        copy.start()
    chunk = out_ref.shape[2]
    for step in range(len(steps)):
        slot = step % 2
        if step + 1 < len(steps):
            for copy in copies(step + 1):
                copy.start()
        for copy in copies(step):
            copy.wait()

        @pl.loop(0, total.shape[0] // CHUNK)
        def _(m):
            columns = pl.ds(pl.multiple_of(m * CHUNK, CHUNK), CHUNK)
            term = cross_rows(left_buf[slot, :, columns], right_buf[slot])
            if step > 0:
                term = term + total[columns, :]
            total[columns, :] = term

    for place in range(8):
        for part in range(out_ref.shape[0]):
            start = (place * out_ref.shape[0] + part) * chunk
            out_ref[part, place] = bf(total[start : start + chunk, :])


def cross_products(lefts, rights, steps, parts=1):
    wide_rows, columns = lefts[0].shape[1], rights[0].shape[1]
    depth = max(sum(piece[4] for piece in step) for step in steps)
    pieces = max(2 * len(step) for step in steps)
    return pl.pallas_call(
        functools.partial(cross_kernel, steps, len(lefts), len(rights)),
        in_specs=[pl.BlockSpec(memory_space=pl.ANY)] * (len(lefts) + len(rights)),
        out_shape=jax.ShapeDtypeStruct((parts, 8, wide_rows // 8 // parts, columns), jnp.bfloat16),
        scratch_shapes=[
            pltpu.VMEM((2, depth, wide_rows), jnp.bfloat16),
            pltpu.VMEM((2, depth, columns), jnp.bfloat16),
            pltpu.VMEM((wide_rows, columns), jnp.float32),
            pltpu.SemaphoreType.DMA((2, pieces)),
        ],
        compiler_params=pltpu.CompilerParams(vmem_limit_bytes=CROSS_VMEM_BYTES),
        cost_estimate=pl.CostEstimate(flops=1, bytes_accessed=1, transcendentals=0),
    )(*lefts, *rights)


def partial_kernel(*refs):
    out_ref, pairs = refs[-1], refs[:-1]
    total = times_transposed(pairs[0][...], pairs[1][...])
    for left, right in zip(pairs[2::2], pairs[3::2]):
        total = total + times_transposed(left[...], right[...])
    out_ref[...] = total.astype(out_ref.dtype)


def partial_product(pairs, side, kind):
    rows, hidden = pairs[0][0].shape
    columns = pairs[0][1].shape[0]
    half = rows // 2
    steps = half // TILE
    left_spec = pl.BlockSpec((TILE, hidden), lambda i: (side * steps + i, 0))
    return tile_calls(
        partial_kernel,
        (steps,),
        [spec for pair in pairs for spec in (left_spec, whole_spec(pair[1]))],
        [array for pair in pairs for array in pair],
        pl.BlockSpec((TILE, columns), lambda i: (i, 0)),
        jax.ShapeDtypeStruct((half, columns), kind),
    )


def plane_body(
    hidden_in,
    cotangent,
    doc_lengths,
    gain_attn_in,
    gain_attn_out,
    gain_ffw_in,
    gain_ffw_out,
    query_codes,
    key_integer_codes,
    value_integer_codes,
    out_codes,
    gate_codes,
    up_codes,
    down_codes,
):
    lengths = doc_lengths[0]
    block_rows, width = hidden_in.shape[1:]
    row_length = block_rows * 8
    place = lax.axis_index("seq")
    core = place % 2
    head = HEAD_SIZE
    half = head // 2
    scale_qk = key_unit * MODEL_WIDTH ** (-0.5)
    scale_in = code_unit * MODEL_WIDTH ** (-0.5)
    scale_out = code_unit * (QUERY_HEADS * HEAD_SIZE) ** (-0.5)
    scale_down = code_unit * FF ** (-0.5)
    head_scale = HEAD_SIZE ** (-0.5)

    row_place = lax.axis_index("row")
    model_rows = query_codes.shape[0]
    hidden_part = gate_codes.shape[1] // 8

    def both_ways(below, above):
        return row_shift(below, 1), row_shift(above, -1)

    near_tokens = gather_near(hidden_in[0])
    down_blocks = pack_codes([down_codes], [exact_two], 4, row_place)
    near_tokens, down_blocks = pin(near_tokens, down_blocks)
    own_down = trade(down_blocks)
    attn_blocks = pack_codes(
        [query_codes, key_integer_codes, value_integer_codes, out_codes], [exact_eight] * 4, 1, 0
    )
    attn_blocks, own_down = pin(attn_blocks, own_down)
    attn_weights, gate_blocks, up_blocks, down_one = pin(
        trade(attn_blocks).reshape(width, 3 * head),
        pack_codes([gate_codes], [exact_four], 1, 0),
        pack_codes([up_codes], [exact_four], 1, 0),
        both_ways(own_down, own_down),
    )
    gate_rows = trade(gate_blocks)
    w_attn_in = attn_weights[:, : 2 * head]
    w_out = attn_weights[:, 2 * head :]

    token_blocks = [(place ^ k) * block_rows + jnp.arange(block_rows) for k in RELATIVE]
    token_index = jnp.concatenate(token_blocks).astype(jnp.int32)
    ends = jnp.cumsum(lengths)
    past = token_index[:, None] >= ends[None, :]
    doc_start = jnp.max(jnp.where(past, ends[None, :], 0), axis=1)
    cosine, sine = rotary_tables(token_index - doc_start, head)
    visible = (token_index[None, :] <= token_index[:, None]) & (
        token_index[None, :] >= doc_start[:, None]
    )

    tokens = wide(hidden_in[0])
    upstream = wide(cotangent[0])
    tokens_mine = gather_far(*near_tokens)
    row_tokens = jnp.concatenate([tokens_mine, seq_swap(tokens_mine, 1)])
    normed_in = bf(norm_gain(wide(row_tokens), gain_attn_in))
    linear = dot(normed_in, w_attn_in)
    query = bf(turn(linear[:, :head] * scale_qk, cosine, sine))
    key_half = linear[:, head : head + half] * scale_qk
    value_half = bf(linear[:, head + half :] * scale_in)
    key_other = other_core(key_half)
    value_other = other_core(value_half)

    def pair(own, other):
        return jnp.where(
            core == 0,
            jnp.concatenate([own, other], axis=-1),
            jnp.concatenate([other, own], axis=-1),
        )

    key = bf(turn(pair(key_half, key_other), cosine, sine))
    value = pair(value_half, value_other)
    bend = jnp.tanh(times_transposed(query, key) * (head_scale / SOFTCAP))
    weights = jnp.where(visible, jnp.exp(SOFTCAP * bend), 0.0)
    totals = jnp.sum(weights, axis=-1, keepdims=True)
    attended_wide = dot(bf(weights), value) / totals
    attended = bf(attended_wide)
    attended, gate_rows, down_two = pin(attended, gate_rows, both_ways(*down_one))
    near_half = row_length // 2
    attn_core = scatter_core(
        lambda side, kind: times_transposed(
            attended[side * near_half :][:near_half], w_out
        ).astype(kind)
    )
    (attn_core,) = pin(attn_core)
    attn_near, down_three = pin(scatter_near(*attn_core), both_ways(*down_two))
    attn_proj, up_blocks = pin(scale_out * scatter_far(*attn_near), up_blocks)
    up_rows = trade(up_blocks)
    middle = tokens + norm_gain(attn_proj, gain_attn_out)
    normed_mid = bf(norm_gain(middle, gain_ffw_in))

    mid_near, up_rows, mid_two, mid_three = pin(
        gather_near(normed_mid), up_rows, row_swap(normed_mid, 2), row_swap(normed_mid, 3)
    )
    mid_mine = gather_far(*mid_near)
    mid_mine, mid_theirs, w_down = pin(
        mid_mine,
        seq_swap(mid_mine, 1),
        ordered_quarters(own_down, *zip(down_one, down_two, down_three)),
    )
    w_gate, w_up = gate_rows.reshape(width, hidden_part), up_rows.reshape(width, hidden_part)

    def up_again(*halves):
        return up_project(halves, w_gate, w_up, scale_in)

    def back_again(halves, factors):
        return back_project(halves, w_down, factors, scale_down)

    def cut(rows):
        return [rows[i * block_rows : (i + 1) * block_rows] for i in range(4)]

    mid_cuts = cut(mid_mine)
    (mixed, *factors), pair_mid_near, third_mid_first = pin(
        up_again(mid_mine, mid_theirs),
        gather_near(jnp.concatenate([mid_two, mid_three])),
        row_swap(mid_cuts[0], 1),
    )
    ffn_core, pair_mid_mine, third_mid_next = pin(
        scatter_core(lambda side, kind: partial_product([(mixed, w_down)], side, kind)),
        gather_far(*pair_mid_near),
        row_swap(mid_cuts[1], 1),
    )
    ffn_near, pair_mid_theirs, third_mid_second = pin(
        scatter_near(*ffn_core), seq_swap(pair_mid_mine, 1), row_swap(mid_cuts[2], 1)
    )
    ffn_proj, third_mid_last, pair_mid_mine = pin(
        scale_down * scatter_far(*ffn_near), row_swap(mid_cuts[3], 1), pair_mid_mine
    )
    third_mid_mine = jnp.concatenate([third_mid_first, third_mid_next, third_mid_second, third_mid_last])
    block_out = bf(middle + norm_gain(ffn_proj, gain_ffw_out))
    grad_ffn, grad_gain_four = norm_back(ffn_proj, gain_ffw_out, upstream)
    grad_ffn_low = bf(grad_ffn)
    grad_near, grad_two, (mine_mixed, *mine_factors) = pin(
        gather_near(grad_ffn_low), row_swap(grad_ffn_low, 2), up_again(pair_mid_mine)
    )
    grad_mine = gather_far(*grad_near)
    grad_mine, grad_theirs, grad_three, third_mid_theirs, (theirs_mixed, *theirs_factors) = pin(
        grad_mine,
        seq_swap(grad_mine, 1),
        row_swap(grad_ffn_low, 3),
        seq_swap(third_mid_mine, 1),
        up_again(pair_mid_theirs),
    )
    grad_cuts = grad_mine[: 2 * block_rows], grad_mine[2 * block_rows :]
    grads_hidden, pair_grad_near, third_grad_first = pin(
        back_again((grad_mine, grad_theirs), factors),
        gather_near(jnp.concatenate([grad_two, grad_three])),
        row_swap(grad_cuts[0], 1),
    )
    pairs = list(zip(grads_hidden, (w_gate, w_up)))
    mid_core, pair_grad_mine, third_grad_last = pin(
        scatter_core(lambda side, kind: partial_product(pairs, side, kind)),
        gather_far(*pair_grad_near),
        row_swap(grad_cuts[1], 1),
    )
    third_grad_mine = jnp.concatenate([third_grad_first, third_grad_last])
    sum_near, pair_grad_theirs, third_grad_theirs, (third_mixed, *third_factors), mine_hidden = pin(
        scatter_near(*mid_core),
        seq_swap(pair_grad_mine, 1),
        seq_swap(third_grad_mine, 1),
        up_again(third_mid_mine, third_mid_theirs),
        back_again((pair_grad_mine,), mine_factors),
    )
    grad_mid, theirs_hidden = pin(
        scale_in * scatter_far(*sum_near), back_again((pair_grad_theirs,), theirs_factors)
    )
    grad_middle_part, grad_gain_three = norm_back(middle, gain_ffw_in, grad_mid)
    grad_middle = upstream + grad_middle_part
    grad_proj, grad_gain_two = norm_back(attn_proj, gain_attn_out, grad_middle)

    row_half = row_length // 2
    mids = (mid_mine, mid_theirs, pair_mid_mine, pair_mid_theirs, third_mid_mine, third_mid_theirs)
    outs = (
        grad_mine,
        grad_theirs,
        pair_grad_mine,
        pair_grad_theirs,
        third_grad_mine,
        third_grad_theirs,
    )
    steps = (
        ((0, 0, 0, 0, row_half), (1, 0, 0, row_half, row_half)),
        ((2, 0, 1, 0, row_length),),
        ((3, 0, 2, 0, row_length),),
        ((4, 0, 3, 0, row_half), (5, 0, 3, row_half, row_half)),
    )
    proj_near, down_blocks, third_grads = pin(
        gather_near(bf(grad_proj)),
        cross_products(outs, (mixed, mine_mixed, theirs_mixed, third_mixed), steps),
        (third_grad_mine, third_grad_theirs),
    )
    proj_mine, down_blocks = pin(gather_far(*proj_near), down_blocks)
    down_blocks = trade(down_blocks[0])
    row_proj = jnp.concatenate([proj_mine, seq_swap(proj_mine, 1)])

    def halve(terms, bit, axis, side):
        kept = lax.dynamic_index_in_dim(terms, side, axis, keepdims=False)
        sent = lax.dynamic_index_in_dim(terms, 1 - side, axis, keepdims=False)
        return bf(wide(kept) + wide(row_swap(sent, bit)))

    def quarters_of(part):
        return bf(part).reshape(8, 2, 2, model_rows // 4, part.shape[1])

    low_bit, high_bit = row_place % 2, row_place // 2

    grad_attended = bf(dot(row_proj, w_out) * scale_out)
    delta = jnp.sum(wide(grad_attended) * attended_wide, axis=-1, keepdims=True)
    probs = weights / totals
    grad_probs = times_transposed(grad_attended, value)
    grad_raw = bf(probs * (grad_probs - delta) * (1.0 - bend * bend))
    grad_query = bf(turn(dot(grad_raw, key) * head_scale, cosine, -sine))
    key_part = cross_rows(grad_raw, query) * head_scale
    value_part = cross_rows(bf(probs), grad_attended)

    def own_half(values, side):
        return lax.dynamic_slice_in_dim(values, side * half, half, axis=1)

    key_sum = key_part + other_core(key_part)
    grad_key = bf(own_half(turn(key_sum, cosine, -sine), core))
    grad_value = bf(own_half(value_part, core) + other_core(own_half(value_part, 1 - core)))
    grad_linear = jnp.concatenate([grad_query, grad_key, grad_value], axis=1)
    grad_linear, out_sum, third_grads = pin(
        grad_linear,
        halve(quarters_of(cross_rows(row_proj, attended)), 1, 2, low_bit),
        third_grads,
    )

    def grad_in_half(side, kind):
        rows = grad_linear[side * near_half :][:near_half]
        total = scale_qk * times_transposed(
            rows[:, : head + half], w_attn_in[:, : head + half]
        ) + scale_in * times_transposed(rows[:, head + half :], w_attn_in[:, head + half :])
        return total.astype(kind)

    in_core, in_terms, out_sum, third_grads = pin(
        scatter_core(grad_in_half),
        quarters_of(cross_rows(normed_in, grad_linear)),
        halve(out_sum, 2, 1, high_bit),
        third_grads,
    )
    third_hidden = back_again(third_grads, third_factors)
    gate_terms, up_terms = zip(grads_hidden, mine_hidden, theirs_hidden, third_hidden)
    in_near, in_sum, gate_blocks, up_terms, down_blocks = pin(
        scatter_near(*in_core),
        halve(in_terms, 1, 2, low_bit),
        cross_products(mids, gate_terms, steps),
        up_terms,
        down_blocks,
    )
    gate_blocks = trade(gate_blocks[0])
    in_sum, grad_in, up_blocks, gate_blocks = pin(
        halve(in_sum, 2, 1, high_bit),
        scatter_far(*in_near),
        cross_products(mids, up_terms, steps),
        gate_blocks,
    )
    grad_tokens, grad_gain_one = norm_back(tokens, gain_attn_in, grad_in)
    grad_input = grad_middle + grad_tokens
    gain_terms = jnp.stack([grad_gain_one, grad_gain_two, grad_gain_three, grad_gain_four])
    sums = jnp.concatenate([in_sum, out_sum], axis=2)
    own_rows, columns = sums.shape[1:]
    gain_terms = bf(gain_terms.reshape(4, 8, model_rows).transpose(1, 0, 2)).reshape(8, -1)
    gain_rows = -(-gain_terms.shape[1] // columns // 8) * 8
    gain_terms = jnp.pad(gain_terms, ((0, 0), (0, gain_rows * columns - gain_terms.shape[1])))
    sums = jnp.concatenate([sums, gain_terms.reshape(8, gain_rows, columns)], axis=1)
    sums, up_blocks = pin(trade(sums), up_blocks)
    up_blocks = trade(up_blocks[0])
    gain_blocks = wide(sums[:, own_rows:]).reshape(8, -1)[:, : 4 * model_rows]
    gain_blocks = gain_blocks.reshape(8, 4, model_rows)
    sums = sums[:, :own_rows]

    def double(blocks, received, side):
        both_sides = jnp.stack([blocks, received])
        return jnp.where(side == 0, both_sides, both_sides[::-1])

    gains = jnp.sum(gain_blocks, axis=0)
    gains = gains + row_swap(gains, 1)
    blocks, gains = pin(
        double(sums, row_swap(sums, 2), high_bit), gains + row_swap(gains, 2)
    )
    received = row_swap(blocks, 1)
    grad_w_gate, grad_w_up, grad_w_down = (
        unpack_blocks(blocks, [hidden_part])[0]
        for blocks in (gate_blocks[None], up_blocks[None], down_blocks[None])
    )
    blocks, grad_w_up = pin(blocks, grad_w_up)
    blocks = double(blocks, received, low_bit).transpose(1, 0, 2, 3, 4)
    attn_grads = unpack_blocks(blocks.reshape(4, *sums.shape), [head, half, half, head])

    return (
        block_out[None],
        grad_input[None],
        gains[0],
        gains[1],
        gains[2],
        gains[3],
        attn_grads[0],
        attn_grads[1],
        attn_grads[2],
        attn_grads[3],
        grad_w_gate,
        grad_w_up,
        grad_w_down,
    )


def solution(mesh):
    body = plane_body if dict(mesh.shape) == {"seq": 8, "row": 4} else token_body
    return jax.shard_map(
        body,
        mesh=mesh,
        in_specs=(
            P("row", "seq", None),
            P("row", "seq", None),
            P("row", None),
            P(),
            P(),
            P(),
            P(),
            P("seq", None),
            P("seq", None),
            P("seq", None),
            P("seq", None),
            P("seq", None),
            P("seq", None),
            P("seq", None),
        ),
        out_specs=(
            P("row", "seq", None),
            P("row", "seq", None),
            P("seq"),
            P("seq"),
            P("seq"),
            P("seq"),
            P("seq", None),
            P("seq", None),
            P("seq", None),
            P("seq", None),
            P("seq", None),
            P("seq", None),
            P("seq", None),
        ),
        check_vma=False,
    )
```
